128 devices in a mesh: gx: 8 (over y, core), gy: 16 (over x, z).
Axes of the slice: x: 4, y: 4, z: 4, core: 2. Of those that a mesh axis runs over, the one named last changes fastest.
Arguments:
- coords: float32 [3, 128, 256, 64], P(None, 'gx', 'gy'), may hold values from 0 to 1
- weights: float32 [128, 256, 64], P('gx', 'gy'), may hold values from 0.2 to 2
- solution: float32 [128, 256, 64], P('gx', 'gy'), may hold values from -6 to 6
- source: float32 [128, 256, 64], P('gx', 'gy'), may hold values from -6 to 6
- counts: int32 [128, 256], P('gx', 'gy'), may hold values from 16 to 64, as said below
- check_points: float32 [3, 256], replicated, may hold values from 0 to 1
- equiv_points: float32 [3, 256], replicated, may hold values from 0 to 1
- check_solve: float32 [256, 256], replicated, may hold values from -0.375 to 0.375
- up_children: float32 [4, 256, 256], replicated, may hold values from -0.1875 to 0.1875
- far_transfer: bfloat16 [40, 256, 256], replicated, may hold values from -0.078125 to 0.078125
- down_children: float32 [4, 256, 256], replicated, may hold values from -0.375 to 0.375
- pair_up: float32 [2, 256, 256], replicated, may hold values from -0.25 to 0.25
- lattice_map: float32 [256, 256], replicated, may hold values from -0.375 to 0.375
- pair_down: float32 [2, 256, 256], replicated, may hold values from -0.375 to 0.375
Outputs:
- residual: float32 [128, 256, 64], P('gx', 'gy')
The draws below stay inside these ranges and needn't reach their ends.
Inputs may be any that keep to these rules, and one draw needn't show every extreme that they name: Slots from counts on are empty; some leaf box holds 64 points.
All inputs are finite; a program needn't handle non-finite values.
Results may differ from the reference program's by a relative error of at most 0.0003.
Values may be sent and summed in bfloat16 or wider, within the bound.
No kernel may reach another device: no remote copies, remote signals or barrier semaphores. Data moves between devices by JAX's collectives and lax.ppermute only.
A program may use at most 128 MiB of HBM per device.

```python
import math
import jax
import jax.numpy as jnp
import numpy as np
from jax import lax

Q = 256
S = 64
LX = 128
LY = 256
N_GX = 8
N_GY = 16


def draw_counts(key, part):
    key = jax.random.fold_in(key, 3)
    first_key, row_key, column_key = jax.random.split(key, 3)
    drawn = jax.random.randint(first_key, (LX, LY), S // 4, S + 1)
    row_pick = jax.random.randint(row_key, (), 0, LX)
    column_pick = jax.random.randint(column_key, (), 0, LY)
    return drawn.at[row_pick, column_pick].set(S).astype(jnp.int32)


def level_of(key, shape, cuts, low, largest):
    level, own = 1.0, jax.random.fold_in(key, 6)
    for position, parts in cuts:
        draws = jnp.exp(jax.random.uniform(jax.random.fold_in(own, position), (parts,), jnp.float32, low / len(cuts), largest / len(cuts)))
        level = level * jnp.repeat(draws, shape[position] // parts).reshape([-1 if axis == position else 1 for axis in range(len(shape))])
    return level


def normal_values(stream_key, extent, scale, limit, cuts=(), kind=jnp.bfloat16):
    values = scale * jax.random.normal(stream_key, extent, jnp.float32)
    if cuts:
        values = values * level_of(stream_key, extent, cuts, -0.22, 0.18)
    return jnp.clip(values, -limit, limit).astype(kind)


def setup_inputs(seed: int = 0) -> dict:
    seeds = jax.random.split(jax.random.key(seed), 15)
    return {
        "coords": jnp.clip(1.0 * jax.random.uniform(seeds[0], (3, LX, LY, S), jnp.float32) ** level_of(seeds[0], (3, LX, LY, S), ((1, 8), (2, 16)), -0.2, 0.2), 0.0, 1.0),
        "weights": jnp.clip(jnp.exp(math.log(2.0) - 2.3025851 * jax.random.uniform(seeds[1], (LX, LY, S), jnp.float32) ** level_of(seeds[1], (LX, LY, S), ((0, 8), (1, 16)), -0.2, 0.2)), 0.2, 2.0),
        "solution": normal_values(seeds[2], (LX, LY, S), 1.0, 6.0, ((0, 8), (1, 16)), jnp.float32),
        "source": normal_values(seeds[3], (LX, LY, S), 1.0, 6.0, ((0, 8), (1, 16)), jnp.float32),
        "counts": draw_counts(jax.random.fold_in(seeds[14], 71), 0),
        "check_points": jnp.clip(jax.random.uniform(seeds[5], (3, Q), jnp.float32, 0.0, 1.0), 0.0, 1.0),
        "equiv_points": jnp.clip(jax.random.uniform(seeds[6], (3, Q), jnp.float32, 0.0, 1.0), 0.0, 1.0),
        "check_solve": normal_values(seeds[7], (Q, Q), Q ** -0.5, 0.375, (), jnp.float32),
        "up_children": normal_values(seeds[8], (4, Q, Q), (4 * Q) ** -0.5, 0.1875, (), jnp.float32),
        "far_transfer": normal_values(seeds[9], (40, Q, Q), (27 * Q) ** -0.5, 0.078125),
        "down_children": normal_values(seeds[10], (4, Q, Q), Q ** -0.5, 0.375, (), jnp.float32),
        "pair_up": normal_values(seeds[11], (2, Q, Q), (2 * Q) ** -0.5, 0.25, (), jnp.float32),
        "lattice_map": normal_values(seeds[12], (Q, Q), Q ** -0.5, 0.375, (), jnp.float32),
        "pair_down": normal_values(seeds[13], (2, Q, Q), Q ** -0.5, 0.375, (), jnp.float32),
    }


sharpness = 25.0
power_law = -2.25
scale_frac = 0.4
highest = lax.Precision.HIGHEST


def kernel(dist_sq):
    return (1.0 + sharpness * dist_sq) ** power_law


def far_offsets():
    result = []
    for shift_x in range(-3, 4):
        for shift_y in range(-3, 4):
            if max(abs(shift_x), abs(shift_y)) >= 2:
                result.append((shift_x, shift_y))
    return result


def reachable(parity, shift_amount):
    return abs((parity + shift_amount) // 2) <= 1


def near_block(padded):
    extent_x = padded.shape[1] - 2
    extent_y = padded.shape[2] - 2
    target = padded[:3, 1:-1, 1:-1]
    summed = jnp.zeros((2, extent_x, extent_y, padded.shape[3]), jnp.float32)
    for shift_x in (-1, 0, 1):
        for shift_y in (-1, 0, 1):
            sources = padded[:, 1 + shift_x:1 + shift_x + extent_x, 1 + shift_y:1 + shift_y + extent_y]
            shifts = (float(shift_x), float(shift_y), 0.0)
            dist_sq = None
            for comp in range(3):
                gap = target[comp][..., :, None] - (sources[comp] + shifts[comp])[..., None, :]
                dist_sq = gap * gap if dist_sq is None else dist_sq + gap * gap
            kernel_vals = kernel(dist_sq)
            summed = summed + jnp.einsum('xyij,cxyj->cxyi', kernel_vals, sources[3:], precision=highest)
    return summed


def check_block(points, check_points):
    dist_sq = None
    for comp in range(3):
        gap = check_points[comp][None, None, :, None] - points[comp][:, :, None, :]
        dist_sq = gap * gap if dist_sq is None else dist_sq + gap * gap
    kernel_vals = kernel(dist_sq)
    return jnp.einsum('xyqj,cxyj->xycq', kernel_vals, points[3:], precision=highest)


def evaluate_block(coords, local_exp, equiv_points):
    dist_sq = None
    for comp in range(3):
        gap = coords[comp][:, :, :, None] - equiv_points[comp][None, None, None, :]
        dist_sq = gap * gap if dist_sq is None else dist_sq + gap * gap
    kernel_vals = kernel(dist_sq)
    return jnp.einsum('xysq,xycq->cxys', kernel_vals, local_exp, precision=highest)


def gather_up(children, up_children):
    width = children.shape[3]
    grouped = children.reshape(children.shape[0] // 2, 2, children.shape[1] // 2, 2, children.shape[2], width)
    return jnp.einsum('xaybcq,abqr->xycr', grouped, up_children.reshape(2, 2, width, width), precision=highest)


def spread_down(parents, down_children):
    width = parents.shape[3]
    spread = jnp.einsum('xycq,abqr->xaybcr', parents, down_children.reshape(2, 2, width, width), precision=highest)
    return spread.reshape(2 * parents.shape[0], 2 * parents.shape[1], parents.shape[2], width)


def far_level(padded, operator):
    extent_x = padded.shape[0] - 6
    extent_y = padded.shape[1] - 6
    width = operator.shape[1]
    summed = jnp.zeros((extent_x, extent_y, padded.shape[2], width), jnp.float32)
    for parity_x in (0, 1):
        for parity_y in (0, 1):
            pieces = []
            chosen = []
            for number, (shift_x, shift_y) in enumerate(far_offsets()):
                if reachable(parity_x, shift_x) and reachable(parity_y, shift_y):
                    start_x = 3 + shift_x + parity_x
                    start_y = 3 + shift_y + parity_y
                    pieces.append(padded[start_x:start_x + extent_x - parity_x:2, start_y:start_y + extent_y - parity_y:2])
                    chosen.append(number)
            stacked = jnp.concatenate(pieces, axis=-1)
            matrix = operator[np.array(chosen)].reshape(len(chosen) * width, width)
            product = jnp.dot(stacked.reshape(-1, len(chosen) * width), matrix, preferred_element_type=jnp.float32)
            summed = summed.at[parity_x::2, parity_y::2].set(product.reshape(extent_x // 2, extent_y // 2, padded.shape[2], width))
    return summed


def tree_root(box_grid, pair_up):
    while box_grid.shape[1] > 1:
        grouped = box_grid.reshape(box_grid.shape[0], box_grid.shape[1] // 2, 2, box_grid.shape[2], box_grid.shape[3])
        box_grid = jnp.einsum('xyecq,eqr->xycr', grouped, pair_up, precision=highest)
    while box_grid.shape[0] > 1:
        grouped = box_grid.reshape(box_grid.shape[0] // 2, 2, 1, box_grid.shape[2], box_grid.shape[3])
        box_grid = jnp.einsum('xeycq,eqr->xycr', grouped, pair_up, precision=highest)
    return box_grid


def descend_grid(root_mult, lattice_map, pair_down):
    box_grid = jnp.dot(root_mult, lattice_map, precision=highest)[None, None]
    while box_grid.shape[0] < N_GX:
        spread = jnp.einsum('xycq,eqr->xeycr', box_grid, pair_down, precision=highest)
        box_grid = spread.reshape(2 * box_grid.shape[0], box_grid.shape[1], box_grid.shape[2], box_grid.shape[3])
    while box_grid.shape[1] < N_GY:
        spread = jnp.einsum('xycq,eqr->xyecr', box_grid, pair_down, precision=highest)
        box_grid = spread.reshape(box_grid.shape[0], 2 * box_grid.shape[1], box_grid.shape[2], box_grid.shape[3])
    return box_grid


def wrap_pad(box_grid):
    return jnp.pad(box_grid, ((3, 3), (3, 3), (0, 0), (0, 0)), mode="wrap")


def reference(coords, weights, solution, source, counts, check_points, equiv_points, check_solve, up_children, far_transfer, down_children, pair_up, lattice_map, pair_down):
    slot_index = jnp.arange(S, dtype=jnp.int32)
    live_slots = (slot_index[None, None, :] < counts[:, :, None]).astype(jnp.float32)
    density = jnp.stack([weights * live_slots, weights * solution * live_slots])
    points = jnp.concatenate([coords, density], axis=0)
    padded_points = jnp.pad(points, ((0, 0), (1, 1), (1, 1), (0, 0)), mode="wrap")
    row_starts = jnp.arange(LX, dtype=jnp.int32)
    near_rows = lax.map(lambda row_start: near_block(lax.dynamic_slice_in_dim(padded_points, row_start, 3, 1)), row_starts)
    near_field = jnp.transpose(near_rows[:, :, 0], (1, 0, 2, 3))
    check_rows = lax.map(lambda row_start: check_block(lax.dynamic_slice_in_dim(points, row_start, 1, 1), check_points), row_starts)
    check_pot = check_rows[:, 0]
    leaf_mult = jnp.einsum('xycq,qr->xycr', check_pot, check_solve, precision=highest)
    parent_mult = gather_up(leaf_mult, up_children)
    grand_mult = gather_up(parent_mult, up_children)
    great_mult = gather_up(grand_mult, up_children)
    device_mult = gather_up(great_mult, up_children)
    root_mult = tree_root(device_mult, pair_up)[0, 0]
    device_local = descend_grid(root_mult, lattice_map, pair_down)
    far_leaves = far_level(wrap_pad(leaf_mult.astype(jnp.bfloat16)), far_transfer)
    far_parents = far_level(wrap_pad(parent_mult.astype(jnp.bfloat16)), far_transfer)
    great_local = spread_down(device_local, down_children)
    grand_local = spread_down(great_local, down_children)
    parent_local = spread_down(grand_local, down_children) + far_parents
    leaf_local = spread_down(parent_local, down_children) + far_leaves
    far_rows = lax.map(lambda row_start: evaluate_block(lax.dynamic_slice_in_dim(coords, row_start, 1, 1), lax.dynamic_slice_in_dim(leaf_local, row_start, 1, 0), equiv_points), row_starts)
    potential = near_field + jnp.transpose(far_rows[:, :, 0], (1, 0, 2, 3))
    return live_slots * (source - scale_frac * (solution * potential[0] - potential[1]))
```

```python
import jax
import jax.numpy as jnp
import numpy as np
from jax import lax
from jax.experimental import pallas as pl
from jax.experimental.pallas import tpu as pltpu
from jax.sharding import PartitionSpec as P

f32 = jnp.float32
bf16 = jnp.bfloat16
scale_frac = 0.4
highest = lax.Precision.HIGHEST
NX = 16
LANES = NX * 64
PADDED = LANES + 128
FEATS = 64
AXES = ("gx", "gy")
VMEM = pl.BlockSpec(memory_space=pltpu.VMEM)
PARAMS = pltpu.CompilerParams(vmem_limit_bytes=60 << 20)


def far_offsets():
    return [
        (x, y) for x in range(-3, 4) for y in range(-3, 4) if max(abs(x), abs(y)) >= 2
    ]


def dot(a, b, precision=None):
    return jnp.dot(a, b, preferred_element_type=f32, precision=precision)


def dot_t(a, b):
    return lax.dot_general(a, b, (((1,), (1,)), ((), ())), preferred_element_type=f32)


def split3(block):
    hi = block.astype(bf16).astype(f32)
    rest = block - hi
    mid = rest.astype(bf16).astype(f32)
    return hi, mid, rest - mid


def centred(block):
    row = lax.broadcasted_iota(jnp.int32, block.shape, 0)
    moved = jnp.where(row < 3, 5.0 * block - 2.5, 0.0)
    return row, moved, jnp.sum(moved * moved, axis=0, keepdims=True)


def row_feats(block):
    row, moved, norm = centred(block)
    packed = jnp.where(
        row < 3, moved, jnp.where(row == 5, norm + 1.0, jnp.where(row == 6, 1.0, 0.0))
    )
    hi, mid, lo = split3(packed)
    role = jnp.concatenate(
        [hi[0:1], mid[0:1], lo[0:1], hi[1:2], mid[1:2], lo[1:2], hi[6:7] * 25.0, hi[7:8]], axis=0
    )
    tens = jnp.where(row < 6, 10.0, 0.0)
    return jnp.concatenate([hi, hi, hi, mid, mid, lo, role, tens], axis=0).astype(bf16)


def col_feats(block, role_scale=1.0):
    row, moved, norm = centred(block)
    packed = jnp.where(row < 3, moved, jnp.where(row == 6, norm, 0.0))
    hi, mid, lo = split3(packed)
    one = jnp.where(row == 5, 1.0, 0.0)
    def part(value, marks, keep_norm):
        out = jnp.where(row < 3, value * -2.0, 0.0)
        if keep_norm:
            out = jnp.where(row == 6, value, out)
        return out + one if marks else out
    ones = jnp.where(row < 7, 1.0, 0.0)
    role = jnp.concatenate(
        [hi[0:1], mid[0:1], lo[0:1], hi[1:2], mid[1:2], lo[1:2], hi[7:8], hi[7:8]], axis=0
    )
    return jnp.concatenate(
        [
            part(hi, True, True),
            part(mid, False, True),
            part(lo, False, True),
            part(hi, True, False),
            part(mid, False, False),
            part(hi, True, False),
            ones * role_scale,
            role * role_scale,
        ],
        axis=0,
    ).astype(bf16)


def power(u):
    return jnp.exp2(jnp.log2(u) * -2.25)


def box_perm(side):
    order = []
    for e in (0, 1):
        for f in (0, 1):
            for b in range(side):
                for a in range(side):
                    for c in (0, 1):
                        order.append(((2 * b + f) * 2 * side + 2 * a + e) * 2 + c)
    out = np.zeros((len(order), len(order)), np.float32)
    out[np.arange(len(order)), order] = 1.0
    return out


def eye(n):
    return (
        lax.broadcasted_iota(jnp.int32, (n, n), 0) == lax.broadcasted_iota(jnp.int32, (n, n), 1)
    ).astype(bf16)


def gather4(blocks, matrices):
    n = blocks.shape[0] // 4
    total = None
    for p in range(4):
        term = dot(blocks[p * n : (p + 1) * n], matrices[p], highest)
        total = term if total is None else total + term
    return total


def upward_kernel(
    place, pts, check_pts, solve, up_child, pair_up, perm8, perm4,
    feats, leaf_r, parent_r, up_out, pot,
):
    check_cols = col_feats(check_pts[...], 0.0)
    ident = eye(128)

    def strip(a, carry):
        block = pts[a]
        rows = row_feats(block)
        for m in range(NX // 2):
            lanes = slice(128 * m, 128 * m + 128)
            f = dot_t(ident, rows[:, lanes]).astype(bf16)
            feats[pl.ds(pl.multiple_of(a * LANES + 128 * m, 128), 128), :] = f
            w = jnp.transpose(block[:, lanes])
            k = power(dot(f, check_cols))
            for half in range(2):
                span = slice(64 * half, 64 * half + 64)
                at = (lax.rem(a, 2) * 2 + half) * 128 + m * 16 + lax.div(a, 2) * 2
                for c in range(2):
                    pot[pl.ds(at + c, 1), :] = jnp.sum(
                        k[span] * w[span, 3 + c : 4 + c], axis=0, keepdims=True
                    )
        return carry

    lax.fori_loop(0, NX, strip, 0)
    leaf = dot(pot[...], solve[...], highest)
    leaf_r[...] = leaf.astype(bf16)
    parent = gather4(leaf, up_child)
    parent = dot(perm8[...], parent, highest)
    parent_r[...] = parent.astype(bf16)
    grand = dot(perm4[...], gather4(parent, up_child), highest)
    great = gather4(grand, up_child)
    vec = None
    for b in range(2):
        for a in range(2):
            at = (b * 2 + a) * 2
            term = dot(
                jnp.concatenate([great[at : at + 2]] * 4, axis=0), up_child[2 * a + b], highest
            )
            vec = term if vec is None else vec + term
    for bit in range(4):
        vec = dot(vec, pair_up[lax.rem(lax.div(place[1], 2**bit), 2)], highest)
    for bit in range(3):
        vec = dot(vec, pair_up[lax.rem(lax.div(place[0], 2**bit), 2)], highest)
    up_out[...] = vec


def role_tiles():
    def column(sx, sy):
        return [-10.0 * sx] * 3 + [-10.0 * sy] * 3 + [float(sx * sx + sy * sy), 0.0] + [
            float(sx)
        ] * 3 + [float(sy)] * 3 + [0.0, 0.0]
    pairs = [((t, -1), (t, 0)) for t in (-1, 0, 1)] + [((-1, 1), (0, 1)), ((1, 1), (1, 1))]
    out = np.zeros((5, 16, 128), np.float32)
    for n, (left, right) in enumerate(pairs):
        out[n, :, :64] = np.array(column(*left))[:, None]
        out[n, :, 64:] = np.array(column(*right))[:, None]
    return out


def sum_lanes(acc0, acc1):
    row = lax.broadcasted_iota(jnp.int32, (8, 256), 0)
    total = None
    for c, acc in enumerate((acc0, acc1)):
        hi = acc.astype(bf16)
        lo = (acc - hi.astype(f32)).astype(bf16)
        ones = jnp.where(row == c, 1.0, 0.0).astype(bf16)
        term = dot_t(ones, jnp.concatenate([hi, lo], axis=1))
        total = term if total is None else total + term
    return total


def near_kernel(pts, feats, roles, out, cols0, cols1, dens1):
    lane = lax.broadcasted_iota(jnp.int32, (1, 128), 1)
    first = lane < 64
    first_cols = lax.broadcasted_iota(jnp.int32, (FEATS, 128), 1) < 64

    def prepare(t, carry):
        block = pts[t]
        cols = col_feats(block)
        cols0[t] = cols
        moved = pltpu.roll(block, PADDED - 64, 1)
        cols1[t] = col_feats(moved)
        dens1[t] = moved
        return carry

    lax.fori_loop(0, NX + 2, prepare, 0)

    def step(i, carry):
        a = lax.div(i, 2)
        half = lax.rem(i, 2)
        for mm in range(4):
            base = pl.multiple_of(half * 512 + mm * 128, 128)
            here = pl.ds(base, 128)
            after = pl.ds(pl.multiple_of(base + 128, 128), 128)
            sums = []
            for odd in range(2):
                own, other = ((cols0, cols1), (cols1, cols0))[odd]
                d_own, d_other = ((pts, dens1), (dens1, pts))[odd]
                far = here if odd == 0 else after
                blocks = [own[a + t, :, here] for t in range(3)]
                blocks.append(jnp.where(first_cols, own[a, :, after], other[a + 1, :, far]))
                blocks.append(own[a + 2, :, after])
                blocks = [
                    jnp.concatenate([x[:48], x[48:] * roles[n]], axis=0)
                    for n, x in enumerate(blocks)
                ]
                rows = feats[pl.ds(pl.multiple_of(a * LANES + base + 64 * odd, 64), 64), :]
                k = power(dot(rows, jnp.concatenate(blocks, axis=1)))
                accs = []
                for c in range(2):
                    r = pl.ds(3 + c, 1)
                    dens = [d_own[a + t, r, here] for t in range(3)]
                    dens.append(jnp.where(first, d_own[a, r, after], d_other[a + 1, r, far]))
                    dens.append(jnp.where(first, d_own[a + 2, r, after], 0.0))
                    acc = None
                    for n in range(5):
                        term = k[:, 128 * n : 128 * n + 128] * dens[n]
                        acc = term if acc is None else acc + term
                    accs.append(acc)
                sums.append(accs)
            both = [jnp.concatenate([sums[0][c], sums[1][c]], axis=0) for c in range(2)]
            out[a, :, here] = sum_lanes(*both)
        return carry

    lax.fori_loop(0, 2 * NX, step, 0)


def reachable(parity, shift):
    return abs((parity + shift) // 2) <= 1


def far_kernel(boxes, transfer, leaf_out, parent_out):
    for px in (0, 1):
        for py in (0, 1):
            total = None
            for number, (sx, sy) in enumerate(far_offsets()):
                if not (reachable(px, sx) and reachable(py, sy)):
                    continue
                dx, dy = (px + sx) // 2, (py + sy) // 2
                source = (px + sx) % 2 * 2 + (py + sy) % 2
                window = jnp.concatenate(
                    [
                        boxes[source, dx + 1, 1 + dy : 9 + dy].reshape(128, 256),
                        boxes[source, dx + 1, 11 + dy : 15 + dy].reshape(64, 256),
                    ],
                    axis=0,
                )
                term = dot(window, transfer[number])
                total = term if total is None else total + term
            p = px * 2 + py
            leaf_out[p] = total[:128]
            parent_out[p] = total[128:]


def downward_kernel(
    place, gathered, lattice, pair_down, down_child, perm8, perm4, far_leaf, far_parent,
    equiv_pts, feats, near, solution, source, live, out, local, pot,
):
    vec = jnp.sum(gathered[...], axis=0)
    vec = dot(jnp.concatenate([vec] * 4, axis=0), lattice[...], highest)
    for bit in (2, 1, 0):
        vec = dot(vec, pair_down[lax.rem(lax.div(place[0], 2**bit), 2)], highest)
    for bit in (3, 2, 1, 0):
        vec = dot(vec, pair_down[lax.rem(lax.div(place[1], 2**bit), 2)], highest)
    great = jnp.concatenate(
        [dot(vec, down_child[2 * a + b], highest)[:2] for b in range(2) for a in range(2)], axis=0
    )
    spread = lambda x: jnp.concatenate([dot(x, down_child[p], highest) for p in range(4)], axis=0)
    grand = dot(perm4[...], spread(great), highest)
    parent = spread(grand) + far_parent[...]
    parent = dot(perm8[...], parent, highest)
    local[...] = spread(parent) + far_leaf[...]
    equiv_cols = col_feats(equiv_pts[...], 0.0)

    def step(i, carry):
        a = lax.div(i, 2)
        half = lax.rem(i, 2)
        for mm in range(4):
            base = pl.multiple_of(half * 512 + mm * 128, 128)
            m = half * 4 + mm
            rows = feats[pl.ds(pl.multiple_of(a * LANES + base, 128), 128), :]
            k = power(dot(rows, equiv_cols))
            accs = []
            for c in range(2):
                parts = []
                for odd in range(2):
                    at = (lax.rem(a, 2) * 2 + odd) * 128 + m * 16 + lax.div(a, 2) * 2 + c
                    weight = local[pl.ds(at, 1), :]
                    kk = k[64 * odd : 64 * odd + 64]
                    parts.append(kk[:, :128] * weight[:, :128] + kk[:, 128:] * weight[:, 128:])
                accs.append(jnp.concatenate(parts, axis=0))
            sums = sum_lanes(*accs) + near[a, :, pl.ds(base, 128)]
            for c in range(2):
                pot[m, pl.ds(16 * c + a, 1), :] = sums[c : c + 1]
        return carry

    lax.fori_loop(0, 2 * NX, step, 0)
    both = jnp.concatenate([pot[m] for m in range(NX // 2)], axis=1)
    result = source[...] - scale_frac * (solution[...] * both[:NX] - both[NX:])
    out[...] = jnp.where(live[...] > 0.0, result, 0.0)


def ring(axis, step):
    count = lax.axis_size(axis)
    return [(i, (i + step) % count) for i in range(count)]


def with_halo(block, axis, dim, width):
    low = lax.ppermute(
        lax.slice_in_dim(block, block.shape[dim] - width, None, axis=dim), axis, ring(axis, 1)
    )
    high = lax.ppermute(lax.slice_in_dim(block, 0, width, axis=dim), axis, ring(axis, -1))
    return low, high


def call(kernel, n_in, out_shape, scratch, smem=0):
    return pl.pallas_call(
        kernel,
        out_shape=out_shape,
        in_specs=[pl.BlockSpec(memory_space=pltpu.SMEM)] * smem + [VMEM] * n_in,
        out_specs=jax.tree.map(lambda _: VMEM, out_shape),
        scratch_shapes=scratch,
        compiler_params=PARAMS,
    )


def shape(*dims, dtype=f32):
    return jax.ShapeDtypeStruct(dims, dtype)


def shards(
    coords, weights, solution, source, counts, check_points, equiv_points, check_solve,
    up_children, far_transfer, down_children, pair_up, lattice_map, pair_down,
):
    slot = lax.broadcasted_iota(jnp.int32, (NX, NX, 64), 2)
    live = (slot < counts[:, :, None]).astype(f32)
    flat = lambda x: x.reshape(NX, LANES)
    live = flat(live)
    sol = flat(solution)
    w0 = flat(weights) * live
    w1 = w0 * sol
    xyz = coords.reshape(3, NX, LANES)
    zero = jnp.zeros_like(w0)
    pts = jnp.stack([xyz[0], xyz[1], xyz[2], w0, w1, zero, zero, zero], axis=1)
    low, high = with_halo(pts, "gx", 0, 1)
    tall = jnp.concatenate([low, pts, high], axis=0)
    low, high = with_halo(tall, "gy", 2, 64)
    padded = jnp.concatenate([low, tall, high], axis=2)

    place = jnp.stack([lax.axis_index("gx"), lax.axis_index("gy")]).astype(jnp.int32)
    eight = lambda x: jnp.pad(x, ((0, 5), (0, 0)))
    perm8, perm4 = box_perm(4), box_perm(2)
    feats, leaf_r, parent_r, up = call(
        upward_kernel, 7,
        (shape(NX * LANES, FEATS, dtype=bf16), shape(512, 256, dtype=bf16),
         shape(128, 256, dtype=bf16), shape(8, 256)),
        [pltpu.VMEM((512, 256), f32)], smem=1,
    )(place, pts, eight(check_points), check_solve, up_children, pair_up, perm8, perm4)

    gathered = lax.all_to_all(
        jnp.broadcast_to(up[None, :2], (128, 2, 256)), AXES, 0, 0, tiled=True
    )

    boxes = jnp.concatenate(
        [
            leaf_r.reshape(4, 8, 16, 256),
            jnp.pad(parent_r.reshape(4, 4, 8, 256), ((0, 0), (0, 0), (0, 8), (0, 0))),
        ],
        axis=1,
    )
    ends = lambda n, p: jnp.concatenate([boxes[:, n : n + 1], boxes[:, p : p + 1]], axis=1)
    low = lax.ppermute(ends(7, 11), "gy", ring("gy", 1))
    high = lax.ppermute(ends(0, 8), "gy", ring("gy", -1))
    wide = jnp.concatenate(
        [low[:, :1], boxes[:, :8], high[:, :1], low[:, 1:], boxes[:, 8:], high[:, 1:]], axis=1
    )
    last = jnp.concatenate([wide[:, :10, 14:16], wide[:, 10:, 6:8]], axis=1)
    low = lax.ppermute(last, "gx", ring("gx", 1))
    high = lax.ppermute(wide[:, :, :2], "gx", ring("gx", -1))
    before = jnp.concatenate([low, wide[:, :, :14]], axis=2)
    after = jnp.concatenate(
        [
            jnp.concatenate([wide[:, :10, 2:], high[:, :10]], axis=2),
            jnp.concatenate([wide[:, 10:, 2:8], high[:, 10:], wide[:, 10:, 8:]], axis=2),
        ],
        axis=1,
    )
    windows = jnp.stack([before, wide, after], axis=1)

    near = call(
        near_kernel, 3, shape(NX, 8, LANES),
        [pltpu.VMEM((NX + 2, FEATS, PADDED), bf16)] * 2 + [pltpu.VMEM((NX + 2, 8, PADDED), f32)],
    )(padded, feats, jnp.asarray(role_tiles(), bf16))

    far_leaf, far_parent = call(
        far_kernel, 2, (shape(4, 128, 256), shape(4, 64, 256)), []
    )(windows, far_transfer)
    far_parent = far_parent.reshape(4, 4, 16, 256)[:, :, :8].reshape(128, 256)

    out = call(
        downward_kernel, 14, shape(NX, LANES),
        [pltpu.VMEM((512, 256), f32), pltpu.VMEM((NX // 2, 2 * NX, 128), f32)], smem=1,
    )(
        place, gathered, lattice_map, pair_down, down_children, perm8.T, perm4.T,
        far_leaf.reshape(512, 256), far_parent, eight(equiv_points), feats, near,
        sol, flat(source), live,
    )
    return out.reshape(NX, NX, 64)


def solution(mesh):
    box = P("gx", "gy", None)
    return jax.shard_map(
        shards,
        mesh=mesh,
        in_specs=(P(None, "gx", "gy", None), box, box, box, P("gx", "gy")) + (P(),) * 9,
        out_specs=box,
        check_vma=False,
    )
```

```python
import jax
import jax.numpy as jnp
import numpy as np
from jax import lax
from jax.experimental import pallas as pl
from jax.experimental.pallas import tpu as pltpu
from jax.sharding import PartitionSpec as P

f32 = jnp.float32
bf16 = jnp.bfloat16
scale_frac = 0.4
NX = 16
LANES = NX * 64
PADDED = LANES + 128
FEATS = 64
AXES = ("gx", "gy")
VMEM = pl.BlockSpec(memory_space=pltpu.VMEM)
PARAMS = pltpu.CompilerParams(vmem_limit_bytes=60 << 20)


def far_offsets():
    return [
        (x, y) for x in range(-3, 4) for y in range(-3, 4) if max(abs(x), abs(y)) >= 2
    ]


def dot(a, b):
    return jnp.dot(a, b, preferred_element_type=f32)


def dot_t(a, b):
    return lax.dot_general(a, b, (((1,), (1,)), ((), ())), preferred_element_type=f32)


def split3(block):
    hi = block.astype(bf16).astype(f32)
    rest = block - hi
    mid = rest.astype(bf16).astype(f32)
    return hi, mid, rest - mid


def centred(block):
    row = lax.broadcasted_iota(jnp.int32, block.shape, 0)
    moved = jnp.where(row < 3, 5.0 * block - 2.5, 0.0)
    return row, moved, jnp.sum(moved * moved, axis=0, keepdims=True)


def row_feats(block):
    row, moved, norm = centred(block)
    packed = jnp.where(
        row < 3, moved, jnp.where(row == 5, norm + 1.0, jnp.where(row == 6, 1.0, 0.0))
    )
    hi, mid, lo = split3(packed)
    role = jnp.concatenate(
        [hi[0:1], mid[0:1], lo[0:1], hi[1:2], mid[1:2], lo[1:2], hi[6:7] * 25.0, hi[7:8]], axis=0
    )
    tens = jnp.where(row < 6, 10.0, 0.0)
    return jnp.concatenate([hi, hi, hi, mid, mid, lo, role, tens], axis=0).astype(bf16)


def col_feats(block, role_scale=1.0):
    row, moved, norm = centred(block)
    packed = jnp.where(row < 3, moved, jnp.where(row == 6, norm, 0.0))
    hi, mid, lo = split3(packed)
    one = jnp.where(row == 5, 1.0, 0.0)
    def part(value, marks, keep_norm):
        out = jnp.where(row < 3, value * -2.0, 0.0)
        if keep_norm:
            out = jnp.where(row == 6, value, out)
        return out + one if marks else out
    ones = jnp.where(row < 7, 1.0, 0.0)
    role = jnp.concatenate(
        [hi[0:1], mid[0:1], lo[0:1], hi[1:2], mid[1:2], lo[1:2], hi[7:8], hi[7:8]], axis=0
    )
    return jnp.concatenate(
        [
            part(hi, True, True),
            part(mid, False, True),
            part(lo, False, True),
            part(hi, True, False),
            part(mid, False, False),
            part(hi, True, False),
            ones * role_scale,
            role * role_scale,
        ],
        axis=0,
    ).astype(bf16)


def power(u):
    return jnp.exp2(jnp.log2(u) * -2.25)


def box_perm(side):
    order = []
    for e in (0, 1):
        for f in (0, 1):
            for b in range(side):
                for a in range(side):
                    for c in (0, 1):
                        order.append(((2 * b + f) * 2 * side + 2 * a + e) * 2 + c)
    out = np.zeros((len(order), len(order)), np.float32)
    out[np.arange(len(order)), order] = 1.0
    return out


def eye(n):
    return (
        lax.broadcasted_iota(jnp.int32, (n, n), 0) == lax.broadcasted_iota(jnp.int32, (n, n), 1)
    ).astype(bf16)


def split_into(source, hi, lo, first):
    def part(i, carry):
        rows = pl.ds(pl.multiple_of(i * 64, 64), 64)
        for n in range(source.shape[0]):
            w = source[n, rows, :]
            h = w.astype(bf16)
            hi[first + n, rows, :] = h
            lo[first + n, rows, :] = (w - h.astype(f32)).astype(bf16)
        return carry

    lax.fori_loop(0, 4, part, 0)


def dot3(x, hi, lo):
    n = x.shape[0]
    top = x.astype(bf16).astype(f32)
    both = jnp.concatenate([top, x - top], axis=0).astype(bf16)
    main = dot(both, hi)
    if n % 16:
        rest = dot(both, lo)
        return main[:n] + main[n:] + rest[:n]
    return main[:n] + main[n:] + dot(top.astype(bf16), lo)


def permute(perm, x):
    hi, mid, lo = split3(x)
    out = dot(perm, jnp.concatenate([hi, mid, lo], axis=1).astype(bf16))
    return out[:, :256] + out[:, 256:512] + out[:, 512:]


def gather4(blocks, hi, lo, first):
    n = blocks.shape[0] // 4
    total = None
    for p in range(4):
        term = dot3(blocks[p * n : (p + 1) * n], hi[first + p], lo[first + p])
        total = term if total is None else total + term
    return total


def pairs(ref, *index):
    even = ref[(*index, pl.ds(0, NX // 2, stride=2))]
    odd = ref[(*index, pl.ds(1, NX // 2, stride=2))]
    return jnp.concatenate([even, odd], axis=1)


def live_pairs(counts, a):
    n = counts[pl.ds(pl.multiple_of(a * 8, 8), 8), :]
    lane = lax.broadcasted_iota(jnp.int32, (8, 128), 1)
    return lax.rem(lane, 64) < jnp.where(lane < 64, n[:, 0:1], n[:, 1:2])


def pad_points(points):
    return jnp.concatenate([points[...], jnp.zeros((5, 256), f32)], axis=0)


def upward_kernel(
    coords, weights, solution, counts, check_pts, solve, up_child, pair_up, perm8, perm4,
    feats, pts, boxes, gy_next, gy_prev, gx_edge, up_out,
    u0, u1, w0, w1, pot, hi, lo,
):
    check_cols = col_feats(pad_points(check_pts), 0.0)
    ident = eye(128)
    split_into(solve, hi, lo, 0)
    split_into(up_child, hi, lo, 1)
    split_into(pair_up, hi, lo, 5)

    def prepare(a, u, w):
        alive = live_pairs(counts, a)
        weight = jnp.where(alive, pairs(weights, a), 0.0)
        parts = [pairs(coords, c, a) for c in range(3)]
        parts += [weight, weight * pairs(solution, a)]
        zero = jnp.zeros((3, 128), f32)
        block = jnp.concatenate(
            [
                jnp.concatenate([x[m : m + 1] for x in parts] + [zero], axis=0)
                for m in range(NX // 2)
            ],
            axis=1,
        )
        pts[a] = block
        rows = row_feats(block)
        for m in range(NX // 2):
            lanes = slice(128 * m, 128 * m + 128)
            f = dot_t(ident, rows[:, lanes]).astype(bf16)
            feats[pl.ds(pl.multiple_of(a * LANES + 128 * m, 128), 128), :] = f
            w[lanes, :] = jnp.transpose(block[:, lanes])
            u[lanes, :] = dot(f, check_cols)

    def finish(a, u, w):
        for m in range(NX // 2):
            for half in range(2):
                span = slice(128 * m + 64 * half, 128 * m + 64 * half + 64)
                k = power(u[span, :])
                at = (lax.rem(a, 2) * 2 + half) * 128 + m * 16 + lax.div(a, 2) * 2
                for c in range(2):
                    pot[pl.ds(at + c, 1), :] = jnp.sum(
                        k * w[span, 3 + c : 4 + c], axis=0, keepdims=True
                    )

    prepare(0, u0, w0)

    def step(i, carry):
        prepare(2 * i + 1, u1, w1)
        finish(2 * i, u0, w0)
        prepare(jnp.minimum(2 * i + 2, NX - 1), u0, w0)
        finish(2 * i + 1, u1, w1)
        return carry

    lax.fori_loop(0, NX // 2, step, 0)
    leaf = dot3(pot[...], hi[0], lo[0])
    parent = permute(perm8[...], gather4(leaf, hi, lo, 1))
    leaf_r = leaf.astype(bf16).astype(f32)
    parent_r = parent.astype(bf16).astype(f32)
    for p in range(4):
        own = leaf_r[128 * p : 128 * p + 128]
        coarse = parent_r[32 * p : 32 * p + 32]
        for b in range(8):
            boxes[p, b] = own[16 * b : 16 * b + 16]
        for b in range(4):
            boxes[p, 8 + b, 0:8] = coarse[8 * b : 8 * b + 8]
            boxes[p, 8 + b, 8:16] = jnp.zeros((8, 256), f32)
        for msg, b, bb in ((gy_next, 7, 3), (gy_prev, 0, 0)):
            msg[16 * p : 16 * p + 16, :] = own[16 * b : 16 * b + 16]
            msg[64 + 8 * p : 72 + 8 * p, :] = coarse[8 * bb : 8 * bb + 8]
        for e in range(2):
            for c in range(2):
                at = 64 * c + 16 * p
                for b in range(8):
                    row = 16 * b + 14 * e + c
                    gx_edge[e, at + 1 + b : at + 2 + b, :] = own[row : row + 1]
                for b in range(4):
                    row = 8 * b + 6 * e + c
                    gx_edge[e, at + 11 + b : at + 12 + b, :] = coarse[row : row + 1]
                for gap in (0, 9, 10, 15):
                    gx_edge[e, at + gap : at + gap + 1, :] = jnp.zeros((1, 256), f32)
    for msg, start in ((gy_next, LANES - 64), (gy_prev, 0)):
        for k in range(4):
            piece = pts[4 * k : 4 * k + 4, :, start : start + 64].reshape(32, 64)
            msg[96:128, 64 * k : 64 * k + 64] = piece
    for e, t in ((0, 0), (1, NX - 1)):
        for k in range(4):
            gx_edge[e, 128 + 8 * k : 136 + 8 * k, :] = pts[t, :, 256 * k : 256 * k + 256]
        gx_edge[e, 160:168, :] = jnp.zeros((8, 256), f32)
    grand = permute(perm4[...], gather4(parent, hi, lo, 1))
    great = gather4(grand, hi, lo, 1)
    vec = None
    for b in range(2):
        for a in range(2):
            at = (b * 2 + a) * 2
            rows = jnp.concatenate([great[at : at + 2]] * 4, axis=0)
            term = dot3(rows, hi[1 + 2 * a + b], lo[1 + 2 * a + b])
            vec = term if vec is None else vec + term
    for axis, bits in ((1, 4), (0, 3)):
        place = lax.axis_index(AXES[axis])
        for bit in range(bits):
            n = 5 + lax.rem(lax.div(place, 2**bit), 2)
            vec = dot3(vec, hi[n], lo[n])
    up_out[...] = vec


def pack_kernel(low, high, edge, out):
    out[...] = edge[...]
    for e in range(2):
        for p in range(4):
            for c in range(2):
                at = 64 * c + 16 * p
                fine = 16 * p + 14 * e + c
                coarse = 64 + 8 * p + 6 * e + c
                for gap, ref, row in (
                    (0, low, fine), (9, high, fine), (10, low, coarse), (15, high, coarse)
                ):
                    out[e, at + gap : at + gap + 1, :] = ref[row : row + 1, :]
        rows = slice(96, 104) if e == 0 else slice(120, 128)
        lanes = slice(0, 64) if e == 0 else slice(192, 256)
        out[e, 160:168, 0:64] = low[rows, lanes]
        out[e, 160:168, 64:128] = high[rows, lanes]


def role_tiles():
    def column(sx, sy):
        return [-10.0 * sx] * 3 + [-10.0 * sy] * 3 + [float(sx * sx + sy * sy), 0.0] + [
            float(sx)
        ] * 3 + [float(sy)] * 3 + [0.0, 0.0]
    pairs = [((t, -1), (t, 0)) for t in (-1, 0, 1)] + [((-1, 1), (0, 1)), ((1, 1), (1, 1))]
    out = np.zeros((5, 16, 128), np.float32)
    for n, (left, right) in enumerate(pairs):
        out[n, :, :64] = np.array(column(*left))[:, None]
        out[n, :, 64:] = np.array(column(*right))[:, None]
    return out


def sum_lanes(acc0, acc1):
    row = lax.broadcasted_iota(jnp.int32, (8, 256), 0)
    total = None
    for c, acc in enumerate((acc0, acc1)):
        hi = acc.astype(bf16)
        lo = (acc - hi.astype(f32)).astype(bf16)
        ones = jnp.where(row == c, 1.0, 0.0).astype(bf16)
        term = dot_t(ones, jnp.concatenate([hi, lo], axis=1))
        total = term if total is None else total + term
    return total


def middle_kernel(
    pts, gy_low, gy_high, gx_low, gx_high, feats, boxes, roles, transfer_hbm,
    near, leaf_out, parent_out,
    transfer, arrived, dens0, dens1, cols0, cols1, u0, u1, extended, windows,
):
    fetch = pltpu.make_async_copy(transfer_hbm, transfer, arrived)
    fetch.start()
    first = lax.broadcasted_iota(jnp.int32, (1, 128), 1) < 64
    first_cols = lax.broadcasted_iota(jnp.int32, (FEATS, 128), 1) < 64

    for t in range(NX + 2):
        if t in (0, NX + 1):
            ref = gx_low if t == 0 else gx_high
            own = jnp.concatenate([ref[128 + 8 * k : 136 + 8 * k, :] for k in range(4)], axis=1)
            low, high = ref[160:168, 0:64], ref[160:168, 64:128]
        else:
            s = t - 1
            rows = slice(96 + 8 * (s % 4), 104 + 8 * (s % 4))
            lanes = slice(64 * (s // 4), 64 * (s // 4) + 64)
            own, low, high = pts[s], gy_low[rows, lanes], gy_high[rows, lanes]
        dens0[t, :, 0:64] = low
        dens0[t, :, 64 : 64 + LANES] = own
        dens0[t, :, 64 + LANES :] = high
        dens1[t, :, 0:LANES] = own
        dens1[t, :, LANES : LANES + 64] = high
        dens1[t, :, LANES + 64 :] = jnp.zeros((8, 64), f32)

    def prepare(t, carry):
        cols0[t] = col_feats(dens0[t])
        cols1[t] = col_feats(dens1[t])
        return carry

    lax.fori_loop(0, NX + 2, prepare, 0)

    def distances(a, half, u):
        for mm in range(4):
            base = half * 512 + mm * 128
            here, after = slice(base, base + 128), slice(base + 128, base + 256)
            for odd in range(2):
                own, other = ((cols0, cols1), (cols1, cols0))[odd]
                far = here if odd == 0 else after
                blocks = [own[a + t, :, here] for t in range(3)]
                blocks.append(jnp.where(first_cols, own[a, :, after], other[a + 1, :, far]))
                blocks.append(own[a + 2, :, after])
                blocks = [
                    jnp.concatenate([x[:48], x[48:] * roles[n]], axis=0)
                    for n, x in enumerate(blocks)
                ]
                start = pl.multiple_of(a * LANES + base + 64 * odd, 64)
                rows = feats[pl.ds(start, 64), :]
                at = 64 * (2 * mm + odd)
                u[at : at + 64, :] = dot(rows, jnp.concatenate(blocks, axis=1))

    def finish(a, half, u):
        for mm in range(4):
            base = half * 512 + mm * 128
            here, after = slice(base, base + 128), slice(base + 128, base + 256)
            sums = []
            for odd in range(2):
                d_own, d_other = ((dens0, dens1), (dens1, dens0))[odd]
                far = here if odd == 0 else after
                accs = [None, None]
                at = 64 * (2 * mm + odd)
                for n in range(5):
                    k = power(u[at : at + 64, 128 * n : 128 * n + 128])
                    for c in range(2):
                        r = slice(3 + c, 4 + c)
                        if n < 3:
                            dens = d_own[a + n, r, here]
                        elif n == 3:
                            dens = jnp.where(first, d_own[a, r, after], d_other[a + 1, r, far])
                        else:
                            dens = jnp.where(first, d_own[a + 2, r, after], 0.0)
                        term = k * dens
                        accs[c] = term if n == 0 else accs[c] + term
                sums.append(accs)
            both = [jnp.concatenate([sums[0][c], sums[1][c]], axis=0) for c in range(2)]
            total = sum_lanes(*both)
            for c in range(2):
                near[c, pl.ds(a * 8 + half * 4 + mm, 1), :] = total[c : c + 1]

    distances(0, 0, u0)

    def step(a, carry):
        distances(a, 1, u1)
        finish(a, 0, u0)
        distances(jnp.minimum(a + 1, NX - 1), 0, u0)
        finish(a, 1, u1)
        return carry

    lax.fori_loop(0, NX, step, 0)

    blank = jnp.zeros((8, 256), f32)
    for p in range(4):
        for slot in range(16):
            n = p * 16 + slot
            own_rows = extended.at[p, slot]
            if slot in (0, 9):
                own_rows[8:24, :] = (gy_low if slot == 0 else gy_high)[16 * p : 16 * p + 16, :]
            elif slot in (10, 15):
                ref = gy_low if slot == 10 else gy_high
                own_rows[8:16, :] = ref[64 + 8 * p : 72 + 8 * p, :]
                own_rows[16:24, :] = blank
            else:
                own_rows[8:24, :] = boxes[p, slot - 1 if slot < 9 else slot - 3]
            end = 24 if slot < 10 else 16
            for c in range(2):
                row = 64 * c + n
                own_rows[6 + c : 7 + c, :] = gx_low[row : row + 1, :]
                own_rows[end + c : end + c + 1, :] = gx_high[row : row + 1, :]
            if slot >= 10:
                own_rows[24:26, :] = jnp.zeros((2, 256), f32)
            for d in range(3):
                windows[p, d, slot] = own_rows[6 + 2 * d : 22 + 2 * d, :].astype(bf16)
    fetch.wait()
    far_level(windows, transfer, leaf_out, parent_out)


def reachable(parity, shift):
    return abs((parity + shift) // 2) <= 1


def far_level(boxes, transfer, leaf_out, parent_out):
    for px in (0, 1):
        for py in (0, 1):
            total = None
            for number, (sx, sy) in enumerate(far_offsets()):
                if not (reachable(px, sx) and reachable(py, sy)):
                    continue
                dx, dy = (px + sx) // 2, (py + sy) // 2
                source = (px + sx) % 2 * 2 + (py + sy) % 2
                window = jnp.concatenate(
                    [
                        boxes[source, dx + 1, 1 + dy : 9 + dy].reshape(128, 256),
                        boxes[source, dx + 1, 11 + dy : 15 + dy].reshape(64, 256),
                    ],
                    axis=0,
                )
                term = dot(window, transfer[number])
                total = term if total is None else total + term
            p = px * 2 + py
            leaf_out[128 * p : 128 * p + 128, :] = total[:128]
            for b in range(4):
                at = 32 * p + 8 * b
                parent_out[at : at + 8, :] = total[128 + 16 * b : 136 + 16 * b]


def downward_kernel(
    gathered, lattice, pair_down, down_child, perm8, perm4, far_leaf, far_parent,
    equiv_pts, feats, near, solution, source, counts, out, local, pot, u0, u1, hi, lo,
):
    split_into(lattice, hi, lo, 0)
    split_into(pair_down, hi, lo, 1)
    split_into(down_child, hi, lo, 3)
    vec = jnp.sum(gathered[...], axis=0)
    vec = dot3(jnp.concatenate([vec] * 4, axis=0), hi[0], lo[0])
    for axis, bits in ((0, 3), (1, 4)):
        place = lax.axis_index(AXES[axis])
        for bit in reversed(range(bits)):
            n = 1 + lax.rem(lax.div(place, 2**bit), 2)
            vec = dot3(vec, hi[n], lo[n])
    child = lambda x, p: dot3(x, hi[3 + p], lo[3 + p])
    great = jnp.concatenate([child(vec, 2 * a + b)[:2] for b in range(2) for a in range(2)], axis=0)
    spread = lambda x: jnp.concatenate([child(x, p) for p in range(4)], axis=0)
    grand = permute(perm4[...], spread(great))
    parent = spread(grand) + far_parent[...]
    parent = permute(perm8[...], parent)
    local[...] = spread(parent) + far_leaf[...]
    equiv_cols = col_feats(pad_points(equiv_pts), 0.0)

    def distances(a, half, u):
        rows = feats[pl.ds(pl.multiple_of(a * LANES + half * 512, 512), 512), :]
        u[...] = dot(rows, equiv_cols)

    def finish(a, half, u):
        for mm in range(4):
            m = half * 4 + mm
            accs = [[], []]
            for odd in range(2):
                at = 64 * (2 * mm + odd)
                k = power(u[at : at + 64, :])
                for c in range(2):
                    row = (lax.rem(a, 2) * 2 + odd) * 128 + m * 16 + lax.div(a, 2) * 2 + c
                    weight = local[pl.ds(row, 1), :]
                    accs[c].append(k[:, :128] * weight[:, :128] + k[:, 128:] * weight[:, 128:])
            total = sum_lanes(*[jnp.concatenate(x, axis=0) for x in accs])
            for c in range(2):
                pot[c, pl.ds(a * 8 + m, 1), :] = total[c : c + 1]

    distances(0, 0, u0)

    def step(a, carry):
        distances(a, 1, u1)
        finish(a, 0, u0)
        distances(jnp.minimum(a + 1, NX - 1), 0, u0)
        finish(a, 1, u1)
        return carry

    lax.fori_loop(0, NX, step, 0)
    for a in range(NX):
        rows = slice(8 * a, 8 * a + 8)
        total = [pot[c, rows, :] + near[c, rows, :] for c in range(2)]
        value = pairs(source, a) - scale_frac * (pairs(solution, a) * total[0] - total[1])
        value = jnp.where(live_pairs(counts, a), value, 0.0)
        out[a, pl.ds(0, NX // 2, stride=2), :] = value[:, :64]
        out[a, pl.ds(1, NX // 2, stride=2), :] = value[:, 64:]


def ring(axis, step):
    count = lax.axis_size(axis)
    return [(i, (i + step) % count) for i in range(count)]


def call(kernel, in_specs, out_shape, scratch):
    return pl.pallas_call(
        kernel,
        out_shape=out_shape,
        in_specs=in_specs,
        out_specs=jax.tree.map(lambda _: VMEM, out_shape),
        scratch_shapes=scratch,
        compiler_params=PARAMS,
    )


def shape(*dims, dtype=f32):
    return jax.ShapeDtypeStruct(dims, dtype)


def shards(
    coords, weights, solution, source, counts, check_points, equiv_points, check_solve,
    up_children, far_transfer, down_children, pair_up, lattice_map, pair_down,
):
    counts = counts.reshape(NX * NX // 2, 2)
    perm8, perm4 = box_perm(4), box_perm(2)
    halves = [pltpu.VMEM((7, 256, 256), bf16)] * 2
    feats, pts, boxes, gy_next, gy_prev, gx_edge, up = call(
        upward_kernel,
        [VMEM] * 10,
        (
            shape(NX * LANES, FEATS, dtype=bf16),
            shape(NX, 8, LANES),
            shape(4, 12, 16, 256),
            shape(128, 256),
            shape(128, 256),
            shape(2, 168, 256),
            shape(8, 256),
        ),
        [pltpu.VMEM((LANES, 256), f32)] * 2
        + [pltpu.VMEM((LANES, 8), f32)] * 2
        + [pltpu.VMEM((512, 256), f32)]
        + halves,
    )(
        coords, weights, solution, counts, check_points, check_solve[None], up_children, pair_up,
        jnp.asarray(perm8, bf16), jnp.asarray(perm4, bf16),
    )
    gy_low = lax.ppermute(gy_next, "gy", ring("gy", 1))
    gy_high = lax.ppermute(gy_prev, "gy", ring("gy", -1))
    edge = call(pack_kernel, [VMEM] * 3, shape(2, 168, 256), [])(gy_low, gy_high, gx_edge)
    gx_low = lax.ppermute(edge[1], "gx", ring("gx", 1))
    gx_high = lax.ppermute(edge[0], "gx", ring("gx", -1))
    gathered = lax.all_to_all(
        jnp.broadcast_to(up[None, :2], (128, 2, 256)), AXES, 0, 0, tiled=True
    )
    near, far_leaf, far_parent = call(
        middle_kernel,
        [VMEM] * 8 + [pl.BlockSpec(memory_space=pl.ANY)],
        (shape(2, 128, 128), shape(512, 256), shape(128, 256)),
        [pltpu.VMEM((40, 256, 256), bf16), pltpu.SemaphoreType.DMA]
        + [pltpu.VMEM((NX + 2, 8, PADDED), f32)] * 2
        + [pltpu.VMEM((NX + 2, FEATS, PADDED), bf16)] * 2
        + [pltpu.VMEM((512, 640), f32)] * 2
        + [pltpu.VMEM((4, 16, 32, 256), f32), pltpu.VMEM((4, 3, 16, 16, 256), bf16)],
    )(
        pts, gy_low, gy_high, gx_low, gx_high, feats, boxes, jnp.asarray(role_tiles(), bf16),
        far_transfer,
    )
    return call(
        downward_kernel,
        [VMEM] * 14,
        shape(NX, NX, 64),
        [pltpu.VMEM((512, 256), f32), pltpu.VMEM((2, 128, 128), f32)]
        + [pltpu.VMEM((512, 256), f32)] * 2
        + halves,
    )(
        gathered, lattice_map[None], pair_down, down_children,
        jnp.asarray(perm8.T, bf16), jnp.asarray(perm4.T, bf16), far_leaf, far_parent,
        equiv_points, feats, near, solution, source, counts,
    )


def solution(mesh):
    box = P("gx", "gy", None)
    return jax.shard_map(
        shards,
        mesh=mesh,
        in_specs=(P(None, "gx", "gy", None), box, box, box, P("gx", "gy")) + (P(),) * 9,
        out_specs=box,
        check_vma=False,
    )
```

```python
import jax
import jax.numpy as jnp
import numpy as np
from jax import lax
from jax.experimental import pallas as pl
from jax.experimental.pallas import tpu as pltpu
from jax.sharding import PartitionSpec as P

f32 = jnp.float32
bf16 = jnp.bfloat16
scale_frac = 0.4
NX = 16
LANES = NX * 64
PADDED = LANES + 128
FEATS = 64
AXES = ("gx", "gy")
VMEM = pl.BlockSpec(memory_space=pltpu.VMEM)
PARAMS = pltpu.CompilerParams(vmem_limit_bytes=60 << 20)


def far_offsets():
    return [
        (x, y) for x in range(-3, 4) for y in range(-3, 4) if max(abs(x), abs(y)) >= 2
    ]


def dot(a, b):
    return jnp.dot(a, b, preferred_element_type=f32)


def dot_t(a, b):
    return lax.dot_general(a, b, (((1,), (1,)), ((), ())), preferred_element_type=f32)


def split3(block):
    hi = block.astype(bf16).astype(f32)
    rest = block - hi
    mid = rest.astype(bf16).astype(f32)
    return hi, mid, rest - mid


def centred(block):
    row = lax.broadcasted_iota(jnp.int32, block.shape, 0)
    moved = jnp.where(row < 3, 5.0 * block - 2.5, 0.0)
    return row, moved, jnp.sum(moved * moved, axis=0, keepdims=True)


def row_feats(block):
    row, moved, norm = centred(block)
    packed = jnp.where(
        row < 3, moved, jnp.where(row == 5, norm + 1.0, jnp.where(row == 6, 1.0, 0.0))
    )
    hi, mid, lo = split3(packed)
    role = jnp.concatenate(
        [hi[0:1], mid[0:1], lo[0:1], hi[1:2], mid[1:2], lo[1:2], hi[6:7] * 25.0, hi[7:8]], axis=0
    )
    tens = jnp.where(row < 6, 10.0, 0.0)
    return jnp.concatenate([hi, hi, hi, mid, mid, lo, role, tens], axis=0).astype(bf16)


def col_feats(block, role_scale=1.0):
    row, moved, norm = centred(block)
    packed = jnp.where(row < 3, moved, jnp.where(row == 6, norm, 0.0))
    hi, mid, lo = split3(packed)
    one = jnp.where(row == 5, 1.0, 0.0)
    def part(value, marks, keep_norm):
        out = jnp.where(row < 3, value * -2.0, 0.0)
        if keep_norm:
            out = jnp.where(row == 6, value, out)
        return out + one if marks else out
    ones = jnp.where(row < 7, 1.0, 0.0)
    role = jnp.concatenate(
        [hi[0:1], mid[0:1], lo[0:1], hi[1:2], mid[1:2], lo[1:2], hi[7:8], hi[7:8]], axis=0
    )
    return jnp.concatenate(
        [
            part(hi, True, True),
            part(mid, False, True),
            part(lo, False, True),
            part(hi, True, False),
            part(mid, False, False),
            part(hi, True, False),
            ones * role_scale,
            role * role_scale,
        ],
        axis=0,
    ).astype(bf16)


def power(u):
    return jnp.exp2(jnp.log2(u) * -2.25)


def box_perm(side):
    order = []
    for e in (0, 1):
        for f in (0, 1):
            for b in range(side):
                for a in range(side):
                    for c in (0, 1):
                        order.append(((2 * b + f) * 2 * side + 2 * a + e) * 2 + c)
    out = np.zeros((len(order), len(order)), np.float32)
    out[np.arange(len(order)), order] = 1.0
    return out


def eye(n):
    return (
        lax.broadcasted_iota(jnp.int32, (n, n), 0) == lax.broadcasted_iota(jnp.int32, (n, n), 1)
    ).astype(bf16)


def split_into(source, hi, lo, first):
    def part(i, carry):
        rows = pl.ds(pl.multiple_of(i * 64, 64), 64)
        for n in range(source.shape[0]):
            w = source[n, rows, :]
            h = w.astype(bf16)
            hi[first + n, rows, :] = h
            lo[first + n, rows, :] = (w - h.astype(f32)).astype(bf16)
        return carry

    lax.fori_loop(0, 4, part, 0)


def dot3(x, hi, lo):
    n = x.shape[0]
    top = x.astype(bf16).astype(f32)
    both = jnp.concatenate([top, x - top], axis=0).astype(bf16)
    main = dot(both, hi)
    if n % 16:
        rest = dot(both, lo)
        return main[:n] + main[n:] + rest[:n]
    return main[:n] + main[n:] + dot(top.astype(bf16), lo)


def permute(perm, x):
    hi, mid, lo = split3(x)
    out = dot(perm, jnp.concatenate([hi, mid, lo], axis=1).astype(bf16))
    return out[:, :256] + out[:, 256:512] + out[:, 512:]


def gather4(blocks, hi, lo, first):
    n = blocks.shape[0] // 4
    total = None
    for p in range(4):
        term = dot3(blocks[p * n : (p + 1) * n], hi[first + p], lo[first + p])
        total = term if total is None else total + term
    return total


def pairs(ref, *index):
    even = ref[(*index, pl.ds(0, NX // 2, stride=2))]
    odd = ref[(*index, pl.ds(1, NX // 2, stride=2))]
    return jnp.concatenate([even, odd], axis=1)


def live_pairs(counts, a):
    row = counts[pl.ds(a, 1), :].astype(f32)
    box = lax.broadcasted_iota(jnp.int32, (NX // 2, NX), 1)
    pair = 2 * lax.broadcasted_iota(jnp.int32, (NX // 2, NX), 0)
    n = [jnp.sum(jnp.where(box == pair + odd, row, 0.0), axis=1, keepdims=True) for odd in (0, 1)]
    lane = lax.broadcasted_iota(jnp.int32, (NX // 2, 128), 1)
    return lax.rem(lane, 64).astype(f32) < jnp.where(lane < 64, n[0], n[1])


def two_parts(x):
    hi = x.astype(bf16)
    return hi, (x - hi.astype(f32)).astype(bf16)


def pad_points(points):
    return jnp.concatenate([points[...], jnp.zeros((5, 256), f32)], axis=0)


def upward_kernel(
    coords, weights, solution, counts, check_pts, solve, up_child, pair_up, perm8, perm4,
    feats, pts, boxes, gy_next, gy_prev, gx_edge, up_out,
    u0, u1, densities, pot, hi, lo, kept, kept_sem,
):
    check_cols = col_feats(pad_points(check_pts), 0.0)
    ident = eye(128)
    split_into(solve, hi, lo, 0)
    split_into(up_child, hi, lo, 1)
    split_into(pair_up, hi, lo, 5)

    row8 = lax.broadcasted_iota(jnp.int32, (8, 128), 0)
    lane8 = lax.broadcasted_iota(jnp.int32, (8, 128), 1)
    own_half = lax.rem(lax.div(row8, 2), 2) == lax.div(lane8, 64)

    def prepare(i, carry):
        for a in (2 * i, 2 * i + 1):
            weight = jnp.where(live_pairs(counts, a), pairs(weights, a), 0.0)
            parts = [pairs(coords, c, a) for c in range(3)]
            parts += [weight, weight * pairs(solution, a)]
            zero = jnp.zeros((3, 128), f32)
            for m in range(NX // 2):
                lanes = slice(128 * m, 128 * m + 128)
                block = jnp.concatenate([x[m : m + 1] for x in parts] + [zero], axis=0)
                pts[a, :, lanes] = block
                f = dot_t(ident, row_feats(block)).astype(bf16)
                kept[pl.ds(pl.multiple_of(a * LANES + 128 * m, 128), 128), :] = f
                both = [x[m : m + 1] for x in parts[3:]]
                dens = jnp.where(own_half, jnp.concatenate(both * 4, axis=0), 0.0)
                high = dens.astype(bf16).astype(f32)
                at = pl.multiple_of(a * 64 + 8 * m, 8)
                densities[pl.ds(at, 8), 0:128] = jnp.where(row8 < 4, high, dens - high)
                densities[pl.ds(at, 8), 128:256] = jnp.where(row8 < 4, high, 0.0)
        return carry

    lax.fori_loop(0, NX // 2, prepare, 0)
    keep = pltpu.make_async_copy(kept, feats, kept_sem)
    keep.start()

    def distances(a, m, u):
        rows = kept[pl.ds(pl.multiple_of(a * LANES + 128 * m, 128), 128), :]
        at = 128 * (m % 4)
        u[at : at + 128, :] = dot(rows, check_cols)

    def finish(a, m, u):
        at = 128 * (m % 4)
        k_hi, k_lo = two_parts(power(u[at : at + 128, :]))
        dens = densities[pl.ds(pl.multiple_of(a * 64 + 8 * m, 8), 8), :].astype(bf16)
        sums = dot(dens, jnp.concatenate([k_hi, k_lo], axis=0))
        sums = sums[:4] + sums[4:]
        row = lax.rem(a, 2) * 256 + m * 16 + lax.div(a, 2) * 2
        for half in range(2):
            for c in range(2):
                n = 2 * half + c
                pot[pl.ds(row + 128 * half + c, 1), :] = sums[n : n + 1]

    for m in range(4):
        distances(0, m, u0)

    def step(a, carry):
        for m in range(4):
            finish(a, m, u0)
            distances(a, m + 4, u1)
        for m in range(4, 8):
            finish(a, m, u1)
            distances(jnp.minimum(a + 1, NX - 1), m - 4, u0)
        return carry

    lax.fori_loop(0, NX, step, 0)
    leaf = dot3(pot[...], hi[0], lo[0])
    parent = permute(perm8[...], gather4(leaf, hi, lo, 1))
    leaf_r = leaf.astype(bf16).astype(f32)
    parent_r = parent.astype(bf16).astype(f32)
    for p in range(4):
        own = leaf_r[128 * p : 128 * p + 128]
        coarse = parent_r[32 * p : 32 * p + 32]
        for b in range(8):
            boxes[p, b] = own[16 * b : 16 * b + 16]
        for b in range(4):
            boxes[p, 8 + b, 0:8] = coarse[8 * b : 8 * b + 8]
            boxes[p, 8 + b, 8:16] = jnp.zeros((8, 256), f32)
        for msg, b, bb in ((gy_next, 7, 3), (gy_prev, 0, 0)):
            msg[16 * p : 16 * p + 16, :] = own[16 * b : 16 * b + 16]
            msg[64 + 8 * p : 72 + 8 * p, :] = coarse[8 * bb : 8 * bb + 8]
        for e in range(2):
            for c in range(2):
                at = 64 * c + 16 * p
                for b in range(8):
                    row = 16 * b + 14 * e + c
                    gx_edge[e, at + 1 + b : at + 2 + b, :] = own[row : row + 1]
                for b in range(4):
                    row = 8 * b + 6 * e + c
                    gx_edge[e, at + 11 + b : at + 12 + b, :] = coarse[row : row + 1]
                for gap in (0, 9, 10, 15):
                    gx_edge[e, at + gap : at + gap + 1, :] = jnp.zeros((1, 256), f32)
    for msg, start in ((gy_next, LANES - 64), (gy_prev, 0)):
        for k in range(4):
            piece = pts[4 * k : 4 * k + 4, :, start : start + 64].reshape(32, 64)
            msg[96:128, 64 * k : 64 * k + 64] = piece
    for e, t in ((0, 0), (1, NX - 1)):
        for k in range(4):
            gx_edge[e, 128 + 8 * k : 136 + 8 * k, :] = pts[t, :, 256 * k : 256 * k + 256]
        gx_edge[e, 160:168, :] = jnp.zeros((8, 256), f32)
    grand = permute(perm4[...], gather4(parent, hi, lo, 1))
    great = gather4(grand, hi, lo, 1)
    vec = None
    for b in range(2):
        for a in range(2):
            at = (b * 2 + a) * 2
            rows = jnp.concatenate([great[at : at + 2]] * 4, axis=0)
            term = dot3(rows, hi[1 + 2 * a + b], lo[1 + 2 * a + b])
            vec = term if vec is None else vec + term
    for axis, bits in ((1, 4), (0, 3)):
        place = lax.axis_index(AXES[axis])
        for bit in range(bits):
            n = 5 + lax.rem(lax.div(place, 2**bit), 2)
            vec = dot3(vec, hi[n], lo[n])
    up_out[...] = jnp.broadcast_to(vec[None, :2], (128, 2, 256))
    keep.wait()


def pack_kernel(low, high, edge, first, last):
    for e, out in enumerate((first, last)):
        out[...] = edge[e]
        for p in range(4):
            for c in range(2):
                at = 64 * c + 16 * p
                fine = 16 * p + 14 * e + c
                coarse = 64 + 8 * p + 6 * e + c
                for gap, ref, row in (
                    (0, low, fine), (9, high, fine), (10, low, coarse), (15, high, coarse)
                ):
                    out[at + gap : at + gap + 1, :] = ref[row : row + 1, :]
        rows = slice(96, 104) if e == 0 else slice(120, 128)
        lanes = slice(0, 64) if e == 0 else slice(192, 256)
        out[160:168, 0:64] = low[rows, lanes]
        out[160:168, 64:128] = high[rows, lanes]


def role_tiles():
    def column(sx, sy):
        return [-10.0 * sx] * 3 + [-10.0 * sy] * 3 + [float(sx * sx + sy * sy), 0.0] + [
            float(sx)
        ] * 3 + [float(sy)] * 3 + [0.0, 0.0]
    pairs = [((t, -1), (t, 0)) for t in (-1, 0, 1)] + [((-1, 1), (0, 1)), ((1, 1), (1, 1))]
    out = np.zeros((5, 16, 128), np.float32)
    for n, (left, right) in enumerate(pairs):
        out[n, :, :64] = np.array(column(*left))[:, None]
        out[n, :, 64:] = np.array(column(*right))[:, None]
    return out


def sum_lanes(acc0, acc1):
    row = lax.broadcasted_iota(jnp.int32, (8, 256), 0)
    total = None
    for c, acc in enumerate((acc0, acc1)):
        hi = acc.astype(bf16)
        lo = (acc - hi.astype(f32)).astype(bf16)
        ones = jnp.where(row == c, 1.0, 0.0).astype(bf16)
        term = dot_t(ones, jnp.concatenate([hi, lo], axis=1))
        total = term if total is None else total + term
    return total


def middle_kernel(
    pts, gy_low, gy_high, gx_low, gx_high, boxes, roles, feats_hbm, transfer_hbm,
    near, leaf_out, parent_out,
    feats, feats_sem, transfer, arrived, dens0, dens1, cols0, cols1, u0, u1, extended, windows,
):
    load = pltpu.make_async_copy(feats_hbm, feats, feats_sem)
    load.start()
    fetch = pltpu.make_async_copy(transfer_hbm, transfer, arrived)
    fetch.start()
    first = lax.broadcasted_iota(jnp.int32, (1, 128), 1) < 64
    first_cols = lax.broadcasted_iota(jnp.int32, (FEATS, 128), 1) < 64

    for t in range(NX + 2):
        if t in (0, NX + 1):
            ref = gx_low if t == 0 else gx_high
            own = jnp.concatenate([ref[128 + 8 * k : 136 + 8 * k, :] for k in range(4)], axis=1)
            low, high = ref[160:168, 0:64], ref[160:168, 64:128]
        else:
            s = t - 1
            rows = slice(96 + 8 * (s % 4), 104 + 8 * (s % 4))
            lanes = slice(64 * (s // 4), 64 * (s // 4) + 64)
            own, low, high = pts[s], gy_low[rows, lanes], gy_high[rows, lanes]
        dens0[t, :, 0:64] = low
        dens0[t, :, 64 : 64 + LANES] = own
        dens0[t, :, 64 + LANES :] = high
        dens1[t, :, 0:LANES] = own
        dens1[t, :, LANES : LANES + 64] = high
        dens1[t, :, LANES + 64 :] = jnp.zeros((8, 64), f32)

    def prepare(t, carry):
        cols0[t] = col_feats(dens0[t])
        cols1[t] = col_feats(dens1[t])
        return carry

    lax.fori_loop(0, NX + 2, prepare, 0)

    def distances(a, half, u, mms=range(4)):
        for mm in mms:
            base = half * 512 + mm * 128
            here, after = slice(base, base + 128), slice(base + 128, base + 256)
            for odd in range(2):
                own, other = ((cols0, cols1), (cols1, cols0))[odd]
                far = here if odd == 0 else after
                blocks = [own[a + t, :, here] for t in range(3)]
                blocks.append(jnp.where(first_cols, own[a, :, after], other[a + 1, :, far]))
                blocks.append(own[a + 2, :, after])
                blocks = [
                    jnp.concatenate([x[:48], x[48:] * roles[n]], axis=0)
                    for n, x in enumerate(blocks)
                ]
                start = pl.multiple_of(a * LANES + base + 64 * odd, 64)
                rows = feats[pl.ds(start, 64), :]
                at = 64 * (2 * mm + odd)
                u[at : at + 64, :] = dot(rows, jnp.concatenate(blocks, axis=1))

    def finish(a, half, u, mms=range(4)):
        for mm in mms:
            base = half * 512 + mm * 128
            here, after = slice(base, base + 128), slice(base + 128, base + 256)
            sums = []
            for odd in range(2):
                d_own, d_other = ((dens0, dens1), (dens1, dens0))[odd]
                far = here if odd == 0 else after
                accs = [None, None]
                at = 64 * (2 * mm + odd)
                for n in range(5):
                    k = power(u[at : at + 64, 128 * n : 128 * n + 128])
                    for c in range(2):
                        r = slice(3 + c, 4 + c)
                        if n < 3:
                            dens = d_own[a + n, r, here]
                        elif n == 3:
                            dens = jnp.where(first, d_own[a, r, after], d_other[a + 1, r, far])
                        else:
                            dens = jnp.where(first, d_own[a + 2, r, after], 0.0)
                        term = k * dens
                        accs[c] = term if n == 0 else accs[c] + term
                sums.append(accs)
            both = [jnp.concatenate([sums[0][c], sums[1][c]], axis=0) for c in range(2)]
            total = sum_lanes(*both)
            for c in range(2):
                near[c, pl.ds(a * 8 + half * 4 + mm, 1), :] = total[c : c + 1]

    load.wait()
    distances(0, 0, u0)

    def step(a, carry):
        for mm in range(4):
            finish(a, 0, u0, (mm,))
            distances(a, 1, u1, (mm,))
        for mm in range(4):
            finish(a, 1, u1, (mm,))
            distances(jnp.minimum(a + 1, NX - 1), 0, u0, (mm,))
        return carry

    lax.fori_loop(0, NX, step, 0)

    blank = jnp.zeros((8, 256), f32)
    for p in range(4):
        for slot in range(16):
            n = p * 16 + slot
            own_rows = extended.at[p, slot]
            if slot in (0, 9):
                own_rows[8:24, :] = (gy_low if slot == 0 else gy_high)[16 * p : 16 * p + 16, :]
            elif slot in (10, 15):
                ref = gy_low if slot == 10 else gy_high
                own_rows[8:16, :] = ref[64 + 8 * p : 72 + 8 * p, :]
                own_rows[16:24, :] = blank
            else:
                own_rows[8:24, :] = boxes[p, slot - 1 if slot < 9 else slot - 3]
            end = 24 if slot < 10 else 16
            for c in range(2):
                row = 64 * c + n
                own_rows[6 + c : 7 + c, :] = gx_low[row : row + 1, :]
                own_rows[end + c : end + c + 1, :] = gx_high[row : row + 1, :]
            if slot >= 10:
                own_rows[24:26, :] = jnp.zeros((2, 256), f32)
            for d in range(3):
                windows[p, d, slot] = own_rows[6 + 2 * d : 22 + 2 * d, :].astype(bf16)
    fetch.wait()
    far_level(windows, transfer, leaf_out, parent_out)


def reachable(parity, shift):
    return abs((parity + shift) // 2) <= 1


def far_level(boxes, transfer, leaf_out, parent_out):
    for px in (0, 1):
        for py in (0, 1):
            total = None
            for number, (sx, sy) in enumerate(far_offsets()):
                if not (reachable(px, sx) and reachable(py, sy)):
                    continue
                dx, dy = (px + sx) // 2, (py + sy) // 2
                source = (px + sx) % 2 * 2 + (py + sy) % 2
                window = jnp.concatenate(
                    [
                        boxes[source, dx + 1, 1 + dy : 9 + dy].reshape(128, 256),
                        boxes[source, dx + 1, 11 + dy : 15 + dy].reshape(64, 256),
                    ],
                    axis=0,
                )
                term = dot(window, transfer[number])
                total = term if total is None else total + term
            p = px * 2 + py
            leaf_out[128 * p : 128 * p + 128, :] = total[:128]
            for b in range(4):
                at = 32 * p + 8 * b
                parent_out[at : at + 8, :] = total[128 + 16 * b : 136 + 16 * b]


def downward_kernel(
    gathered, lattice, pair_down, down_child, perm8, perm4, far_leaf, far_parent,
    equiv_pts, near, solution, source, counts, feats_hbm, out,
    local, pot, u0, u1, hi, lo, feats, feats_sem,
):
    load = pltpu.make_async_copy(feats_hbm, feats, feats_sem)
    load.start()
    split_into(lattice, hi, lo, 0)
    split_into(pair_down, hi, lo, 1)
    split_into(down_child, hi, lo, 3)
    vec = jnp.sum(gathered[...], axis=0)
    vec = dot3(jnp.concatenate([vec] * 4, axis=0), hi[0], lo[0])
    for axis, bits in ((0, 3), (1, 4)):
        place = lax.axis_index(AXES[axis])
        for bit in reversed(range(bits)):
            n = 1 + lax.rem(lax.div(place, 2**bit), 2)
            vec = dot3(vec, hi[n], lo[n])
    child = lambda x, p: dot3(x, hi[3 + p], lo[3 + p])
    great = jnp.concatenate([child(vec, 2 * a + b)[:2] for b in range(2) for a in range(2)], axis=0)
    spread = lambda x: jnp.concatenate([child(x, p) for p in range(4)], axis=0)
    grand = permute(perm4[...], spread(great))
    parent = spread(grand) + far_parent[...]
    parent = permute(perm8[...], parent)
    local[...] = spread(parent) + far_leaf[...]
    equiv_cols = col_feats(pad_points(equiv_pts), 0.0)

    first = lax.broadcasted_iota(jnp.int32, (2, 128), 1) < 64
    is_top = jnp.where(lax.broadcasted_iota(jnp.int32, (8, 128), 0) < 4, 1.0, 0.0)

    def distances(a, m, u):
        rows = feats[pl.ds(pl.multiple_of(a * LANES + 128 * m, 128), 128), :]
        at = 128 * (m % 4)
        u[at : at + 128, :] = dot(rows, equiv_cols)

    def finish(a, m, u):
        at = 128 * (m % 4)
        k_hi, k_lo = two_parts(power(u[at : at + 128, :]))
        row = lax.rem(a, 2) * 256 + m * 16 + lax.div(a, 2) * 2
        weight = jnp.concatenate(
            [local[pl.ds(row + 128 * half + c, 1), :] for half in range(2) for c in range(2)], axis=0
        )
        top = weight.astype(bf16).astype(f32)
        both = jnp.concatenate([top, weight - top], axis=0).astype(bf16)
        sums = dot_t(both, k_hi) + dot_t(jnp.concatenate([top, top], axis=0).astype(bf16), k_lo) * is_top
        sums = sums[:4] + sums[4:]
        total = jnp.where(first, sums[:2], sums[2:])
        for c in range(2):
            pot[c, pl.ds(a * 8 + m, 1), :] = total[c : c + 1]

    load.wait()
    for m in range(4):
        distances(0, m, u0)

    def step(a, carry):
        for m in range(4):
            finish(a, m, u0)
            distances(a, m + 4, u1)
        for m in range(4, 8):
            finish(a, m, u1)
            distances(jnp.minimum(a + 1, NX - 1), m - 4, u0)
        return carry

    lax.fori_loop(0, NX, step, 0)
    for a in range(NX):
        rows = slice(8 * a, 8 * a + 8)
        total = [pot[c, rows, :] + near[c, rows, :] for c in range(2)]
        value = pairs(source, a) - scale_frac * (pairs(solution, a) * total[0] - total[1])
        value = jnp.where(live_pairs(counts, a), value, 0.0)
        out[a, pl.ds(0, NX // 2, stride=2), :] = value[:, :64]
        out[a, pl.ds(1, NX // 2, stride=2), :] = value[:, 64:]


def ring(axis, step):
    count = lax.axis_size(axis)
    return [(i, (i + step) % count) for i in range(count)]


def call(kernel, in_specs, out_shape, scratch, out_specs=None):
    return pl.pallas_call(
        kernel,
        out_shape=out_shape,
        in_specs=in_specs,
        out_specs=out_specs or jax.tree.map(lambda _: VMEM, out_shape),
        scratch_shapes=scratch,
        compiler_params=PARAMS,
    )


def shape(*dims, dtype=f32):
    return jax.ShapeDtypeStruct(dims, dtype)


def shards(
    coords, weights, solution, source, counts, check_points, equiv_points, check_solve,
    up_children, far_transfer, down_children, pair_up, lattice_map, pair_down,
):
    perm8, perm4 = box_perm(4), box_perm(2)
    halves = [pltpu.VMEM((7, 256, 256), bf16)] * 2
    feats, pts, boxes, gy_next, gy_prev, gx_edge, up = call(
        upward_kernel,
        [VMEM] * 10,
        (
            shape(NX * LANES, FEATS, dtype=bf16),
            shape(NX, 8, LANES),
            shape(4, 12, 16, 256),
            shape(128, 256),
            shape(128, 256),
            shape(2, 168, 256),
            shape(128, 2, 256),
        ),
        [pltpu.VMEM((512, 256), f32)] * 2
        + [pltpu.VMEM((LANES, 256), f32)]
        + [pltpu.VMEM((512, 256), f32)]
        + halves
        + [pltpu.VMEM((NX * LANES, FEATS), bf16), pltpu.SemaphoreType.DMA],
        out_specs=(pl.BlockSpec(memory_space=pl.ANY),) + (VMEM,) * 6,
    )(
        coords, weights, solution, counts, check_points, check_solve[None], up_children, pair_up,
        jnp.asarray(perm8, bf16), jnp.asarray(perm4, bf16),
    )
    gy_low = lax.ppermute(gy_next, "gy", ring("gy", 1))
    gy_high = lax.ppermute(gy_prev, "gy", ring("gy", -1))
    first, last = call(pack_kernel, [VMEM] * 3, (shape(168, 256), shape(168, 256)), [])(
        gy_low, gy_high, gx_edge
    )
    gx_low = lax.ppermute(last, "gx", ring("gx", 1))
    gx_high = lax.ppermute(first, "gx", ring("gx", -1))
    gathered = lax.all_to_all(up, AXES, 0, 0, tiled=True)
    near, far_leaf, far_parent = call(
        middle_kernel,
        [VMEM] * 7 + [pl.BlockSpec(memory_space=pl.ANY)] * 2,
        (shape(2, 128, 128), shape(512, 256), shape(128, 256)),
        [pltpu.VMEM((NX * LANES, FEATS), bf16), pltpu.SemaphoreType.DMA]
        + [pltpu.VMEM((40, 256, 256), bf16), pltpu.SemaphoreType.DMA]
        + [pltpu.VMEM((NX + 2, 8, PADDED), f32)] * 2
        + [pltpu.VMEM((NX + 2, FEATS, PADDED), bf16)] * 2
        + [pltpu.VMEM((512, 640), f32)] * 2
        + [pltpu.VMEM((4, 16, 32, 256), f32), pltpu.VMEM((4, 3, 16, 16, 256), bf16)],
    )(
        pts, gy_low, gy_high, gx_low, gx_high, boxes, jnp.asarray(role_tiles(), bf16), feats,
        far_transfer,
    )
    return call(
        downward_kernel,
        [VMEM] * 13 + [pl.BlockSpec(memory_space=pl.ANY)],
        shape(NX, NX, 64),
        [pltpu.VMEM((512, 256), f32), pltpu.VMEM((2, 128, 128), f32)]
        + [pltpu.VMEM((512, 256), f32)] * 2
        + halves
        + [pltpu.VMEM((NX * LANES, FEATS), bf16), pltpu.SemaphoreType.DMA],
    )(
        gathered, lattice_map[None], pair_down, down_children,
        jnp.asarray(perm8.T, bf16), jnp.asarray(perm4.T, bf16), far_leaf, far_parent,
        equiv_points, near, solution, source, counts, feats,
    )


def solution(mesh):
    box = P("gx", "gy", None)
    return jax.shard_map(
        shards,
        mesh=mesh,
        in_specs=(P(None, "gx", "gy", None), box, box, box, P("gx", "gy")) + (P(),) * 9,
        out_specs=box,
        check_vma=False,
    )
```

```python
import jax
import jax.numpy as jnp
import numpy as np
from jax import lax
from jax.experimental import pallas as pl
from jax.experimental.pallas import tpu as pltpu
from jax.sharding import PartitionSpec as P

f32 = jnp.float32
bf16 = jnp.bfloat16
scale_frac = 0.4
NX = 16
LANES = NX * 64
PADDED = LANES + 128
FEATS = 64
AXES = ("gx", "gy")
VMEM = pl.BlockSpec(memory_space=pltpu.VMEM)
PARAMS = pltpu.CompilerParams(vmem_limit_bytes=60 << 20)


def far_offsets():
    return [
        (x, y) for x in range(-3, 4) for y in range(-3, 4) if max(abs(x), abs(y)) >= 2
    ]


def dot(a, b):
    return jnp.dot(a, b, preferred_element_type=f32)


def dot_t(a, b):
    return lax.dot_general(a, b, (((1,), (1,)), ((), ())), preferred_element_type=f32)


def split3(block):
    hi = block.astype(bf16).astype(f32)
    rest = block - hi
    mid = rest.astype(bf16).astype(f32)
    return hi, mid, rest - mid


def centred(block):
    row = lax.broadcasted_iota(jnp.int32, block.shape, 0)
    moved = jnp.where(row < 3, 5.0 * block - 2.5, 0.0)
    return row, moved, jnp.sum(moved * moved, axis=0, keepdims=True)


def row_feats(block):
    row, moved, norm = centred(block)
    packed = jnp.where(
        row < 3, moved, jnp.where(row == 5, norm + 1.0, jnp.where(row == 6, 1.0, 0.0))
    )
    hi, mid, lo = split3(packed)
    role = jnp.concatenate(
        [hi[0:1], mid[0:1], lo[0:1], hi[1:2], mid[1:2], lo[1:2], hi[6:7] * 25.0, hi[7:8]], axis=0
    )
    tens = jnp.where(row < 6, 10.0, 0.0)
    return jnp.concatenate([hi, hi, hi, mid, mid, lo, role, tens], axis=0).astype(bf16)


def col_feats(block, role_scale=1.0):
    row, moved, norm = centred(block)
    packed = jnp.where(row < 3, moved * -2.0, jnp.where(row == 6, norm, 0.0))
    hi, mid, lo = split3(packed)
    main = hi + jnp.where(row == 5, 1.0, 0.0)
    ones = jnp.where(row < 7, role_scale, 0.0)
    role = jnp.concatenate(
        [hi[0:1], mid[0:1], lo[0:1], hi[1:2], mid[1:2], lo[1:2], hi[7:8], hi[7:8]], axis=0
    )
    return jnp.concatenate(
        [main, mid, lo, main, mid, main, ones, role * role_scale], axis=0
    ).astype(bf16)


def power(u):
    return jnp.exp2(jnp.log2(u) * -2.25)


def box_perm(side):
    order = []
    for e in (0, 1):
        for f in (0, 1):
            for b in range(side):
                for a in range(side):
                    for c in (0, 1):
                        order.append(((2 * b + f) * 2 * side + 2 * a + e) * 2 + c)
    out = np.zeros((len(order), len(order)), np.float32)
    out[np.arange(len(order)), order] = 1.0
    return out


def eye(n):
    return (
        lax.broadcasted_iota(jnp.int32, (n, n), 0) == lax.broadcasted_iota(jnp.int32, (n, n), 1)
    ).astype(bf16)


def split_into(source, hi, lo, first):
    def part(i, carry):
        rows = pl.ds(pl.multiple_of(i * 64, 64), 64)
        for n in range(source.shape[0]):
            w = source[n, rows, :]
            h = w.astype(bf16)
            hi[first + n, rows, :] = h
            lo[first + n, rows, :] = (w - h.astype(f32)).astype(bf16)
        return carry

    lax.fori_loop(0, 4, part, 0)


def dot3(x, hi, lo):
    n = x.shape[0]
    top = x.astype(bf16).astype(f32)
    both = jnp.concatenate([top, x - top], axis=0).astype(bf16)
    main = dot(both, hi)
    if n % 16:
        rest = dot(both, lo)
        return main[:n] + main[n:] + rest[:n]
    return main[:n] + main[n:] + dot(top.astype(bf16), lo)


def permute(perm, x):
    hi, mid, lo = split3(x)
    out = dot(perm, jnp.concatenate([hi, mid, lo], axis=1).astype(bf16))
    return out[:, :256] + out[:, 256:512] + out[:, 512:]


def gather4(blocks, hi, lo, first):
    n = blocks.shape[0] // 4
    total = None
    for p in range(4):
        term = dot3(blocks[p * n : (p + 1) * n], hi[first + p], lo[first + p])
        total = term if total is None else total + term
    return total


def pairs(ref, *index):
    even = ref[(*index, pl.ds(0, NX // 2, stride=2))]
    odd = ref[(*index, pl.ds(1, NX // 2, stride=2))]
    return jnp.concatenate([even, odd], axis=1)


def live_pairs(counts, a):
    row = counts[pl.ds(a, 1), :].astype(f32)
    box = lax.broadcasted_iota(jnp.int32, (NX // 2, NX), 1)
    pair = 2 * lax.broadcasted_iota(jnp.int32, (NX // 2, NX), 0)
    n = [jnp.sum(jnp.where(box == pair + odd, row, 0.0), axis=1, keepdims=True) for odd in (0, 1)]
    lane = lax.broadcasted_iota(jnp.int32, (NX // 2, 128), 1)
    return lax.rem(lane, 64).astype(f32) < jnp.where(lane < 64, n[0], n[1])


def two_parts(x):
    hi = x.astype(bf16)
    return hi, (x - hi.astype(f32)).astype(bf16)


def pad_points(points):
    return jnp.concatenate([points[...], jnp.zeros((5, 256), f32)], axis=0)


def upward_kernel(
    coords, weights, solution, counts, check_pts, solve, up_child, pair_up, perm8, perm4,
    feats, pts, boxes, gy_next, gy_prev, gx_edge, up_out,
    u0, u1, densities, pot, hi, lo, kept, kept_sem,
):
    check_cols = col_feats(pad_points(check_pts), 0.0)
    ident = eye(128)
    split_into(solve, hi, lo, 0)
    split_into(up_child, hi, lo, 1)
    split_into(pair_up, hi, lo, 5)

    row8 = lax.broadcasted_iota(jnp.int32, (8, 128), 0)
    lane8 = lax.broadcasted_iota(jnp.int32, (8, 128), 1)
    own_half = lax.rem(lax.div(row8, 2), 2) == lax.div(lane8, 64)

    def prepare(i, carry):
        for a in (4 * i, 4 * i + 1, 4 * i + 2, 4 * i + 3):
            weight = jnp.where(live_pairs(counts, a), pairs(weights, a), 0.0)
            parts = [pairs(coords, c, a) for c in range(3)]
            parts += [weight, weight * pairs(solution, a)]
            zero = jnp.zeros((3, 128), f32)
            for m in range(NX // 2):
                lanes = slice(128 * m, 128 * m + 128)
                block = jnp.concatenate([x[m : m + 1] for x in parts] + [zero], axis=0)
                pts[a, :, lanes] = block
                f = dot_t(ident, row_feats(block)).astype(bf16)
                kept[pl.ds(pl.multiple_of(a * LANES + 128 * m, 128), 128), :] = f
                both = [x[m : m + 1] for x in parts[3:]]
                dens = jnp.where(own_half, jnp.concatenate(both * 4, axis=0), 0.0)
                high = dens.astype(bf16).astype(f32)
                at = pl.multiple_of(a * 64 + 8 * m, 8)
                densities[pl.ds(at, 8), 0:128] = jnp.where(row8 < 4, high, dens - high)
                densities[pl.ds(at, 8), 128:256] = jnp.where(row8 < 4, high, 0.0)
        return carry

    lax.fori_loop(0, NX // 4, prepare, 0)
    keep = pltpu.make_async_copy(kept, feats, kept_sem)
    keep.start()

    def distances(a, m, u):
        rows = kept[pl.ds(pl.multiple_of(a * LANES + 128 * m, 128), 128), :]
        at = 128 * (m % 4)
        u[at : at + 128, :] = dot(rows, check_cols)

    def finish(a, m, u):
        at = 128 * (m % 4)
        k_hi, k_lo = two_parts(power(u[at : at + 128, :]))
        dens = densities[pl.ds(pl.multiple_of(a * 64 + 8 * m, 8), 8), :].astype(bf16)
        sums = dot(dens, jnp.concatenate([k_hi, k_lo], axis=0))
        sums = sums[:4] + sums[4:]
        row = lax.rem(a, 2) * 256 + m * 16 + lax.div(a, 2) * 2
        for half in range(2):
            for c in range(2):
                n = 2 * half + c
                pot[pl.ds(row + 128 * half + c, 1), :] = sums[n : n + 1]

    for m in range(4):
        distances(0, m, u0)

    def step(i, carry):
        for a in (2 * i, 2 * i + 1):
            for m in range(4):
                distances(a, m + 4, u1)
                finish(a, m, u0)
            for m in range(4, 8):
                distances(jnp.minimum(a + 1, NX - 1), m - 4, u0)
                finish(a, m, u1)
        return carry

    lax.fori_loop(0, NX // 2, step, 0)
    leaf = dot3(pot[...], hi[0], lo[0])
    parent = permute(perm8[...], gather4(leaf, hi, lo, 1))
    leaf_r = leaf.astype(bf16).astype(f32)
    parent_r = parent.astype(bf16).astype(f32)
    for p in range(4):
        own = leaf_r[128 * p : 128 * p + 128]
        coarse = parent_r[32 * p : 32 * p + 32]
        for b in range(8):
            boxes[p, b] = own[16 * b : 16 * b + 16]
        for b in range(4):
            boxes[p, 8 + b, 0:8] = coarse[8 * b : 8 * b + 8]
            boxes[p, 8 + b, 8:16] = jnp.zeros((8, 256), f32)
        for msg, b, bb in ((gy_next, 7, 3), (gy_prev, 0, 0)):
            msg[16 * p : 16 * p + 16, :] = own[16 * b : 16 * b + 16]
            msg[64 + 8 * p : 72 + 8 * p, :] = coarse[8 * bb : 8 * bb + 8]
        for e in range(2):
            for c in range(2):
                at = 64 * c + 16 * p
                for b in range(8):
                    row = 16 * b + 14 * e + c
                    gx_edge[e, at + 1 + b : at + 2 + b, :] = own[row : row + 1]
                for b in range(4):
                    row = 8 * b + 6 * e + c
                    gx_edge[e, at + 11 + b : at + 12 + b, :] = coarse[row : row + 1]
                for gap in (0, 9, 10, 15):
                    gx_edge[e, at + gap : at + gap + 1, :] = jnp.zeros((1, 256), f32)
    for msg, start in ((gy_next, LANES - 64), (gy_prev, 0)):
        for k in range(4):
            piece = pts[4 * k : 4 * k + 4, :, start : start + 64].reshape(32, 64)
            msg[96:128, 64 * k : 64 * k + 64] = piece
    for e, t in ((0, 0), (1, NX - 1)):
        for k in range(4):
            gx_edge[e, 128 + 8 * k : 136 + 8 * k, :] = pts[t, :, 256 * k : 256 * k + 256]
        gx_edge[e, 160:168, :] = jnp.zeros((8, 256), f32)
    grand = permute(perm4[...], gather4(parent, hi, lo, 1))
    great = gather4(grand, hi, lo, 1)
    vec = None
    for b in range(2):
        for a in range(2):
            at = (b * 2 + a) * 2
            rows = jnp.concatenate([great[at : at + 2]] * 4, axis=0)
            term = dot3(rows, hi[1 + 2 * a + b], lo[1 + 2 * a + b])
            vec = term if vec is None else vec + term
    for axis, bits in ((1, 4), (0, 3)):
        place = lax.axis_index(AXES[axis])
        for bit in range(bits):
            n = 5 + lax.rem(lax.div(place, 2**bit), 2)
            vec = dot3(vec, hi[n], lo[n])
    up_out[...] = jnp.broadcast_to(vec[None, :2], (128, 2, 256))
    keep.wait()


def pack_kernel(low, high, edge, first, last):
    for e, out in enumerate((first, last)):
        out[...] = edge[e]
        for p in range(4):
            for c in range(2):
                at = 64 * c + 16 * p
                fine = 16 * p + 14 * e + c
                coarse = 64 + 8 * p + 6 * e + c
                for gap, ref, row in (
                    (0, low, fine), (9, high, fine), (10, low, coarse), (15, high, coarse)
                ):
                    out[at + gap : at + gap + 1, :] = ref[row : row + 1, :]
        rows = slice(96, 104) if e == 0 else slice(120, 128)
        lanes = slice(0, 64) if e == 0 else slice(192, 256)
        out[160:168, 0:64] = low[rows, lanes]
        out[160:168, 64:128] = high[rows, lanes]


def role_tiles():
    def column(sx, sy):
        return [-10.0 * sx] * 3 + [-10.0 * sy] * 3 + [float(sx * sx + sy * sy), 0.0] + [
            -0.5 * sx
        ] * 3 + [-0.5 * sy] * 3 + [0.0, 0.0]
    pairs = [((t, -1), (t, 0)) for t in (-1, 0, 1)] + [((-1, 1), (0, 1)), ((1, 1), (1, 1))]
    out = np.zeros((5, 16, 128), np.float32)
    for n, (left, right) in enumerate(pairs):
        out[n, :, :64] = np.array(column(*left))[:, None]
        out[n, :, 64:] = np.array(column(*right))[:, None]
    return out


def sum_lanes(acc0, acc1):
    row = lax.broadcasted_iota(jnp.int32, (8, 256), 0)
    total = None
    for c, acc in enumerate((acc0, acc1)):
        hi = acc.astype(bf16)
        lo = (acc - hi.astype(f32)).astype(bf16)
        ones = jnp.where(row == c, 1.0, 0.0).astype(bf16)
        term = dot_t(ones, jnp.concatenate([hi, lo], axis=1))
        total = term if total is None else total + term
    return total


def middle_kernel(
    pts, gy_low, gy_high, gx_low, gx_high, boxes, roles, feats_hbm, transfer_hbm,
    near, leaf_out, parent_out,
    feats, feats_sem, transfer, arrived, dens0, dens1, cols0, cols1, u0, u1, v0, v1, extended, windows,
):
    load = pltpu.make_async_copy(feats_hbm, feats, feats_sem)
    load.start()
    fetch = pltpu.make_async_copy(transfer_hbm, transfer, arrived)
    fetch.start()
    first = lax.broadcasted_iota(jnp.int32, (1, 128), 1) < 64
    first_cols = lax.broadcasted_iota(jnp.int32, (FEATS, 128), 1) < 64

    for t in range(NX + 2):
        if t in (0, NX + 1):
            ref = gx_low if t == 0 else gx_high
            own = jnp.concatenate([ref[128 + 8 * k : 136 + 8 * k, :] for k in range(4)], axis=1)
            low, high = ref[160:168, 0:64], ref[160:168, 64:128]
        else:
            s = t - 1
            rows = slice(96 + 8 * (s % 4), 104 + 8 * (s % 4))
            lanes = slice(64 * (s // 4), 64 * (s // 4) + 64)
            own, low, high = pts[s], gy_low[rows, lanes], gy_high[rows, lanes]
        dens0[t, :, 0:64] = low
        dens0[t, :, 64 : 64 + LANES] = own
        dens0[t, :, 64 + LANES :] = high
        dens1[t, :, 0:LANES] = own
        dens1[t, :, LANES : LANES + 64] = high
        dens1[t, :, LANES + 64 :] = jnp.zeros((8, 64), f32)

    def prepare(t, carry):
        cols0[t] = col_feats(dens0[t])
        cols1[t] = col_feats(dens1[t])
        return carry

    lax.fori_loop(0, NX + 2, prepare, 0)

    spare = jnp.zeros((FEATS, 128), bf16)

    def distances(a, half, u, u_last, mms=range(4)):
        for mm in mms:
            base = half * 512 + mm * 128
            here, after = slice(base, base + 128), slice(base + 128, base + 256)
            both = []
            for odd in range(2):
                own, other = ((cols0, cols1), (cols1, cols0))[odd]
                far = here if odd == 0 else after
                blocks = [own[a + t, :, here] for t in range(3)]
                blocks.append(jnp.where(first_cols, own[a, :, after], other[a + 1, :, far]))
                blocks = [
                    jnp.concatenate([x[:48], x[48:] * roles[n]], axis=0)
                    for n, x in enumerate(blocks)
                ]
                start = pl.multiple_of(a * LANES + base + 64 * odd, 64)
                rows = feats[pl.ds(start, 64), :]
                both.append(rows)
                at = 64 * (2 * mm + odd)
                u[at : at + 64, :] = dot(rows, jnp.concatenate(blocks, axis=1))
            last = cols0[a + 2, :, after]
            last = jnp.concatenate([last[:48], last[48:] * roles[4]], axis=0)
            split = jnp.concatenate(
                [jnp.where(first_cols, last, spare), jnp.where(first_cols, spare, last)], axis=0
            )
            u_last[64 * mm : 64 * mm + 64, :] = dot(jnp.concatenate(both, axis=1), split)

    def finish(a, half, u, u_last, mms=range(4)):
        for mm in mms:
            base = half * 512 + mm * 128
            here, after = slice(base, base + 128), slice(base + 128, base + 256)
            sums = []
            for odd in range(2):
                d_own, d_other = ((dens0, dens1), (dens1, dens0))[odd]
                far = here if odd == 0 else after
                accs = [None, None]
                at = 64 * (2 * mm + odd)
                for n in range(4):
                    k = power(u[at : at + 64, 128 * n : 128 * n + 128])
                    for c in range(2):
                        r = slice(3 + c, 4 + c)
                        if n < 3:
                            dens = d_own[a + n, r, here]
                        else:
                            dens = jnp.where(first, d_own[a, r, after], d_other[a + 1, r, far])
                        term = k * dens
                        accs[c] = term if n == 0 else accs[c] + term
                sums.append(accs)
            k = power(u_last[64 * mm : 64 * mm + 64, :])
            both = []
            for c in range(2):
                term = k * dens0[a + 2, 3 + c : 4 + c, after]
                both.append(
                    jnp.concatenate(
                        [
                            sums[0][c] + jnp.where(first, term, 0.0),
                            sums[1][c] + jnp.where(first, 0.0, term),
                        ],
                        axis=0,
                    )
                )
            total = sum_lanes(*both)
            for c in range(2):
                near[c, pl.ds(a * 8 + half * 4 + mm, 1), :] = total[c : c + 1]

    load.wait()
    distances(0, 0, u0, v0)

    def step(i, carry):
        for a in (2 * i, 2 * i + 1):
            for mm in range(4):
                finish(a, 0, u0, v0, (mm,))
                distances(a, 1, u1, v1, (mm,))
            for mm in range(4):
                finish(a, 1, u1, v1, (mm,))
                distances(jnp.minimum(a + 1, NX - 1), 0, u0, v0, (mm,))
        return carry

    lax.fori_loop(0, NX // 2, step, 0)

    blank = jnp.zeros((8, 256), f32)
    for p in range(4):
        for slot in range(16):
            n = p * 16 + slot
            own_rows = extended.at[p, slot]
            if slot in (0, 9):
                own_rows[8:24, :] = (gy_low if slot == 0 else gy_high)[16 * p : 16 * p + 16, :]
            elif slot in (10, 15):
                ref = gy_low if slot == 10 else gy_high
                own_rows[8:16, :] = ref[64 + 8 * p : 72 + 8 * p, :]
                own_rows[16:24, :] = blank
            else:
                own_rows[8:24, :] = boxes[p, slot - 1 if slot < 9 else slot - 3]
            end = 24 if slot < 10 else 16
            for c in range(2):
                row = 64 * c + n
                own_rows[6 + c : 7 + c, :] = gx_low[row : row + 1, :]
                own_rows[end + c : end + c + 1, :] = gx_high[row : row + 1, :]
            if slot >= 10:
                own_rows[24:26, :] = jnp.zeros((2, 256), f32)
            for d in range(3):
                windows[p, d, slot] = own_rows[6 + 2 * d : 22 + 2 * d, :].astype(bf16)
    fetch.wait()
    far_level(windows, transfer, leaf_out, parent_out)


def reachable(parity, shift):
    return abs((parity + shift) // 2) <= 1


def far_level(boxes, transfer, leaf_out, parent_out):
    for px in (0, 1):
        for py in (0, 1):
            total = None
            for number, (sx, sy) in enumerate(far_offsets()):
                if not (reachable(px, sx) and reachable(py, sy)):
                    continue
                dx, dy = (px + sx) // 2, (py + sy) // 2
                source = (px + sx) % 2 * 2 + (py + sy) % 2
                window = jnp.concatenate(
                    [
                        boxes[source, dx + 1, 1 + dy : 9 + dy].reshape(128, 256),
                        boxes[source, dx + 1, 11 + dy : 15 + dy].reshape(64, 256),
                    ],
                    axis=0,
                )
                term = dot(window, transfer[number])
                total = term if total is None else total + term
            p = px * 2 + py
            leaf_out[128 * p : 128 * p + 128, :] = total[:128]
            for b in range(4):
                at = 32 * p + 8 * b
                parent_out[at : at + 8, :] = total[128 + 16 * b : 136 + 16 * b]


def downward_kernel(
    gathered, lattice, pair_down, down_child, perm8, perm4, far_leaf, far_parent,
    equiv_pts, near, solution, source, counts, feats_hbm, out,
    local, pot, u0, u1, hi, lo, feats, feats_sem,
):
    load = pltpu.make_async_copy(feats_hbm, feats, feats_sem)
    load.start()
    split_into(lattice, hi, lo, 0)
    split_into(pair_down, hi, lo, 1)
    split_into(down_child, hi, lo, 3)
    vec = jnp.sum(gathered[...], axis=0)
    vec = dot3(jnp.concatenate([vec] * 4, axis=0), hi[0], lo[0])
    for axis, bits in ((0, 3), (1, 4)):
        place = lax.axis_index(AXES[axis])
        for bit in reversed(range(bits)):
            n = 1 + lax.rem(lax.div(place, 2**bit), 2)
            vec = dot3(vec, hi[n], lo[n])
    child = lambda x, p: dot3(x, hi[3 + p], lo[3 + p])
    great = jnp.concatenate([child(vec, 2 * a + b)[:2] for b in range(2) for a in range(2)], axis=0)
    spread = lambda x: jnp.concatenate([child(x, p) for p in range(4)], axis=0)
    grand = permute(perm4[...], spread(great))
    parent = spread(grand) + far_parent[...]
    parent = permute(perm8[...], parent)
    local[...] = spread(parent) + far_leaf[...]
    equiv_cols = col_feats(pad_points(equiv_pts), 0.0)

    first = lax.broadcasted_iota(jnp.int32, (2, 128), 1) < 64
    is_top = jnp.where(lax.broadcasted_iota(jnp.int32, (8, 128), 0) < 4, 1.0, 0.0)

    def distances(a, m, u):
        rows = feats[pl.ds(pl.multiple_of(a * LANES + 128 * m, 128), 128), :]
        at = 128 * (m % 4)
        u[at : at + 128, :] = dot(rows, equiv_cols)

    def finish(a, m, u):
        at = 128 * (m % 4)
        k_hi, k_lo = two_parts(power(u[at : at + 128, :]))
        row = lax.rem(a, 2) * 256 + m * 16 + lax.div(a, 2) * 2
        weight = jnp.concatenate(
            [local[pl.ds(row + 128 * half + c, 1), :] for half in range(2) for c in range(2)], axis=0
        )
        top = weight.astype(bf16).astype(f32)
        both = jnp.concatenate([top, weight - top], axis=0).astype(bf16)
        sums = dot_t(both, k_hi) + dot_t(jnp.concatenate([top, top], axis=0).astype(bf16), k_lo) * is_top
        sums = sums[:4] + sums[4:]
        total = jnp.where(first, sums[:2], sums[2:])
        for c in range(2):
            pot[c, pl.ds(a * 8 + m, 1), :] = total[c : c + 1]

    load.wait()
    for m in range(4):
        distances(0, m, u0)

    def step(i, carry):
        for a in (2 * i, 2 * i + 1):
            for m in range(4):
                distances(a, m + 4, u1)
                finish(a, m, u0)
            for m in range(4, 8):
                distances(jnp.minimum(a + 1, NX - 1), m - 4, u0)
                finish(a, m, u1)
        return carry

    lax.fori_loop(0, NX // 2, step, 0)
    for a in range(NX):
        rows = slice(8 * a, 8 * a + 8)
        total = [pot[c, rows, :] + near[c, rows, :] for c in range(2)]
        value = pairs(source, a) - scale_frac * (pairs(solution, a) * total[0] - total[1])
        value = jnp.where(live_pairs(counts, a), value, 0.0)
        out[a, pl.ds(0, NX // 2, stride=2), :] = value[:, :64]
        out[a, pl.ds(1, NX // 2, stride=2), :] = value[:, 64:]


def ring(axis, step):
    count = lax.axis_size(axis)
    return [(i, (i + step) % count) for i in range(count)]


def call(kernel, in_specs, out_shape, scratch, out_specs=None):
    return pl.pallas_call(
        kernel,
        out_shape=out_shape,
        in_specs=in_specs,
        out_specs=out_specs or jax.tree.map(lambda _: VMEM, out_shape),
        scratch_shapes=scratch,
        compiler_params=PARAMS,
    )


def shape(*dims, dtype=f32):
    return jax.ShapeDtypeStruct(dims, dtype)


def shards(
    coords, weights, solution, source, counts, check_points, equiv_points, check_solve,
    up_children, far_transfer, down_children, pair_up, lattice_map, pair_down,
):
    perm8, perm4 = box_perm(4), box_perm(2)
    halves = [pltpu.VMEM((7, 256, 256), bf16)] * 2
    feats, pts, boxes, gy_next, gy_prev, gx_edge, up = call(
        upward_kernel,
        [VMEM] * 10,
        (
            shape(NX * LANES, FEATS, dtype=bf16),
            shape(NX, 8, LANES),
            shape(4, 12, 16, 256),
            shape(128, 256),
            shape(128, 256),
            shape(2, 168, 256),
            shape(128, 2, 256),
        ),
        [pltpu.VMEM((512, 256), f32)] * 2
        + [pltpu.VMEM((LANES, 256), f32)]
        + [pltpu.VMEM((512, 256), f32)]
        + halves
        + [pltpu.VMEM((NX * LANES, FEATS), bf16), pltpu.SemaphoreType.DMA],
        out_specs=(pl.BlockSpec(memory_space=pl.ANY),) + (VMEM,) * 6,
    )(
        coords, weights, solution, counts, check_points, check_solve[None], up_children, pair_up,
        jnp.asarray(perm8, bf16), jnp.asarray(perm4, bf16),
    )
    gy_low = lax.ppermute(gy_next, "gy", ring("gy", 1))
    gy_high = lax.ppermute(gy_prev, "gy", ring("gy", -1))
    first, last = call(pack_kernel, [VMEM] * 3, (shape(168, 256), shape(168, 256)), [])(
        gy_low, gy_high, gx_edge
    )
    gx_low = lax.ppermute(last, "gx", ring("gx", 1))
    gx_high = lax.ppermute(first, "gx", ring("gx", -1))
    gathered = lax.all_to_all(up, AXES, 0, 0, tiled=True)
    near, far_leaf, far_parent = call(
        middle_kernel,
        [VMEM] * 7 + [pl.BlockSpec(memory_space=pl.ANY)] * 2,
        (shape(2, 128, 128), shape(512, 256), shape(128, 256)),
        [pltpu.VMEM((NX * LANES, FEATS), bf16), pltpu.SemaphoreType.DMA]
        + [pltpu.VMEM((40, 256, 256), bf16), pltpu.SemaphoreType.DMA]
        + [pltpu.VMEM((NX + 2, 8, PADDED), f32)] * 2
        + [pltpu.VMEM((NX + 2, FEATS, PADDED), bf16)] * 2
        + [pltpu.VMEM((512, 512), f32)] * 2
        + [pltpu.VMEM((256, 128), f32)] * 2
        + [pltpu.VMEM((4, 16, 32, 256), f32), pltpu.VMEM((4, 3, 16, 16, 256), bf16)],
    )(
        pts, gy_low, gy_high, gx_low, gx_high, boxes, jnp.asarray(role_tiles(), bf16), feats,
        far_transfer,
    )
    return call(
        downward_kernel,
        [VMEM] * 13 + [pl.BlockSpec(memory_space=pl.ANY)],
        shape(NX, NX, 64),
        [pltpu.VMEM((512, 256), f32), pltpu.VMEM((2, 128, 128), f32)]
        + [pltpu.VMEM((512, 256), f32)] * 2
        + halves
        + [pltpu.VMEM((NX * LANES, FEATS), bf16), pltpu.SemaphoreType.DMA],
    )(
        gathered, lattice_map[None], pair_down, down_children,
        jnp.asarray(perm8.T, bf16), jnp.asarray(perm4.T, bf16), far_leaf, far_parent,
        equiv_points, near, solution, source, counts, feats,
    )


def solution(mesh):
    box = P("gx", "gy", None)
    return jax.shard_map(
        shards,
        mesh=mesh,
        in_specs=(P(None, "gx", "gy", None), box, box, box, P("gx", "gy")) + (P(),) * 9,
        out_specs=box,
        check_vma=False,
    )
```

```python
import jax
import jax.numpy as jnp
import numpy as np
from jax import lax
from jax.experimental import pallas as pl
from jax.experimental.pallas import tpu as pltpu
from jax.sharding import PartitionSpec as P

f32 = jnp.float32
bf16 = jnp.bfloat16
scale_frac = 0.4
NX = 16
LANES = NX * 64
PADDED = LANES + 128
FEATS = 64
AXES = ("gx", "gy")
VMEM = pl.BlockSpec(memory_space=pltpu.VMEM)
PARAMS = pltpu.CompilerParams(vmem_limit_bytes=60 << 20)


def far_offsets():
    return [
        (x, y) for x in range(-3, 4) for y in range(-3, 4) if max(abs(x), abs(y)) >= 2
    ]


def dot(a, b):
    return jnp.dot(a, b, preferred_element_type=f32)


def dot_t(a, b):
    return lax.dot_general(a, b, (((1,), (1,)), ((), ())), preferred_element_type=f32)


def split3(block):
    hi = block.astype(bf16).astype(f32)
    rest = block - hi
    mid = rest.astype(bf16).astype(f32)
    return hi, mid, rest - mid


def centred(block):
    row = lax.broadcasted_iota(jnp.int32, block.shape, 0)
    moved = jnp.where(row < 3, 5.0 * block - 2.5, 0.0)
    return row, moved, jnp.sum(moved * moved, axis=0, keepdims=True)


def row_feats(block):
    row, moved, norm = centred(block)
    packed = jnp.where(
        row < 3, moved, jnp.where(row == 5, norm + 1.0, jnp.where(row == 6, 1.0, 0.0))
    )
    hi, mid, lo = split3(packed)
    role = jnp.concatenate(
        [hi[0:1], mid[0:1], lo[0:1], hi[1:2], mid[1:2], lo[1:2], hi[6:7] * 25.0, hi[7:8]], axis=0
    )
    tens = jnp.where(row < 6, 10.0, 0.0)
    return jnp.concatenate([hi, hi, hi, mid, mid, lo, role, tens], axis=0).astype(bf16)


def col_feats(block, role_scale=1.0):
    row, moved, norm = centred(block)
    packed = jnp.where(row < 3, moved * -2.0, jnp.where(row == 6, norm, 0.0))
    hi, mid, lo = split3(packed)
    main = hi + jnp.where(row == 5, 1.0, 0.0)
    ones = jnp.where(row < 7, role_scale, 0.0)
    role = jnp.concatenate(
        [hi[0:1], mid[0:1], lo[0:1], hi[1:2], mid[1:2], lo[1:2], hi[7:8], hi[7:8]], axis=0
    )
    return jnp.concatenate(
        [main, mid, lo, main, mid, main, ones, role * role_scale], axis=0
    ).astype(bf16)


def power(u):
    return jnp.exp2(jnp.log2(u) * -2.25)


def box_perm(side):
    order = []
    for e in (0, 1):
        for f in (0, 1):
            for b in range(side):
                for a in range(side):
                    for c in (0, 1):
                        order.append(((2 * b + f) * 2 * side + 2 * a + e) * 2 + c)
    out = np.zeros((len(order), len(order)), np.float32)
    out[np.arange(len(order)), order] = 1.0
    return out


def eye(n):
    return (
        lax.broadcasted_iota(jnp.int32, (n, n), 0) == lax.broadcasted_iota(jnp.int32, (n, n), 1)
    ).astype(bf16)


def split_into(source, hi, lo, first):
    def part(i, carry):
        rows = pl.ds(pl.multiple_of(i * 64, 64), 64)
        for n in range(source.shape[0]):
            w = source[n, rows, :]
            h = w.astype(bf16)
            hi[first + n, rows, :] = h
            lo[first + n, rows, :] = (w - h.astype(f32)).astype(bf16)
        return carry

    lax.fori_loop(0, 4, part, 0)


def dot3(x, hi, lo):
    n = x.shape[0]
    top = x.astype(bf16).astype(f32)
    both = jnp.concatenate([top, x - top], axis=0).astype(bf16)
    main = dot(both, hi)
    if n % 16:
        rest = dot(both, lo)
        return main[:n] + main[n:] + rest[:n]
    return main[:n] + main[n:] + dot(top.astype(bf16), lo)


def permute(perm, x):
    hi, mid, lo = split3(x)
    out = dot(perm, jnp.concatenate([hi, mid, lo], axis=1).astype(bf16))
    return out[:, :256] + out[:, 256:512] + out[:, 512:]


def gather4(blocks, hi, lo, first):
    n = blocks.shape[0] // 4
    total = None
    for p in range(4):
        term = dot3(blocks[p * n : (p + 1) * n], hi[first + p], lo[first + p])
        total = term if total is None else total + term
    return total


def pairs(ref, *index):
    even = ref[(*index, pl.ds(0, NX // 2, stride=2))]
    odd = ref[(*index, pl.ds(1, NX // 2, stride=2))]
    return jnp.concatenate([even, odd], axis=1)


def live_pairs(counts, a):
    row = counts[pl.ds(a, 1), :].astype(f32)
    box = lax.broadcasted_iota(jnp.int32, (NX // 2, NX), 1)
    pair = 2 * lax.broadcasted_iota(jnp.int32, (NX // 2, NX), 0)
    n = [jnp.sum(jnp.where(box == pair + odd, row, 0.0), axis=1, keepdims=True) for odd in (0, 1)]
    lane = lax.broadcasted_iota(jnp.int32, (NX // 2, 128), 1)
    return lax.rem(lane, 64).astype(f32) < jnp.where(lane < 64, n[0], n[1])


def two_parts(x):
    hi = x.astype(bf16)
    return hi, (x - hi.astype(f32)).astype(bf16)


def pad_points(points):
    return jnp.concatenate([points[...], jnp.zeros((5, 256), f32)], axis=0)


def upward_kernel(
    coords, weights, solution, counts, check_pts, solve, up_child, pair_up, perm8, perm4,
    feats, pts, boxes, gy_next, gy_prev, gx_edge, up_out,
    u0, u1, densities, pot, hi, lo, kept, kept_sem,
):
    check_cols = col_feats(pad_points(check_pts), 0.0)
    ident = eye(128)
    split_into(solve, hi, lo, 0)
    split_into(up_child, hi, lo, 1)
    split_into(pair_up, hi, lo, 5)

    row8 = lax.broadcasted_iota(jnp.int32, (8, 128), 0)
    lane8 = lax.broadcasted_iota(jnp.int32, (8, 128), 1)
    own_half = lax.rem(lax.div(row8, 2), 2) == lax.div(lane8, 64)

    def prepare(i, carry):
        for a in (4 * i, 4 * i + 1, 4 * i + 2, 4 * i + 3):
            weight = jnp.where(live_pairs(counts, a), pairs(weights, a), 0.0)
            parts = [pairs(coords, c, a) for c in range(3)]
            parts += [weight, weight * pairs(solution, a)]
            zero = jnp.zeros((3, 128), f32)
            for m in range(NX // 2):
                lanes = slice(128 * m, 128 * m + 128)
                block = jnp.concatenate([x[m : m + 1] for x in parts] + [zero], axis=0)
                pts[a, :, lanes] = block
                f = dot_t(ident, row_feats(block)).astype(bf16)
                kept[pl.ds(pl.multiple_of(a * LANES + 128 * m, 128), 128), :] = f
                both = [x[m : m + 1] for x in parts[3:]]
                dens = jnp.where(own_half, jnp.concatenate(both * 4, axis=0), 0.0)
                high = dens.astype(bf16).astype(f32)
                at = pl.multiple_of(a * 64 + 8 * m, 8)
                densities[pl.ds(at, 8), 0:128] = jnp.where(row8 < 4, high, dens - high)
                densities[pl.ds(at, 8), 128:256] = jnp.where(row8 < 4, high, 0.0)
        return carry

    lax.fori_loop(0, NX // 4, prepare, 0)
    keep = pltpu.make_async_copy(kept, feats, kept_sem)
    keep.start()

    def distances(a, m, u):
        rows = kept[pl.ds(pl.multiple_of(a * LANES + 128 * m, 128), 128), :]
        at = 128 * (m % 4)
        u[at : at + 128, :] = dot(rows, check_cols)

    def finish(a, m, u):
        at = 128 * (m % 4)
        k_hi, k_lo = two_parts(power(u[at : at + 128, :]))
        dens = densities[pl.ds(pl.multiple_of(a * 64 + 8 * m, 8), 8), :].astype(bf16)
        sums = dot(dens, jnp.concatenate([k_hi, k_lo], axis=0))
        sums = sums[:4] + sums[4:]
        row = lax.rem(a, 2) * 256 + m * 16 + lax.div(a, 2) * 2
        for half in range(2):
            for c in range(2):
                n = 2 * half + c
                pot[pl.ds(row + 128 * half + c, 1), :] = sums[n : n + 1]

    for m in range(4):
        distances(0, m, u0)

    def step(i, carry):
        for a in (2 * i, 2 * i + 1):
            for m in range(4):
                distances(a, m + 4, u1)
                finish(a, m, u0)
            for m in range(4, 8):
                distances(jnp.minimum(a + 1, NX - 1), m - 4, u0)
                finish(a, m, u1)
        return carry

    lax.fori_loop(0, NX // 2, step, 0)
    leaf = dot3(pot[...], hi[0], lo[0])
    parent = permute(perm8[...], gather4(leaf, hi, lo, 1))
    leaf_r = leaf.astype(bf16).astype(f32)
    parent_r = parent.astype(bf16).astype(f32)
    for p in range(4):
        own = leaf_r[128 * p : 128 * p + 128]
        coarse = parent_r[32 * p : 32 * p + 32]
        for b in range(8):
            boxes[p, b] = own[16 * b : 16 * b + 16]
        for b in range(4):
            boxes[p, 8 + b, 0:8] = coarse[8 * b : 8 * b + 8]
            boxes[p, 8 + b, 8:16] = jnp.zeros((8, 256), f32)
        for msg, b, bb in ((gy_next, 7, 3), (gy_prev, 0, 0)):
            msg[16 * p : 16 * p + 16, :] = own[16 * b : 16 * b + 16]
            msg[64 + 8 * p : 72 + 8 * p, :] = coarse[8 * bb : 8 * bb + 8]
        for e in range(2):
            for c in range(2):
                at = 64 * c + 16 * p
                for b in range(8):
                    row = 16 * b + 14 * e + c
                    gx_edge[e, at + 1 + b : at + 2 + b, :] = own[row : row + 1]
                for b in range(4):
                    row = 8 * b + 6 * e + c
                    gx_edge[e, at + 11 + b : at + 12 + b, :] = coarse[row : row + 1]
                for gap in (0, 9, 10, 15):
                    gx_edge[e, at + gap : at + gap + 1, :] = jnp.zeros((1, 256), f32)
    for msg, start in ((gy_next, LANES - 64), (gy_prev, 0)):
        for k in range(4):
            piece = pts[4 * k : 4 * k + 4, :, start : start + 64].reshape(32, 64)
            msg[96:128, 64 * k : 64 * k + 64] = piece
    for e, t in ((0, 0), (1, NX - 1)):
        for k in range(4):
            gx_edge[e, 128 + 8 * k : 136 + 8 * k, :] = pts[t, :, 256 * k : 256 * k + 256]
        gx_edge[e, 160:168, :] = jnp.zeros((8, 256), f32)
    grand = permute(perm4[...], gather4(parent, hi, lo, 1))
    great = gather4(grand, hi, lo, 1)
    vec = None
    for b in range(2):
        for a in range(2):
            at = (b * 2 + a) * 2
            rows = jnp.concatenate([great[at : at + 2]] * 4, axis=0)
            term = dot3(rows, hi[1 + 2 * a + b], lo[1 + 2 * a + b])
            vec = term if vec is None else vec + term
    for axis, bits in ((1, 4), (0, 3)):
        place = lax.axis_index(AXES[axis])
        for bit in range(bits):
            n = 5 + lax.rem(lax.div(place, 2**bit), 2)
            vec = dot3(vec, hi[n], lo[n])
    up_out[...] = jnp.broadcast_to(vec[None, :2], (128, 2, 256))
    keep.wait()


def pack_kernel(low, high, edge, first, last):
    for e, out in enumerate((first, last)):
        out[...] = edge[e]
        for p in range(4):
            for c in range(2):
                at = 64 * c + 16 * p
                fine = 16 * p + 14 * e + c
                coarse = 64 + 8 * p + 6 * e + c
                for gap, ref, row in (
                    (0, low, fine), (9, high, fine), (10, low, coarse), (15, high, coarse)
                ):
                    out[at + gap : at + gap + 1, :] = ref[row : row + 1, :]
        rows = slice(96, 104) if e == 0 else slice(120, 128)
        lanes = slice(0, 64) if e == 0 else slice(192, 256)
        out[160:168, 0:64] = low[rows, lanes]
        out[160:168, 64:128] = high[rows, lanes]


def role_tiles():
    def column(sx, sy):
        return [-10.0 * sx] * 3 + [-10.0 * sy] * 3 + [float(sx * sx + sy * sy), 0.0] + [
            -0.5 * sx
        ] * 3 + [-0.5 * sy] * 3 + [0.0, 0.0]
    pairs = [((t, -1), (t, 0)) for t in (-1, 0, 1)] + [((-1, 1), (0, 1)), ((1, 1), (1, 1))]
    out = np.zeros((5, 16, 128), np.float32)
    for n, (left, right) in enumerate(pairs):
        out[n, :, :64] = np.array(column(*left))[:, None]
        out[n, :, 64:] = np.array(column(*right))[:, None]
    return out


def sum_lanes(acc0, acc1):
    row = lax.broadcasted_iota(jnp.int32, (8, 256), 0)
    total = None
    for c, acc in enumerate((acc0, acc1)):
        hi = acc.astype(bf16)
        lo = (acc - hi.astype(f32)).astype(bf16)
        ones = jnp.where(row == c, 1.0, 0.0).astype(bf16)
        term = dot_t(ones, jnp.concatenate([hi, lo], axis=1))
        total = term if total is None else total + term
    return total


def near_strips(
    strips, pts, gy_low, gy_high, gx_low, gx_high, roles, near, feats, dens0, dens1,
    cols0, cols1,
):
    first = lax.broadcasted_iota(jnp.int32, (1, 128), 1) < 64
    first_cols = lax.broadcasted_iota(jnp.int32, (FEATS, 128), 1) < 64

    for t in strips:
        if t in (0, NX + 1):
            ref = gx_low if t == 0 else gx_high
            own = jnp.concatenate([ref[128 + 8 * k : 136 + 8 * k, :] for k in range(4)], axis=1)
            low, high = ref[160:168, 0:64], ref[160:168, 64:128]
        else:
            s = t - 1
            rows = slice(96 + 8 * (s % 4), 104 + 8 * (s % 4))
            lanes = slice(64 * (s // 4), 64 * (s // 4) + 64)
            own, low, high = pts[s], gy_low[rows, lanes], gy_high[rows, lanes]
        dens0[t, :, 0:64] = low
        dens0[t, :, 64 : 64 + LANES] = own
        dens0[t, :, 64 + LANES :] = high
        dens1[t, :, 0:LANES] = own
        dens1[t, :, LANES : LANES + 64] = high
        dens1[t, :, LANES + 64 :] = jnp.zeros((8, 64), f32)

    def prepare(i, carry):
        t = strips[0] + i
        if len(strips) < NX:
            t = jnp.where(i < 3, i, i + NX - 4)
        cols0[t] = col_feats(dens0[t])
        cols1[t] = col_feats(dens1[t])
        return carry

    lax.fori_loop(0, len(strips), prepare, 0)

    spare = jnp.zeros((FEATS, 128), bf16)

    def distances(a, half, u, u_last, mms=range(4)):
        for mm in mms:
            base = half * 512 + mm * 128
            here, after = slice(base, base + 128), slice(base + 128, base + 256)
            both = []
            for odd in range(2):
                own, other = ((cols0, cols1), (cols1, cols0))[odd]
                far = here if odd == 0 else after
                blocks = [own[a + t, :, here] for t in range(3)]
                blocks.append(jnp.where(first_cols, own[a, :, after], other[a + 1, :, far]))
                blocks = [
                    jnp.concatenate([x[:48], x[48:] * roles[n]], axis=0)
                    for n, x in enumerate(blocks)
                ]
                start = pl.multiple_of(a * LANES + base + 64 * odd, 64)
                rows = feats[pl.ds(start, 64), :]
                both.append(rows)
                at = 64 * (2 * mm + odd)
                u[at : at + 64, :] = dot(rows, jnp.concatenate(blocks, axis=1))
            last = cols0[a + 2, :, after]
            last = jnp.concatenate([last[:48], last[48:] * roles[4]], axis=0)
            split = jnp.concatenate(
                [jnp.where(first_cols, last, spare), jnp.where(first_cols, spare, last)], axis=0
            )
            u_last[64 * mm : 64 * mm + 64, :] = dot(jnp.concatenate(both, axis=1), split)

    def finish(a, half, u, u_last, mms=range(4)):
        for mm in mms:
            base = half * 512 + mm * 128
            here, after = slice(base, base + 128), slice(base + 128, base + 256)
            sums = []
            for odd in range(2):
                d_own, d_other = ((dens0, dens1), (dens1, dens0))[odd]
                far = here if odd == 0 else after
                dens = []
                for c in range(2):
                    r = slice(3 + c, 4 + c)
                    dens.append([d_own[a + n, r, here] for n in range(3)])
                    dens[c].append(jnp.where(first, d_own[a, r, after], d_other[a + 1, r, far]))
                parts = [[], []]
                for chunk in range(4):
                    at = 64 * (2 * mm + odd) + 16 * chunk
                    k = [power(u[at : at + 16, 128 * n : 128 * n + 128]) for n in range(4)]
                    for c in range(2):
                        parts[c].append(
                            (k[0] * dens[c][0] + k[1] * dens[c][1])
                            + (k[2] * dens[c][2] + k[3] * dens[c][3])
                        )
                sums.append([jnp.concatenate(p, axis=0) for p in parts])
            k = power(u_last[64 * mm : 64 * mm + 64, :])
            both = []
            for c in range(2):
                term = k * dens0[a + 2, 3 + c : 4 + c, after]
                both.append(
                    jnp.concatenate(
                        [
                            sums[0][c] + jnp.where(first, term, 0.0),
                            sums[1][c] + jnp.where(first, 0.0, term),
                        ],
                        axis=0,
                    )
                )
            total = sum_lanes(*both)
            for c in range(2):
                near[c, pl.ds(a * 8 + half * 4 + mm, 1), :] = total[c : c + 1]

    return distances, finish


def inner_kernel(
    pts, gy_low, gy_high, roles, feats_hbm, near,
    feats, feats_sem, dens0, dens1, cols0, cols1, u0, u1, v0, v1,
):
    load = pltpu.make_async_copy(feats_hbm, feats, feats_sem)
    load.start()
    distances, finish = near_strips(
        range(1, NX + 1), pts, gy_low, gy_high, None, None, roles, near, feats, dens0, dens1,
        cols0, cols1,
    )
    load.wait()
    distances(jnp.int32(1), 0, u0, v0)

    def step(i, carry):
        for a in (2 * i + 1, 2 * i + 2):
            for mm in range(4):
                finish(a, 0, u0, v0, (mm,))
                distances(a, 1, u1, v1, (mm,))
            for mm in range(4):
                finish(a, 1, u1, v1, (mm,))
                distances(jnp.minimum(a + 1, NX - 2), 0, u0, v0, (mm,))
        return carry

    lax.fori_loop(0, NX // 2 - 1, step, 0)


def middle_kernel(
    pts, gy_low, gy_high, gx_low, gx_high, boxes, roles, feats_hbm, transfer_hbm,
    near, leaf_out, parent_out,
    feats, feats_sem, transfer, arrived, dens0, dens1, cols0, cols1, u0, u1, v0, v1,
    extended, windows,
):
    loads = [
        pltpu.make_async_copy(
            feats_hbm.at[pl.ds(a * LANES, LANES)], feats.at[pl.ds(a * LANES, LANES)],
            feats_sem.at[n],
        )
        for n, a in enumerate((0, NX - 1))
    ]
    for load in loads:
        load.start()
    fetch = pltpu.make_async_copy(transfer_hbm, transfer, arrived)
    fetch.start()
    distances, finish = near_strips(
        (0, 1, 2, NX - 1, NX, NX + 1), pts, gy_low, gy_high, gx_low, gx_high, roles, near,
        feats, dens0, dens1, cols0, cols1,
    )
    for load in loads:
        load.wait()
    low_strip, high_strip = jnp.int32(0), jnp.int32(NX - 1)
    distances(low_strip, 0, u0, v0)
    for mm in range(4):
        finish(low_strip, 0, u0, v0, (mm,))
        distances(low_strip, 1, u1, v1, (mm,))
    for mm in range(4):
        finish(low_strip, 1, u1, v1, (mm,))
        distances(high_strip, 0, u0, v0, (mm,))
    for mm in range(4):
        finish(high_strip, 0, u0, v0, (mm,))
        distances(high_strip, 1, u1, v1, (mm,))
    finish(high_strip, 1, u1, v1)

    blank = jnp.zeros((8, 256), f32)
    for p in range(4):
        for slot in range(16):
            n = p * 16 + slot
            own_rows = extended.at[p, slot]
            if slot in (0, 9):
                own_rows[8:24, :] = (gy_low if slot == 0 else gy_high)[16 * p : 16 * p + 16, :]
            elif slot in (10, 15):
                ref = gy_low if slot == 10 else gy_high
                own_rows[8:16, :] = ref[64 + 8 * p : 72 + 8 * p, :]
                own_rows[16:24, :] = blank
            else:
                own_rows[8:24, :] = boxes[p, slot - 1 if slot < 9 else slot - 3]
            end = 24 if slot < 10 else 16
            for c in range(2):
                row = 64 * c + n
                own_rows[6 + c : 7 + c, :] = gx_low[row : row + 1, :]
                own_rows[end + c : end + c + 1, :] = gx_high[row : row + 1, :]
            if slot >= 10:
                own_rows[24:26, :] = jnp.zeros((2, 256), f32)
            for d in range(3):
                windows[p, d, slot] = own_rows[6 + 2 * d : 22 + 2 * d, :].astype(bf16)
    fetch.wait()
    far_level(windows, transfer, leaf_out, parent_out)


def reachable(parity, shift):
    return abs((parity + shift) // 2) <= 1


def far_level(boxes, transfer, leaf_out, parent_out):
    for px in (0, 1):
        for py in (0, 1):
            total = None
            for number, (sx, sy) in enumerate(far_offsets()):
                if not (reachable(px, sx) and reachable(py, sy)):
                    continue
                dx, dy = (px + sx) // 2, (py + sy) // 2
                source = (px + sx) % 2 * 2 + (py + sy) % 2
                window = jnp.concatenate(
                    [
                        boxes[source, dx + 1, 1 + dy : 9 + dy].reshape(128, 256),
                        boxes[source, dx + 1, 11 + dy : 15 + dy].reshape(64, 256),
                    ],
                    axis=0,
                )
                term = dot(window, transfer[number])
                total = term if total is None else total + term
            p = px * 2 + py
            leaf_out[128 * p : 128 * p + 128, :] = total[:128]
            for b in range(4):
                at = 32 * p + 8 * b
                parent_out[at : at + 8, :] = total[128 + 16 * b : 136 + 16 * b]


def downward_kernel(
    gathered, lattice, pair_down, down_child, perm8, perm4, far_leaf, far_parent,
    equiv_pts, inner, near, solution, source, counts, feats_hbm, out,
    local, pot, u0, u1, hi, lo, feats, feats_sem,
):
    load = pltpu.make_async_copy(feats_hbm, feats, feats_sem)
    load.start()
    split_into(lattice, hi, lo, 0)
    split_into(pair_down, hi, lo, 1)
    split_into(down_child, hi, lo, 3)
    vec = jnp.sum(gathered[...], axis=0)
    vec = dot3(jnp.concatenate([vec] * 4, axis=0), hi[0], lo[0])
    for axis, bits in ((0, 3), (1, 4)):
        place = lax.axis_index(AXES[axis])
        for bit in reversed(range(bits)):
            n = 1 + lax.rem(lax.div(place, 2**bit), 2)
            vec = dot3(vec, hi[n], lo[n])
    child = lambda x, p: dot3(x, hi[3 + p], lo[3 + p])
    great = jnp.concatenate([child(vec, 2 * a + b)[:2] for b in range(2) for a in range(2)], axis=0)
    spread = lambda x: jnp.concatenate([child(x, p) for p in range(4)], axis=0)
    grand = permute(perm4[...], spread(great))
    parent = spread(grand) + far_parent[...]
    parent = permute(perm8[...], parent)
    local[...] = spread(parent) + far_leaf[...]
    equiv_cols = col_feats(pad_points(equiv_pts), 0.0)

    first = lax.broadcasted_iota(jnp.int32, (2, 128), 1) < 64
    is_top = jnp.where(lax.broadcasted_iota(jnp.int32, (8, 128), 0) < 4, 1.0, 0.0)

    def distances(a, m, u):
        rows = feats[pl.ds(pl.multiple_of(a * LANES + 128 * m, 128), 128), :]
        at = 128 * (m % 4)
        u[at : at + 128, :] = dot(rows, equiv_cols)

    def finish(a, m, u):
        at = 128 * (m % 4)
        k_hi, k_lo = two_parts(power(u[at : at + 128, :]))
        row = lax.rem(a, 2) * 256 + m * 16 + lax.div(a, 2) * 2
        weight = jnp.concatenate(
            [local[pl.ds(row + 128 * half + c, 1), :] for half in range(2) for c in range(2)], axis=0
        )
        top = weight.astype(bf16).astype(f32)
        both = jnp.concatenate([top, weight - top], axis=0).astype(bf16)
        sums = dot_t(both, k_hi) + dot_t(jnp.concatenate([top, top], axis=0).astype(bf16), k_lo) * is_top
        sums = sums[:4] + sums[4:]
        total = jnp.where(first, sums[:2], sums[2:])
        for c in range(2):
            pot[c, pl.ds(a * 8 + m, 1), :] = total[c : c + 1]

    load.wait()
    for m in range(4):
        distances(0, m, u0)

    def step(i, carry):
        for a in (2 * i, 2 * i + 1):
            for m in range(4):
                distances(a, m + 4, u1)
                finish(a, m, u0)
            for m in range(4, 8):
                distances(jnp.minimum(a + 1, NX - 1), m - 4, u0)
                finish(a, m, u1)
        return carry

    lax.fori_loop(0, NX // 2, step, 0)
    for a in range(NX):
        rows = slice(8 * a, 8 * a + 8)
        close = near if a in (0, NX - 1) else inner
        total = [pot[c, rows, :] + close[c, rows, :] for c in range(2)]
        value = pairs(source, a) - scale_frac * (pairs(solution, a) * total[0] - total[1])
        value = jnp.where(live_pairs(counts, a), value, 0.0)
        out[a, pl.ds(0, NX // 2, stride=2), :] = value[:, :64]
        out[a, pl.ds(1, NX // 2, stride=2), :] = value[:, 64:]


def ring(axis, step):
    count = lax.axis_size(axis)
    return [(i, (i + step) % count) for i in range(count)]


def call(kernel, in_specs, out_shape, scratch, out_specs=None, cost=None):
    return pl.pallas_call(
        kernel,
        out_shape=out_shape,
        in_specs=in_specs,
        out_specs=out_specs or jax.tree.map(lambda _: VMEM, out_shape),
        scratch_shapes=scratch,
        compiler_params=PARAMS,
        cost_estimate=cost,
    )


def shape(*dims, dtype=f32):
    return jax.ShapeDtypeStruct(dims, dtype)


def shards(
    coords, weights, solution, source, counts, check_points, equiv_points, check_solve,
    up_children, far_transfer, down_children, pair_up, lattice_map, pair_down,
):
    perm8, perm4 = box_perm(4), box_perm(2)
    halves = [pltpu.VMEM((7, 256, 256), bf16)] * 2
    feats, pts, boxes, gy_next, gy_prev, gx_edge, up = call(
        upward_kernel,
        [VMEM] * 10,
        (
            shape(NX * LANES, FEATS, dtype=bf16),
            shape(NX, 8, LANES),
            shape(4, 12, 16, 256),
            shape(128, 256),
            shape(128, 256),
            shape(2, 168, 256),
            shape(128, 2, 256),
        ),
        [pltpu.VMEM((512, 256), f32)] * 2
        + [pltpu.VMEM((LANES, 256), f32)]
        + [pltpu.VMEM((512, 256), f32)]
        + halves
        + [pltpu.VMEM((NX * LANES, FEATS), bf16), pltpu.SemaphoreType.DMA],
        out_specs=(pl.BlockSpec(memory_space=pl.ANY),) + (VMEM,) * 6,
    )(
        coords, weights, solution, counts, check_points, check_solve[None], up_children, pair_up,
        jnp.asarray(perm8, bf16), jnp.asarray(perm4, bf16),
    )
    gy_low = lax.ppermute(gy_next, "gy", ring("gy", 1))
    gy_high = lax.ppermute(gy_prev, "gy", ring("gy", -1))
    first, last = call(pack_kernel, [VMEM] * 3, (shape(168, 256), shape(168, 256)), [])(
        gy_low, gy_high, gx_edge
    )
    gx_low = lax.ppermute(last, "gx", ring("gx", 1))
    gx_high = lax.ppermute(first, "gx", ring("gx", -1))
    gathered = lax.all_to_all(up, AXES, 0, 0, tiled=True)
    roles = jnp.asarray(role_tiles(), bf16)
    near_scratch = (
        [pltpu.VMEM((NX + 2, 8, PADDED), f32)] * 2
        + [pltpu.VMEM((NX + 2, FEATS, PADDED), bf16)] * 2
        + [pltpu.VMEM((512, 512), f32)] * 2
        + [pltpu.VMEM((256, 128), f32)] * 2
    )
    gy_low_in, gy_high_in, _ = lax.optimization_barrier((gy_low, gy_high, first))
    inner = call(
        inner_kernel,
        [VMEM] * 4 + [pl.BlockSpec(memory_space=pl.ANY)],
        shape(2, 128, 128),
        [pltpu.VMEM((NX * LANES, FEATS), bf16), pltpu.SemaphoreType.DMA] + near_scratch,
        cost=pl.CostEstimate(flops=4 * 10**10, bytes_accessed=10**7, transcendentals=2 * 10**7),
    )(pts, gy_low_in, gy_high_in, roles, feats)
    near, far_leaf, far_parent = call(
        middle_kernel,
        [VMEM] * 7 + [pl.BlockSpec(memory_space=pl.ANY)] * 2,
        (shape(2, 128, 128), shape(512, 256), shape(128, 256)),
        [pltpu.VMEM((NX * LANES, FEATS), bf16), pltpu.SemaphoreType.DMA((2,))]
        + [pltpu.VMEM((40, 256, 256), bf16), pltpu.SemaphoreType.DMA]
        + near_scratch
        + [pltpu.VMEM((4, 16, 32, 256), f32), pltpu.VMEM((4, 3, 16, 16, 256), bf16)],
    )(
        pts, gy_low, gy_high, gx_low, gx_high, boxes, roles, feats,
        far_transfer,
    )
    return call(
        downward_kernel,
        [VMEM] * 14 + [pl.BlockSpec(memory_space=pl.ANY)],
        shape(NX, NX, 64),
        [pltpu.VMEM((512, 256), f32), pltpu.VMEM((2, 128, 128), f32)]
        + [pltpu.VMEM((512, 256), f32)] * 2
        + halves
        + [pltpu.VMEM((NX * LANES, FEATS), bf16), pltpu.SemaphoreType.DMA],
    )(
        gathered, lattice_map[None], pair_down, down_children,
        jnp.asarray(perm8.T, bf16), jnp.asarray(perm4.T, bf16), far_leaf, far_parent,
        equiv_points, inner, near, solution, source, counts, feats,
    )


def solution(mesh):
    box = P("gx", "gy", None)
    return jax.shard_map(
        shards,
        mesh=mesh,
        in_specs=(P(None, "gx", "gy", None), box, box, box, P("gx", "gy")) + (P(),) * 9,
        out_specs=box,
        check_vma=False,
    )
```

```python
import jax
import jax.numpy as jnp
import numpy as np
from jax import lax
from jax.experimental import pallas as pl
from jax.experimental.pallas import tpu as pltpu
from jax.sharding import PartitionSpec as P

f32 = jnp.float32
bf16 = jnp.bfloat16
scale_frac = 0.4
NX = 16
LANES = NX * 64
PADDED = LANES + 128
FEATS = 64
AXES = ("gx", "gy")
VMEM = pl.BlockSpec(memory_space=pltpu.VMEM)
PARAMS = pltpu.CompilerParams(vmem_limit_bytes=60 << 20)


def far_offsets():
    return [
        (x, y) for x in range(-3, 4) for y in range(-3, 4) if max(abs(x), abs(y)) >= 2
    ]


def dot(a, b):
    return jnp.dot(a, b, preferred_element_type=f32)


def dot_t(a, b):
    return lax.dot_general(a, b, (((1,), (1,)), ((), ())), preferred_element_type=f32)


def split3(block):
    hi = block.astype(bf16).astype(f32)
    rest = block - hi
    mid = rest.astype(bf16).astype(f32)
    return hi, mid, rest - mid


def centred(block):
    row = lax.broadcasted_iota(jnp.int32, block.shape, 0)
    moved = jnp.where(row < 3, 5.0 * block - 2.5, 0.0)
    return row, moved, jnp.sum(moved * moved, axis=0, keepdims=True)


def row_feats(block):
    row, moved, norm = centred(block)
    packed = jnp.where(
        row < 3, moved, jnp.where(row == 5, norm + 1.0, jnp.where(row == 6, 1.0, 0.0))
    )
    hi, mid, lo = split3(packed)
    role = jnp.concatenate(
        [hi[0:1], mid[0:1], lo[0:1], hi[1:2], mid[1:2], lo[1:2], hi[6:7] * 25.0, hi[7:8]], axis=0
    )
    tens = jnp.where(row < 6, 10.0, 0.0)
    return jnp.concatenate([hi, hi, hi, mid, mid, lo, role, tens], axis=0).astype(bf16)


def col_feats(block, role_scale=1.0):
    row, moved, norm = centred(block)
    packed = jnp.where(row < 3, moved * -2.0, jnp.where(row == 6, norm, 0.0))
    hi, mid, lo = split3(packed)
    main = hi + jnp.where(row == 5, 1.0, 0.0)
    ones = jnp.where(row < 7, role_scale, 0.0)
    role = jnp.concatenate(
        [hi[0:1], mid[0:1], lo[0:1], hi[1:2], mid[1:2], lo[1:2], hi[7:8], hi[7:8]], axis=0
    )
    return jnp.concatenate(
        [main, mid, lo, main, mid, main, ones, role * role_scale], axis=0
    ).astype(bf16)


def power(u):
    return jnp.exp2(jnp.log2(u) * -2.25)


def box_perm(side):
    order = []
    for e in (0, 1):
        for f in (0, 1):
            for b in range(side):
                for a in range(side):
                    for c in (0, 1):
                        order.append(((2 * b + f) * 2 * side + 2 * a + e) * 2 + c)
    out = np.zeros((len(order), len(order)), np.float32)
    out[np.arange(len(order)), order] = 1.0
    return out


def eye(n):
    return (
        lax.broadcasted_iota(jnp.int32, (n, n), 0) == lax.broadcasted_iota(jnp.int32, (n, n), 1)
    ).astype(bf16)


def split_into(source, hi, lo, first):
    def part(i, carry):
        rows = pl.ds(pl.multiple_of(i * 64, 64), 64)
        for n in range(source.shape[0]):
            w = source[n, rows, :]
            h = w.astype(bf16)
            hi[first + n, rows, :] = h
            lo[first + n, rows, :] = (w - h.astype(f32)).astype(bf16)
        return carry

    lax.fori_loop(0, 4, part, 0)


def dot3(x, hi, lo):
    n = x.shape[0]
    top = x.astype(bf16).astype(f32)
    both = jnp.concatenate([top, x - top], axis=0).astype(bf16)
    main = dot(both, hi)
    if n % 16:
        rest = dot(both, lo)
        return main[:n] + main[n:] + rest[:n]
    return main[:n] + main[n:] + dot(top.astype(bf16), lo)


def permute(perm, x):
    hi, mid, lo = split3(x)
    out = dot(perm, jnp.concatenate([hi, mid, lo], axis=1).astype(bf16))
    return out[:, :256] + out[:, 256:512] + out[:, 512:]


def gather4(blocks, hi, lo, first):
    n = blocks.shape[0] // 4
    total = None
    for p in range(4):
        term = dot3(blocks[p * n : (p + 1) * n], hi[first + p], lo[first + p])
        total = term if total is None else total + term
    return total


def pairs(ref, *index):
    even = ref[(*index, pl.ds(0, NX // 2, stride=2))]
    odd = ref[(*index, pl.ds(1, NX // 2, stride=2))]
    return jnp.concatenate([even, odd], axis=1)


def live_pairs(counts, a):
    row = counts[pl.ds(a, 1), :].astype(f32)
    box = lax.broadcasted_iota(jnp.int32, (NX // 2, NX), 1)
    pair = 2 * lax.broadcasted_iota(jnp.int32, (NX // 2, NX), 0)
    n = [jnp.sum(jnp.where(box == pair + odd, row, 0.0), axis=1, keepdims=True) for odd in (0, 1)]
    lane = lax.broadcasted_iota(jnp.int32, (NX // 2, 128), 1)
    return lax.rem(lane, 64).astype(f32) < jnp.where(lane < 64, n[0], n[1])


def two_parts(x):
    hi = x.astype(bf16)
    return hi, (x - hi.astype(f32)).astype(bf16)


def pad_points(points):
    return jnp.concatenate([points[...], jnp.zeros((5, 256), f32)], axis=0)


def upward_kernel(
    coords, weights, solution, counts, check_pts, perm8, perm4, solve, up_child, pair_up,
    feats, pts_out, boxes, gy_next, gy_prev, gx_edge, up_out,
    u0, u1, densities, pot, hi, lo, kept, kept_sem, pts, pts_sem, matrices, matrix_sem,
):
    check_cols = col_feats(pad_points(check_pts), 0.0)
    ident = eye(128)
    loads = [
        pltpu.make_async_copy(source, matrices.at[pl.ds(at, count)], matrix_sem.at[n])
        for n, (source, at, count) in enumerate(((solve, 0, 1), (up_child, 1, 4), (pair_up, 5, 2)))
    ]
    for load in loads:
        load.start()

    row8 = lax.broadcasted_iota(jnp.int32, (8, 128), 0)
    lane8 = lax.broadcasted_iota(jnp.int32, (8, 128), 1)
    own_half = lax.rem(lax.div(row8, 2), 2) == lax.div(lane8, 64)

    def prepare(i, carry):
        for a in (4 * i, 4 * i + 1, 4 * i + 2, 4 * i + 3):
            weight = jnp.where(live_pairs(counts, a), pairs(weights, a), 0.0)
            parts = [pairs(coords, c, a) for c in range(3)]
            parts += [weight, weight * pairs(solution, a)]
            zero = jnp.zeros((3, 128), f32)
            for m in range(NX // 2):
                lanes = slice(128 * m, 128 * m + 128)
                block = jnp.concatenate([x[m : m + 1] for x in parts] + [zero], axis=0)
                pts[a, :, lanes] = block
                f = dot_t(ident, row_feats(block)).astype(bf16)
                kept[pl.ds(pl.multiple_of(a * LANES + 128 * m, 128), 128), :] = f
                both = [x[m : m + 1] for x in parts[3:]]
                dens = jnp.where(own_half, jnp.concatenate(both * 4, axis=0), 0.0)
                high = dens.astype(bf16).astype(f32)
                at = pl.multiple_of(a * 64 + 8 * m, 8)
                densities[pl.ds(at, 8), 0:128] = jnp.where(row8 < 4, high, dens - high)
                densities[pl.ds(at, 8), 128:256] = jnp.where(row8 < 4, high, 0.0)
        return carry

    lax.fori_loop(0, NX // 4, prepare, 0)
    keep = pltpu.make_async_copy(kept, feats, kept_sem)
    keep.start()
    keep_pts = pltpu.make_async_copy(pts, pts_out, pts_sem)
    keep_pts.start()
    for load in loads:
        load.wait()
    split_into(matrices, hi, lo, 0)

    def distances(a, m, u):
        rows = kept[pl.ds(pl.multiple_of(a * LANES + 128 * m, 128), 128), :]
        at = 128 * (m % 4)
        u[at : at + 128, :] = dot(rows, check_cols)

    def finish(a, m, u):
        at = 128 * (m % 4)
        k_hi, k_lo = two_parts(power(u[at : at + 128, :]))
        dens = densities[pl.ds(pl.multiple_of(a * 64 + 8 * m, 8), 8), :].astype(bf16)
        sums = dot(dens, jnp.concatenate([k_hi, k_lo], axis=0))
        sums = sums[:4] + sums[4:]
        row = lax.rem(a, 2) * 256 + m * 16 + lax.div(a, 2) * 2
        for half in range(2):
            for c in range(2):
                n = 2 * half + c
                pot[pl.ds(row + 128 * half + c, 1), :] = sums[n : n + 1]

    for m in range(4):
        distances(0, m, u0)

    def step(i, carry):
        for a in (2 * i, 2 * i + 1):
            for m in range(4):
                distances(a, m + 4, u1)
                finish(a, m, u0)
            for m in range(4, 8):
                distances(jnp.minimum(a + 1, NX - 1), m - 4, u0)
                finish(a, m, u1)
        return carry

    lax.fori_loop(0, NX // 2, step, 0)
    leaf = dot3(pot[...], hi[0], lo[0])
    parent = permute(perm8[...], gather4(leaf, hi, lo, 1))
    leaf_r = leaf.astype(bf16).astype(f32)
    parent_r = parent.astype(bf16).astype(f32)
    for p in range(4):
        own = leaf_r[128 * p : 128 * p + 128]
        coarse = parent_r[32 * p : 32 * p + 32]
        for b in range(8):
            boxes[p, b] = own[16 * b : 16 * b + 16]
        for b in range(4):
            boxes[p, 8 + b, 0:8] = coarse[8 * b : 8 * b + 8]
            boxes[p, 8 + b, 8:16] = jnp.zeros((8, 256), f32)
        for msg, b, bb in ((gy_next, 7, 3), (gy_prev, 0, 0)):
            msg[16 * p : 16 * p + 16, :] = own[16 * b : 16 * b + 16]
            msg[64 + 8 * p : 72 + 8 * p, :] = coarse[8 * bb : 8 * bb + 8]
        for e in range(2):
            for c in range(2):
                at = 64 * c + 16 * p
                for b in range(8):
                    row = 16 * b + 14 * e + c
                    gx_edge[e, at + 1 + b : at + 2 + b, :] = own[row : row + 1]
                for b in range(4):
                    row = 8 * b + 6 * e + c
                    gx_edge[e, at + 11 + b : at + 12 + b, :] = coarse[row : row + 1]
                for gap in (0, 9, 10, 15):
                    gx_edge[e, at + gap : at + gap + 1, :] = jnp.zeros((1, 256), f32)
    for msg, start in ((gy_next, LANES - 64), (gy_prev, 0)):
        for k in range(4):
            piece = pts[4 * k : 4 * k + 4, :, start : start + 64].reshape(32, 64)
            msg[96:128, 64 * k : 64 * k + 64] = piece
    for e, t in ((0, 0), (1, NX - 1)):
        for k in range(4):
            gx_edge[e, 128 + 8 * k : 136 + 8 * k, :] = pts[t, :, 256 * k : 256 * k + 256]
        gx_edge[e, 160:168, :] = jnp.zeros((8, 256), f32)
    grand = permute(perm4[...], gather4(parent, hi, lo, 1))
    great = gather4(grand, hi, lo, 1)
    vec = None
    for b in range(2):
        for a in range(2):
            at = (b * 2 + a) * 2
            rows = jnp.concatenate([great[at : at + 2]] * 4, axis=0)
            term = dot3(rows, hi[1 + 2 * a + b], lo[1 + 2 * a + b])
            vec = term if vec is None else vec + term
    for axis, bits in ((1, 4), (0, 3)):
        place = lax.axis_index(AXES[axis])
        for bit in range(bits):
            n = 5 + lax.rem(lax.div(place, 2**bit), 2)
            vec = dot3(vec, hi[n], lo[n])
    up_out[...] = jnp.broadcast_to(vec[None, :2], (128, 2, 256))
    keep.wait()
    keep_pts.wait()


def pack_kernel(low, high, edge, first, last):
    for e, out in enumerate((first, last)):
        out[...] = edge[e]
        for p in range(4):
            for c in range(2):
                at = 64 * c + 16 * p
                fine = 16 * p + 14 * e + c
                coarse = 64 + 8 * p + 6 * e + c
                for gap, ref, row in (
                    (0, low, fine), (9, high, fine), (10, low, coarse), (15, high, coarse)
                ):
                    out[at + gap : at + gap + 1, :] = ref[row : row + 1, :]
        rows = slice(96, 104) if e == 0 else slice(120, 128)
        lanes = slice(0, 64) if e == 0 else slice(192, 256)
        out[160:168, 0:64] = low[rows, lanes]
        out[160:168, 64:128] = high[rows, lanes]


def role_tiles():
    def column(sx, sy):
        return [-10.0 * sx] * 3 + [-10.0 * sy] * 3 + [float(sx * sx + sy * sy), 0.0] + [
            -0.5 * sx
        ] * 3 + [-0.5 * sy] * 3 + [0.0, 0.0]
    pairs = [((t, -1), (t, 0)) for t in (-1, 0, 1)] + [((-1, 1), (0, 1)), ((1, 1), (1, 1))]
    out = np.zeros((5, 16, 128), np.float32)
    for n, (left, right) in enumerate(pairs):
        out[n, :, :64] = np.array(column(*left))[:, None]
        out[n, :, 64:] = np.array(column(*right))[:, None]
    return out


def sum_lanes(acc0, acc1):
    row = lax.broadcasted_iota(jnp.int32, (8, 256), 0)
    total = None
    for c, acc in enumerate((acc0, acc1)):
        hi = acc.astype(bf16)
        lo = (acc - hi.astype(f32)).astype(bf16)
        ones = jnp.where(row == c, 1.0, 0.0).astype(bf16)
        term = dot_t(ones, jnp.concatenate([hi, lo], axis=1))
        total = term if total is None else total + term
    return total


def near_strips(
    strips, pts, gy_low, gy_high, gx_low, gx_high, roles, near, feats, dens0, dens1,
    cols0, cols1,
):
    first = lax.broadcasted_iota(jnp.int32, (1, 128), 1) < 64
    first_cols = lax.broadcasted_iota(jnp.int32, (FEATS, 128), 1) < 64

    for t in strips:
        if t in (0, NX + 1):
            ref = gx_low if t == 0 else gx_high
            own = jnp.concatenate([ref[128 + 8 * k : 136 + 8 * k, :] for k in range(4)], axis=1)
            low, high = ref[160:168, 0:64], ref[160:168, 64:128]
        else:
            s = t - 1
            rows = slice(96 + 8 * (s % 4), 104 + 8 * (s % 4))
            lanes = slice(64 * (s // 4), 64 * (s // 4) + 64)
            own, low, high = pts[s], gy_low[rows, lanes], gy_high[rows, lanes]
        dens0[t, :, 0:64] = low
        dens0[t, :, 64 : 64 + LANES] = own
        dens0[t, :, 64 + LANES :] = high
        dens1[t, :, 0:LANES] = own
        dens1[t, :, LANES : LANES + 64] = high
        dens1[t, :, LANES + 64 :] = jnp.zeros((8, 64), f32)

    def prepare(i, carry):
        t = strips[0] + i
        if len(strips) < NX:
            t = jnp.where(i < 3, i, i + NX - 4)
        cols0[t] = col_feats(dens0[t])
        cols1[t] = col_feats(dens1[t])
        return carry

    lax.fori_loop(0, len(strips), prepare, 0)

    spare = jnp.zeros((FEATS, 128), bf16)

    def distances(a, half, u, u_last, mms=range(4)):
        for mm in mms:
            base = half * 512 + mm * 128
            here, after = slice(base, base + 128), slice(base + 128, base + 256)
            both = []
            for odd in range(2):
                own, other = ((cols0, cols1), (cols1, cols0))[odd]
                far = here if odd == 0 else after
                blocks = [own[a + t, :, here] for t in range(3)]
                blocks.append(jnp.where(first_cols, own[a, :, after], other[a + 1, :, far]))
                blocks = [
                    jnp.concatenate([x[:48], x[48:] * roles[n]], axis=0)
                    for n, x in enumerate(blocks)
                ]
                start = pl.multiple_of(a * LANES + base + 64 * odd, 64)
                rows = feats[pl.ds(start, 64), :]
                both.append(rows)
                at = 64 * (2 * mm + odd)
                u[at : at + 64, :] = dot(rows, jnp.concatenate(blocks, axis=1))
            last = cols0[a + 2, :, after]
            last = jnp.concatenate([last[:48], last[48:] * roles[4]], axis=0)
            split = jnp.concatenate(
                [jnp.where(first_cols, last, spare), jnp.where(first_cols, spare, last)], axis=0
            )
            u_last[64 * mm : 64 * mm + 64, :] = dot(jnp.concatenate(both, axis=1), split)

    def finish(a, half, u, u_last, mms=range(4)):
        for mm in mms:
            base = half * 512 + mm * 128
            here, after = slice(base, base + 128), slice(base + 128, base + 256)
            sums = []
            for odd in range(2):
                d_own, d_other = ((dens0, dens1), (dens1, dens0))[odd]
                far = here if odd == 0 else after
                dens = []
                for c in range(2):
                    r = slice(3 + c, 4 + c)
                    dens.append([d_own[a + n, r, here] for n in range(3)])
                    dens[c].append(jnp.where(first, d_own[a, r, after], d_other[a + 1, r, far]))
                parts = [[], []]
                for chunk in range(4):
                    at = 64 * (2 * mm + odd) + 16 * chunk
                    k = [power(u[at : at + 16, 128 * n : 128 * n + 128]) for n in range(4)]
                    for c in range(2):
                        parts[c].append(
                            (k[0] * dens[c][0] + k[1] * dens[c][1])
                            + (k[2] * dens[c][2] + k[3] * dens[c][3])
                        )
                sums.append([jnp.concatenate(p, axis=0) for p in parts])
            k = power(u_last[64 * mm : 64 * mm + 64, :])
            both = []
            for c in range(2):
                term = k * dens0[a + 2, 3 + c : 4 + c, after]
                both.append(
                    jnp.concatenate(
                        [
                            sums[0][c] + jnp.where(first, term, 0.0),
                            sums[1][c] + jnp.where(first, 0.0, term),
                        ],
                        axis=0,
                    )
                )
            total = sum_lanes(*both)
            for c in range(2):
                near[c, pl.ds(a * 8 + half * 4 + mm, 1), :] = total[c : c + 1]

    return distances, finish


def inner_kernel(
    pts, gy_low, gy_high, roles, feats_hbm, near,
    feats, feats_sem, dens0, dens1, cols0, cols1, u0, u1, v0, v1,
):
    load = pltpu.make_async_copy(feats_hbm, feats, feats_sem)
    load.start()
    distances, finish = near_strips(
        range(1, NX + 1), pts, gy_low, gy_high, None, None, roles, near, feats, dens0, dens1,
        cols0, cols1,
    )
    load.wait()
    distances(jnp.int32(1), 0, u0, v0)

    def step(i, carry):
        for a in (2 * i + 1, 2 * i + 2):
            for mm in range(4):
                finish(a, 0, u0, v0, (mm,))
                distances(a, 1, u1, v1, (mm,))
            for mm in range(4):
                finish(a, 1, u1, v1, (mm,))
                distances(jnp.minimum(a + 1, NX - 2), 0, u0, v0, (mm,))
        return carry

    lax.fori_loop(0, NX // 2 - 1, step, 0)


def middle_kernel(
    pts, gy_low, gy_high, gx_low, gx_high, boxes, roles, feats_hbm, transfer_hbm,
    near, leaf_out, parent_out,
    feats, feats_sem, transfer, arrived, dens0, dens1, cols0, cols1, u0, u1, v0, v1,
    extended, windows,
):
    loads = [
        pltpu.make_async_copy(
            feats_hbm.at[pl.ds(a * LANES, LANES)], feats.at[pl.ds(a * LANES, LANES)],
            feats_sem.at[n],
        )
        for n, a in enumerate((0, NX - 1))
    ]
    for load in loads:
        load.start()
    fetch = pltpu.make_async_copy(transfer_hbm, transfer, arrived)
    fetch.start()
    distances, finish = near_strips(
        (0, 1, 2, NX - 1, NX, NX + 1), pts, gy_low, gy_high, gx_low, gx_high, roles, near,
        feats, dens0, dens1, cols0, cols1,
    )
    for load in loads:
        load.wait()
    low_strip, high_strip = jnp.int32(0), jnp.int32(NX - 1)
    distances(low_strip, 0, u0, v0)
    for mm in range(4):
        finish(low_strip, 0, u0, v0, (mm,))
        distances(low_strip, 1, u1, v1, (mm,))
    for mm in range(4):
        finish(low_strip, 1, u1, v1, (mm,))
        distances(high_strip, 0, u0, v0, (mm,))
    for mm in range(4):
        finish(high_strip, 0, u0, v0, (mm,))
        distances(high_strip, 1, u1, v1, (mm,))
    finish(high_strip, 1, u1, v1)

    blank = jnp.zeros((8, 256), f32)
    for p in range(4):
        for slot in range(16):
            n = p * 16 + slot
            own_rows = extended.at[p, slot]
            if slot in (0, 9):
                own_rows[8:24, :] = (gy_low if slot == 0 else gy_high)[16 * p : 16 * p + 16, :]
            elif slot in (10, 15):
                ref = gy_low if slot == 10 else gy_high
                own_rows[8:16, :] = ref[64 + 8 * p : 72 + 8 * p, :]
                own_rows[16:24, :] = blank
            else:
                own_rows[8:24, :] = boxes[p, slot - 1 if slot < 9 else slot - 3]
            end = 24 if slot < 10 else 16
            for c in range(2):
                row = 64 * c + n
                own_rows[6 + c : 7 + c, :] = gx_low[row : row + 1, :]
                own_rows[end + c : end + c + 1, :] = gx_high[row : row + 1, :]
            if slot >= 10:
                own_rows[24:26, :] = jnp.zeros((2, 256), f32)
            for d in range(3):
                windows[p, d, slot] = own_rows[6 + 2 * d : 22 + 2 * d, :].astype(bf16)
    fetch.wait()
    far_level(windows, transfer, leaf_out, parent_out)


def reachable(parity, shift):
    return abs((parity + shift) // 2) <= 1


def far_level(boxes, transfer, leaf_out, parent_out):
    for px in (0, 1):
        for py in (0, 1):
            total = None
            for number, (sx, sy) in enumerate(far_offsets()):
                if not (reachable(px, sx) and reachable(py, sy)):
                    continue
                dx, dy = (px + sx) // 2, (py + sy) // 2
                source = (px + sx) % 2 * 2 + (py + sy) % 2
                window = jnp.concatenate(
                    [
                        boxes[source, dx + 1, 1 + dy : 9 + dy].reshape(128, 256),
                        boxes[source, dx + 1, 11 + dy : 15 + dy].reshape(64, 256),
                    ],
                    axis=0,
                )
                term = dot(window, transfer[number])
                total = term if total is None else total + term
            p = px * 2 + py
            leaf_out[128 * p : 128 * p + 128, :] = total[:128]
            for b in range(4):
                at = 32 * p + 8 * b
                parent_out[at : at + 8, :] = total[128 + 16 * b : 136 + 16 * b]


def downward_kernel(
    gathered, lattice, pair_down, down_child, perm8, perm4, far_leaf, far_parent,
    equiv_pts, inner, near, solution, source, counts, feats_hbm, out,
    local, pot, u0, u1, hi, lo, feats, feats_sem,
):
    load = pltpu.make_async_copy(feats_hbm, feats, feats_sem)
    load.start()
    split_into(lattice, hi, lo, 0)
    split_into(pair_down, hi, lo, 1)
    split_into(down_child, hi, lo, 3)
    vec = jnp.sum(gathered[...], axis=0)
    vec = dot3(jnp.concatenate([vec] * 4, axis=0), hi[0], lo[0])
    for axis, bits in ((0, 3), (1, 4)):
        place = lax.axis_index(AXES[axis])
        for bit in reversed(range(bits)):
            n = 1 + lax.rem(lax.div(place, 2**bit), 2)
            vec = dot3(vec, hi[n], lo[n])
    child = lambda x, p: dot3(x, hi[3 + p], lo[3 + p])
    great = jnp.concatenate([child(vec, 2 * a + b)[:2] for b in range(2) for a in range(2)], axis=0)
    spread = lambda x: jnp.concatenate([child(x, p) for p in range(4)], axis=0)
    grand = permute(perm4[...], spread(great))
    parent = spread(grand) + far_parent[...]
    parent = permute(perm8[...], parent)
    local[...] = spread(parent) + far_leaf[...]
    equiv_cols = col_feats(pad_points(equiv_pts), 0.0)

    first = lax.broadcasted_iota(jnp.int32, (2, 128), 1) < 64
    is_top = jnp.where(lax.broadcasted_iota(jnp.int32, (8, 128), 0) < 4, 1.0, 0.0)

    def distances(a, m, u):
        rows = feats[pl.ds(pl.multiple_of(a * LANES + 128 * m, 128), 128), :]
        at = 128 * (m % 4)
        u[at : at + 128, :] = dot(rows, equiv_cols)

    def finish(a, m, u):
        at = 128 * (m % 4)
        k_hi, k_lo = two_parts(power(u[at : at + 128, :]))
        row = lax.rem(a, 2) * 256 + m * 16 + lax.div(a, 2) * 2
        weight = jnp.concatenate(
            [local[pl.ds(row + 128 * half + c, 1), :] for half in range(2) for c in range(2)], axis=0
        )
        top = weight.astype(bf16).astype(f32)
        both = jnp.concatenate([top, weight - top], axis=0).astype(bf16)
        sums = dot_t(both, k_hi) + dot_t(jnp.concatenate([top, top], axis=0).astype(bf16), k_lo) * is_top
        sums = sums[:4] + sums[4:]
        total = jnp.where(first, sums[:2], sums[2:])
        for c in range(2):
            pot[c, pl.ds(a * 8 + m, 1), :] = total[c : c + 1]

    load.wait()
    for m in range(4):
        distances(0, m, u0)

    def step(i, carry):
        for a in (2 * i, 2 * i + 1):
            for m in range(4):
                distances(a, m + 4, u1)
                finish(a, m, u0)
            for m in range(4, 8):
                distances(jnp.minimum(a + 1, NX - 1), m - 4, u0)
                finish(a, m, u1)
        return carry

    lax.fori_loop(0, NX // 2, step, 0)
    for a in range(NX):
        rows = slice(8 * a, 8 * a + 8)
        close = near if a in (0, NX - 1) else inner
        total = [pot[c, rows, :] + close[c, rows, :] for c in range(2)]
        value = pairs(source, a) - scale_frac * (pairs(solution, a) * total[0] - total[1])
        value = jnp.where(live_pairs(counts, a), value, 0.0)
        out[a, pl.ds(0, NX // 2, stride=2), :] = value[:, :64]
        out[a, pl.ds(1, NX // 2, stride=2), :] = value[:, 64:]


def ring(axis, step):
    count = lax.axis_size(axis)
    return [(i, (i + step) % count) for i in range(count)]


def call(kernel, in_specs, out_shape, scratch, out_specs=None, cost=None):
    return pl.pallas_call(
        kernel,
        out_shape=out_shape,
        in_specs=in_specs,
        out_specs=out_specs or jax.tree.map(lambda _: VMEM, out_shape),
        scratch_shapes=scratch,
        compiler_params=PARAMS,
        cost_estimate=cost,
    )


def shape(*dims, dtype=f32):
    return jax.ShapeDtypeStruct(dims, dtype)


def shards(
    coords, weights, solution, source, counts, check_points, equiv_points, check_solve,
    up_children, far_transfer, down_children, pair_up, lattice_map, pair_down,
):
    perm8, perm4 = box_perm(4), box_perm(2)
    halves = [pltpu.VMEM((7, 256, 256), bf16)] * 2
    feats, pts, boxes, gy_next, gy_prev, gx_edge, up = call(
        upward_kernel,
        [VMEM] * 7 + [pl.BlockSpec(memory_space=pl.ANY)] * 3,
        (
            shape(NX * LANES, FEATS, dtype=bf16),
            shape(NX, 8, LANES),
            shape(4, 12, 16, 256),
            shape(128, 256),
            shape(128, 256),
            shape(2, 168, 256),
            shape(128, 2, 256),
        ),
        [pltpu.VMEM((512, 256), f32)] * 2
        + [pltpu.VMEM((LANES, 256), f32)]
        + [pltpu.VMEM((512, 256), f32)]
        + halves
        + [pltpu.VMEM((NX * LANES, FEATS), bf16), pltpu.SemaphoreType.DMA]
        + [pltpu.VMEM((NX, 8, LANES), f32), pltpu.SemaphoreType.DMA]
        + [pltpu.VMEM((7, 256, 256), f32), pltpu.SemaphoreType.DMA((3,))],
        out_specs=(pl.BlockSpec(memory_space=pl.ANY),) * 2 + (VMEM,) * 5,
    )(
        coords, weights, solution, counts, check_points, jnp.asarray(perm8, bf16),
        jnp.asarray(perm4, bf16), check_solve[None], up_children, pair_up,
    )
    gy_low = lax.ppermute(gy_next, "gy", ring("gy", 1))
    gy_high = lax.ppermute(gy_prev, "gy", ring("gy", -1))
    first, last = call(pack_kernel, [VMEM] * 3, (shape(168, 256), shape(168, 256)), [])(
        gy_low, gy_high, gx_edge
    )
    gx_low = lax.ppermute(last, "gx", ring("gx", 1))
    gx_high = lax.ppermute(first, "gx", ring("gx", -1))
    gathered = lax.all_to_all(up, AXES, 0, 0, tiled=True)
    roles = jnp.asarray(role_tiles(), bf16)
    near_scratch = (
        [pltpu.VMEM((NX + 2, 8, PADDED), f32)] * 2
        + [pltpu.VMEM((NX + 2, FEATS, PADDED), bf16)] * 2
        + [pltpu.VMEM((512, 512), f32)] * 2
        + [pltpu.VMEM((256, 128), f32)] * 2
    )
    gy_low_in, gy_high_in, _ = lax.optimization_barrier((gy_low, gy_high, first))
    inner = call(
        inner_kernel,
        [VMEM] * 4 + [pl.BlockSpec(memory_space=pl.ANY)],
        shape(2, 128, 128),
        [pltpu.VMEM((NX * LANES, FEATS), bf16), pltpu.SemaphoreType.DMA] + near_scratch,
        cost=pl.CostEstimate(flops=4 * 10**10, bytes_accessed=10**7, transcendentals=2 * 10**7),
    )(pts, gy_low_in, gy_high_in, roles, feats)
    near, far_leaf, far_parent = call(
        middle_kernel,
        [VMEM] * 7 + [pl.BlockSpec(memory_space=pl.ANY)] * 2,
        (shape(2, 128, 128), shape(512, 256), shape(128, 256)),
        [pltpu.VMEM((NX * LANES, FEATS), bf16), pltpu.SemaphoreType.DMA((2,))]
        + [pltpu.VMEM((40, 256, 256), bf16), pltpu.SemaphoreType.DMA]
        + near_scratch
        + [pltpu.VMEM((4, 16, 32, 256), f32), pltpu.VMEM((4, 3, 16, 16, 256), bf16)],
    )(
        pts, gy_low, gy_high, gx_low, gx_high, boxes, roles, feats,
        far_transfer,
    )
    return call(
        downward_kernel,
        [VMEM] * 14 + [pl.BlockSpec(memory_space=pl.ANY)],
        shape(NX, NX, 64),
        [pltpu.VMEM((512, 256), f32), pltpu.VMEM((2, 128, 128), f32)]
        + [pltpu.VMEM((512, 256), f32)] * 2
        + halves
        + [pltpu.VMEM((NX * LANES, FEATS), bf16), pltpu.SemaphoreType.DMA],
    )(
        gathered, lattice_map[None], pair_down, down_children,
        jnp.asarray(perm8.T, bf16), jnp.asarray(perm4.T, bf16), far_leaf, far_parent,
        equiv_points, inner, near, solution, source, counts, feats,
    )


def solution(mesh):
    box = P("gx", "gy", None)
    return jax.shard_map(
        shards,
        mesh=mesh,
        in_specs=(P(None, "gx", "gy", None), box, box, box, P("gx", "gy")) + (P(),) * 9,
        out_specs=box,
        check_vma=False,
    )
```

```python
import jax
import jax.numpy as jnp
import numpy as np
from jax import lax
from jax.experimental import pallas as pl
from jax.experimental.pallas import tpu as pltpu
from jax.sharding import PartitionSpec as P

f32 = jnp.float32
bf16 = jnp.bfloat16
scale_frac = 0.4
NX = 16
LANES = NX * 64
PADDED = LANES + 128
FEATS = 64
AXES = ("gx", "gy")
VMEM = pl.BlockSpec(memory_space=pltpu.VMEM)
PARAMS = pltpu.CompilerParams(vmem_limit_bytes=60 << 20)


def far_offsets():
    return [
        (x, y) for x in range(-3, 4) for y in range(-3, 4) if max(abs(x), abs(y)) >= 2
    ]


def dot(a, b):
    return jnp.dot(a, b, preferred_element_type=f32)


def dot_t(a, b):
    return lax.dot_general(a, b, (((1,), (1,)), ((), ())), preferred_element_type=f32)


def split3(block):
    hi = block.astype(bf16).astype(f32)
    rest = block - hi
    mid = rest.astype(bf16).astype(f32)
    return hi, mid, rest - mid


def centred(block):
    row = lax.broadcasted_iota(jnp.int32, block.shape, 0)
    moved = jnp.where(row < 3, 5.0 * block - 2.5, 0.0)
    return row, moved, jnp.sum(moved * moved, axis=0, keepdims=True)


def row_feats(block):
    row, moved, norm = centred(block)
    packed = jnp.where(
        row < 3, moved, jnp.where(row == 5, norm + 1.0, jnp.where(row == 6, 1.0, 0.0))
    )
    hi, mid, lo = split3(packed)
    role = jnp.concatenate(
        [hi[0:1], mid[0:1], lo[0:1], hi[1:2], mid[1:2], lo[1:2], hi[6:7] * 25.0, hi[7:8]], axis=0
    )
    tens = jnp.where(row < 6, 10.0, 0.0)
    return jnp.concatenate([hi, hi, hi, mid, mid, lo, role, tens], axis=0).astype(bf16)


def col_feats(block, role_scale=1.0):
    row, moved, norm = centred(block)
    packed = jnp.where(row < 3, moved * -2.0, jnp.where(row == 6, norm, 0.0))
    hi, mid, lo = split3(packed)
    main = hi + jnp.where(row == 5, 1.0, 0.0)
    ones = jnp.where(row < 7, role_scale, 0.0)
    role = jnp.concatenate(
        [hi[0:1], mid[0:1], lo[0:1], hi[1:2], mid[1:2], lo[1:2], hi[7:8], hi[7:8]], axis=0
    )
    return jnp.concatenate(
        [main, mid, lo, main, mid, main, ones, role * role_scale], axis=0
    ).astype(bf16)


def power(u):
    return jnp.exp2(jnp.log2(u) * -2.25)


def box_perm(side):
    order = []
    for e in (0, 1):
        for f in (0, 1):
            for b in range(side):
                for a in range(side):
                    for c in (0, 1):
                        order.append(((2 * b + f) * 2 * side + 2 * a + e) * 2 + c)
    out = np.zeros((len(order), len(order)), np.float32)
    out[np.arange(len(order)), order] = 1.0
    return out


def eye(n):
    return (
        lax.broadcasted_iota(jnp.int32, (n, n), 0) == lax.broadcasted_iota(jnp.int32, (n, n), 1)
    ).astype(bf16)


def split_into(source, hi, lo, first):
    def part(i, carry):
        rows = pl.ds(pl.multiple_of(i * 64, 64), 64)
        for n in range(source.shape[0]):
            w = source[n, rows, :]
            h = w.astype(bf16)
            hi[first + n, rows, :] = h
            lo[first + n, rows, :] = (w - h.astype(f32)).astype(bf16)
        return carry

    lax.fori_loop(0, 4, part, 0)


def dot3(x, hi, lo):
    n = x.shape[0]
    top = x.astype(bf16).astype(f32)
    both = jnp.concatenate([top, x - top], axis=0).astype(bf16)
    main = dot(both, hi)
    if n % 16:
        rest = dot(both, lo)
        return main[:n] + main[n:] + rest[:n]
    return main[:n] + main[n:] + dot(top.astype(bf16), lo)


def permute(perm, x):
    hi, mid, lo = split3(x)
    out = dot(perm, jnp.concatenate([hi, mid, lo], axis=1).astype(bf16))
    return out[:, :256] + out[:, 256:512] + out[:, 512:]


def gather4(blocks, hi, lo, first):
    n = blocks.shape[0] // 4
    total = None
    for p in range(4):
        term = dot3(blocks[p * n : (p + 1) * n], hi[first + p], lo[first + p])
        total = term if total is None else total + term
    return total


def pairs(ref, *index):
    even = ref[(*index, pl.ds(0, NX // 2, stride=2))]
    odd = ref[(*index, pl.ds(1, NX // 2, stride=2))]
    return jnp.concatenate([even, odd], axis=1)


def live_pairs(counts, a):
    row = counts[pl.ds(a, 1), :].astype(f32)
    box = lax.broadcasted_iota(jnp.int32, (NX // 2, NX), 1)
    pair = 2 * lax.broadcasted_iota(jnp.int32, (NX // 2, NX), 0)
    n = [jnp.sum(jnp.where(box == pair + odd, row, 0.0), axis=1, keepdims=True) for odd in (0, 1)]
    lane = lax.broadcasted_iota(jnp.int32, (NX // 2, 128), 1)
    return lax.rem(lane, 64).astype(f32) < jnp.where(lane < 64, n[0], n[1])


def two_parts(x):
    hi = x.astype(bf16)
    return hi, (x - hi.astype(f32)).astype(bf16)


def pad_points(points):
    return jnp.concatenate([points[...], jnp.zeros((5, 256), f32)], axis=0)


def upward_kernel(
    coords, weights, solution, counts, check_pts, perm8, perm4, solve, up_child, pair_up,
    feats, pts_out, boxes, gy_next, gy_prev, gx_edge, up_out,
    u0, u1, densities, pot, hi, lo, kept, kept_sem, pts, pts_sem, matrices, matrix_sem,
):
    check_cols = col_feats(pad_points(check_pts), 0.0)
    ident = eye(128)
    loads = [
        pltpu.make_async_copy(source, matrices.at[pl.ds(at, count)], matrix_sem.at[n])
        for n, (source, at, count) in enumerate(((solve, 0, 1), (up_child, 1, 4), (pair_up, 5, 2)))
    ]
    for load in loads:
        load.start()

    row8 = lax.broadcasted_iota(jnp.int32, (8, 128), 0)
    lane8 = lax.broadcasted_iota(jnp.int32, (8, 128), 1)
    own_half = lax.rem(lax.div(row8, 2), 2) == lax.div(lane8, 64)

    def prepare(i, carry):
        for a in (4 * i, 4 * i + 1, 4 * i + 2, 4 * i + 3):
            weight = jnp.where(live_pairs(counts, a), pairs(weights, a), 0.0)
            parts = [pairs(coords, c, a) for c in range(3)]
            parts += [weight, weight * pairs(solution, a)]
            zero = jnp.zeros((3, 128), f32)
            for m in range(NX // 2):
                lanes = slice(128 * m, 128 * m + 128)
                block = jnp.concatenate([x[m : m + 1] for x in parts] + [zero], axis=0)
                pts[a, :, lanes] = block
                f = dot_t(ident, row_feats(block)).astype(bf16)
                kept[pl.ds(pl.multiple_of(a * LANES + 128 * m, 128), 128), :] = f
                both = [x[m : m + 1] for x in parts[3:]]
                dens = jnp.where(own_half, jnp.concatenate(both * 4, axis=0), 0.0)
                high = dens.astype(bf16).astype(f32)
                at = pl.multiple_of(a * 64 + 8 * m, 8)
                densities[pl.ds(at, 8), 0:128] = jnp.where(row8 < 4, high, dens - high)
                densities[pl.ds(at, 8), 128:256] = jnp.where(row8 < 4, high, 0.0)
        return carry

    lax.fori_loop(0, NX // 4, prepare, 0)
    keep = pltpu.make_async_copy(kept, feats, kept_sem)
    keep.start()
    keep_pts = pltpu.make_async_copy(pts, pts_out, pts_sem)
    keep_pts.start()
    for load in loads:
        load.wait()
    split_into(matrices, hi, lo, 0)

    def distances(a, m, u):
        rows = kept[pl.ds(pl.multiple_of(a * LANES + 128 * m, 128), 128), :]
        at = 128 * (m % 4)
        u[at : at + 128, :] = dot(rows, check_cols)

    def finish(a, m, u):
        at = 128 * (m % 4)
        k_hi, k_lo = two_parts(power(u[at : at + 128, :]))
        dens = densities[pl.ds(pl.multiple_of(a * 64 + 8 * m, 8), 8), :].astype(bf16)
        sums = dot(dens, jnp.concatenate([k_hi, k_lo], axis=0))
        sums = sums[:4] + sums[4:]
        row = lax.rem(a, 2) * 256 + m * 16 + lax.div(a, 2) * 2
        for half in range(2):
            for c in range(2):
                n = 2 * half + c
                pot[pl.ds(row + 128 * half + c, 1), :] = sums[n : n + 1]

    for m in range(4):
        distances(0, m, u0)

    def step(i, carry):
        for a in (2 * i, 2 * i + 1):
            for m in range(4):
                distances(a, m + 4, u1)
                finish(a, m, u0)
            for m in range(4, 8):
                distances(jnp.minimum(a + 1, NX - 1), m - 4, u0)
                finish(a, m, u1)
        return carry

    lax.fori_loop(0, NX // 2, step, 0)
    leaf = dot3(pot[...], hi[0], lo[0])
    parent = permute(perm8[...], gather4(leaf, hi, lo, 1))
    leaf_r = leaf.astype(bf16).astype(f32)
    parent_r = parent.astype(bf16).astype(f32)
    for p in range(4):
        own = leaf_r[128 * p : 128 * p + 128]
        coarse = parent_r[32 * p : 32 * p + 32]
        for b in range(8):
            boxes[p, b] = own[16 * b : 16 * b + 16]
        for b in range(4):
            boxes[p, 8 + b, 0:8] = coarse[8 * b : 8 * b + 8]
            boxes[p, 8 + b, 8:16] = jnp.zeros((8, 256), f32)
        for msg, b, bb in ((gy_next, 7, 3), (gy_prev, 0, 0)):
            msg[16 * p : 16 * p + 16, :] = own[16 * b : 16 * b + 16]
            msg[64 + 8 * p : 72 + 8 * p, :] = coarse[8 * bb : 8 * bb + 8]
        for e in range(2):
            for c in range(2):
                at = 64 * c + 16 * p
                for b in range(8):
                    row = 16 * b + 14 * e + c
                    gx_edge[e, at + 1 + b : at + 2 + b, :] = own[row : row + 1]
                for b in range(4):
                    row = 8 * b + 6 * e + c
                    gx_edge[e, at + 11 + b : at + 12 + b, :] = coarse[row : row + 1]
                for gap in (0, 9, 10, 15):
                    gx_edge[e, at + gap : at + gap + 1, :] = jnp.zeros((1, 256), f32)
    for msg, start in ((gy_next, LANES - 64), (gy_prev, 0)):
        for k in range(4):
            piece = pts[4 * k : 4 * k + 4, :, start : start + 64].reshape(32, 64)
            msg[96:128, 64 * k : 64 * k + 64] = piece
    for e, t in ((0, 0), (1, NX - 1)):
        for k in range(4):
            gx_edge[e, 128 + 8 * k : 136 + 8 * k, :] = pts[t, :, 256 * k : 256 * k + 256]
        gx_edge[e, 160:168, :] = jnp.zeros((8, 256), f32)
    grand = permute(perm4[...], gather4(parent, hi, lo, 1))
    great = gather4(grand, hi, lo, 1)
    vec = None
    for b in range(2):
        for a in range(2):
            at = (b * 2 + a) * 2
            rows = jnp.concatenate([great[at : at + 2]] * 4, axis=0)
            term = dot3(rows, hi[1 + 2 * a + b], lo[1 + 2 * a + b])
            vec = term if vec is None else vec + term
    for axis, bits in ((1, 4), (0, 3)):
        place = lax.axis_index(AXES[axis])
        for bit in range(bits):
            n = 5 + lax.rem(lax.div(place, 2**bit), 2)
            vec = dot3(vec, hi[n], lo[n])
    up_out[...] = jnp.broadcast_to(vec[None, :2], (128, 2, 256))
    keep.wait()
    keep_pts.wait()


def pack_kernel(low, high, edge, first, last):
    for e, out in enumerate((first, last)):
        out[...] = edge[e]
        for p in range(4):
            for c in range(2):
                at = 64 * c + 16 * p
                fine = 16 * p + 14 * e + c
                coarse = 64 + 8 * p + 6 * e + c
                for gap, ref, row in (
                    (0, low, fine), (9, high, fine), (10, low, coarse), (15, high, coarse)
                ):
                    out[at + gap : at + gap + 1, :] = ref[row : row + 1, :]
        rows = slice(96, 104) if e == 0 else slice(120, 128)
        lanes = slice(0, 64) if e == 0 else slice(192, 256)
        out[160:168, 0:64] = low[rows, lanes]
        out[160:168, 64:128] = high[rows, lanes]


def role_tiles():
    def column(sx, sy):
        return [-10.0 * sx] * 3 + [-10.0 * sy] * 3 + [float(sx * sx + sy * sy), 0.0] + [
            -0.5 * sx
        ] * 3 + [-0.5 * sy] * 3 + [0.0, 0.0]
    pairs = [((t, -1), (t, 0)) for t in (-1, 0, 1)] + [((-1, 1), (0, 1)), ((1, 1), (1, 1))]
    out = np.zeros((5, 16, 128), np.float32)
    for n, (left, right) in enumerate(pairs):
        out[n, :, :64] = np.array(column(*left))[:, None]
        out[n, :, 64:] = np.array(column(*right))[:, None]
    return out


def sum_lanes(acc0, acc1):
    row = lax.broadcasted_iota(jnp.int32, (8, 256), 0)
    total = None
    for c, acc in enumerate((acc0, acc1)):
        hi = acc.astype(bf16)
        lo = (acc - hi.astype(f32)).astype(bf16)
        ones = jnp.where(row == c, 1.0, 0.0).astype(bf16)
        term = dot_t(ones, jnp.concatenate([hi, lo], axis=1))
        total = term if total is None else total + term
    return total


def near_strips(
    strips, pts, gy_low, gy_high, gx_low, gx_high, roles, near, feats, dens0, dens1,
    cols0, cols1,
):
    first = lax.broadcasted_iota(jnp.int32, (1, 128), 1) < 64
    first_cols = lax.broadcasted_iota(jnp.int32, (FEATS, 128), 1) < 64

    for t in strips:
        if t in (0, NX + 1):
            ref = gx_low if t == 0 else gx_high
            own = jnp.concatenate([ref[128 + 8 * k : 136 + 8 * k, :] for k in range(4)], axis=1)
            low, high = ref[160:168, 0:64], ref[160:168, 64:128]
        else:
            s = t - 1
            rows = slice(96 + 8 * (s % 4), 104 + 8 * (s % 4))
            lanes = slice(64 * (s // 4), 64 * (s // 4) + 64)
            own, low, high = pts[s], gy_low[rows, lanes], gy_high[rows, lanes]
        dens0[t, :, 0:64] = low
        dens0[t, :, 64 : 64 + LANES] = own
        dens0[t, :, 64 + LANES :] = high
        dens1[t, :, 0:LANES] = own
        dens1[t, :, LANES : LANES + 64] = high
        dens1[t, :, LANES + 64 :] = jnp.zeros((8, 64), f32)

    def prepare(i, carry):
        t = strips[0] + i
        if len(strips) < NX:
            t = jnp.where(i < 3, i, i + NX - 4)
        cols0[t] = col_feats(dens0[t])
        cols1[t] = col_feats(dens1[t])
        return carry

    lax.fori_loop(0, len(strips), prepare, 0)

    spare = jnp.zeros((FEATS, 128), bf16)

    def distances(a, half, u, u_last, mms=range(4)):
        for mm in mms:
            base = half * 512 + mm * 128
            here, after = slice(base, base + 128), slice(base + 128, base + 256)
            both = []
            for odd in range(2):
                own, other = ((cols0, cols1), (cols1, cols0))[odd]
                far = here if odd == 0 else after
                blocks = [own[a + t, :, here] for t in range(3)]
                blocks.append(jnp.where(first_cols, own[a, :, after], other[a + 1, :, far]))
                blocks = [
                    jnp.concatenate([x[:48], x[48:] * roles[n]], axis=0)
                    for n, x in enumerate(blocks)
                ]
                start = pl.multiple_of(a * LANES + base + 64 * odd, 64)
                rows = feats[pl.ds(start, 64), :]
                both.append(rows)
                at = 64 * (2 * mm + odd)
                u[at : at + 64, :] = dot(rows, jnp.concatenate(blocks, axis=1))
            last = cols0[a + 2, :, after]
            last = jnp.concatenate([last[:48], last[48:] * roles[4]], axis=0)
            split = jnp.concatenate(
                [jnp.where(first_cols, last, spare), jnp.where(first_cols, spare, last)], axis=0
            )
            u_last[64 * mm : 64 * mm + 64, :] = dot(jnp.concatenate(both, axis=1), split)

    def finish(a, half, u, u_last, mms=range(4)):
        for mm in mms:
            base = half * 512 + mm * 128
            here, after = slice(base, base + 128), slice(base + 128, base + 256)
            sums = []
            for odd in range(2):
                d_own, d_other = ((dens0, dens1), (dens1, dens0))[odd]
                far = here if odd == 0 else after
                dens = []
                for c in range(2):
                    r = slice(3 + c, 4 + c)
                    dens.append([d_own[a + n, r, here] for n in range(3)])
                    dens[c].append(jnp.where(first, d_own[a, r, after], d_other[a + 1, r, far]))
                parts = [[], []]
                for chunk in range(4):
                    at = 64 * (2 * mm + odd) + 16 * chunk
                    k = [power(u[at : at + 16, 128 * n : 128 * n + 128]) for n in range(4)]
                    for c in range(2):
                        parts[c].append(
                            (k[0] * dens[c][0] + k[1] * dens[c][1])
                            + (k[2] * dens[c][2] + k[3] * dens[c][3])
                        )
                sums.append([jnp.concatenate(p, axis=0) for p in parts])
            k = power(u_last[64 * mm : 64 * mm + 64, :])
            both = []
            for c in range(2):
                term = k * dens0[a + 2, 3 + c : 4 + c, after]
                both.append(
                    jnp.concatenate(
                        [
                            sums[0][c] + jnp.where(first, term, 0.0),
                            sums[1][c] + jnp.where(first, 0.0, term),
                        ],
                        axis=0,
                    )
                )
            total = sum_lanes(*both)
            for c in range(2):
                near[c, pl.ds(a * 8 + half * 4 + mm, 1), :] = total[c : c + 1]

    return distances, finish


def inner_kernel(
    pts, gy_low, gy_high, roles, feats_hbm, near,
    feats, feats_sem, dens0, dens1, cols0, cols1, u0, u1, v0, v1,
):
    load = pltpu.make_async_copy(feats_hbm, feats, feats_sem)
    load.start()
    distances, finish = near_strips(
        range(1, NX + 1), pts, gy_low, gy_high, None, None, roles, near, feats, dens0, dens1,
        cols0, cols1,
    )
    load.wait()
    distances(jnp.int32(1), 0, u0, v0)

    def step(i, carry):
        for a in (2 * i + 1, 2 * i + 2):
            for mm in range(4):
                finish(a, 0, u0, v0, (mm,))
                distances(a, 1, u1, v1, (mm,))
            for mm in range(4):
                finish(a, 1, u1, v1, (mm,))
                distances(jnp.minimum(a + 1, NX - 2), 0, u0, v0, (mm,))
        return carry

    lax.fori_loop(0, NX // 2 - 1, step, 0)


def middle_kernel(
    pts, gy_low, gy_high, gx_low, gx_high, boxes, roles, feats_hbm, transfer_hbm,
    near, leaf_out, parent_out,
    feats, feats_sem, transfer, arrived, dens0, dens1, cols0, cols1, u0, u1, v0, v1,
    extended, windows,
):
    loads = [
        pltpu.make_async_copy(
            feats_hbm.at[pl.ds(a * LANES, LANES)], feats.at[pl.ds(a * LANES, LANES)],
            feats_sem.at[n],
        )
        for n, a in enumerate((0, NX - 1))
    ]
    for load in loads:
        load.start()
    fetch = pltpu.make_async_copy(transfer_hbm, transfer, arrived)
    fetch.start()
    distances, finish = near_strips(
        (0, 1, 2, NX - 1, NX, NX + 1), pts, gy_low, gy_high, gx_low, gx_high, roles, near,
        feats, dens0, dens1, cols0, cols1,
    )
    for load in loads:
        load.wait()
    low_strip, high_strip = jnp.int32(0), jnp.int32(NX - 1)
    distances(low_strip, 0, u0, v0)
    for mm in range(4):
        finish(low_strip, 0, u0, v0, (mm,))
        distances(low_strip, 1, u1, v1, (mm,))
    for mm in range(4):
        finish(low_strip, 1, u1, v1, (mm,))
        distances(high_strip, 0, u0, v0, (mm,))
    for mm in range(4):
        finish(high_strip, 0, u0, v0, (mm,))
        distances(high_strip, 1, u1, v1, (mm,))
    finish(high_strip, 1, u1, v1)

    blank = jnp.zeros((8, 256), f32)
    for p in range(4):
        for slot in range(16):
            n = p * 16 + slot
            own_rows = extended.at[p, slot]
            if slot in (0, 9):
                own_rows[8:24, :] = (gy_low if slot == 0 else gy_high)[16 * p : 16 * p + 16, :]
            elif slot in (10, 15):
                ref = gy_low if slot == 10 else gy_high
                own_rows[8:16, :] = ref[64 + 8 * p : 72 + 8 * p, :]
                own_rows[16:24, :] = blank
            else:
                own_rows[8:24, :] = boxes[p, slot - 1 if slot < 9 else slot - 3]
            end = 24 if slot < 10 else 16
            for c in range(2):
                row = 64 * c + n
                own_rows[6 + c : 7 + c, :] = gx_low[row : row + 1, :]
                own_rows[end + c : end + c + 1, :] = gx_high[row : row + 1, :]
            if slot >= 10:
                own_rows[24:26, :] = jnp.zeros((2, 256), f32)
            for d in range(3):
                windows[p, d, slot] = own_rows[6 + 2 * d : 22 + 2 * d, :].astype(bf16)
    fetch.wait()
    far_level(windows, transfer, leaf_out, parent_out)


def reachable(parity, shift):
    return abs((parity + shift) // 2) <= 1


def far_level(boxes, transfer, leaf_out, parent_out):
    for px in (0, 1):
        for py in (0, 1):
            total = None
            for number, (sx, sy) in enumerate(far_offsets()):
                if not (reachable(px, sx) and reachable(py, sy)):
                    continue
                dx, dy = (px + sx) // 2, (py + sy) // 2
                source = (px + sx) % 2 * 2 + (py + sy) % 2
                window = jnp.concatenate(
                    [
                        boxes[source, dx + 1, 1 + dy : 9 + dy].reshape(128, 256),
                        boxes[source, dx + 1, 11 + dy : 15 + dy].reshape(64, 256),
                    ],
                    axis=0,
                )
                term = dot(window, transfer[number])
                total = term if total is None else total + term
            p = px * 2 + py
            leaf_out[128 * p : 128 * p + 128, :] = total[:128]
            for b in range(4):
                at = 32 * p + 8 * b
                parent_out[at : at + 8, :] = total[128 + 16 * b : 136 + 16 * b]


def downward_kernel(
    gathered, lattice, pair_down, down_child, perm8, perm4, far_leaf, far_parent,
    equiv_pts, counts, inner_hbm, near_hbm, solution_hbm, source_hbm, feats_hbm, out,
    local, pot, u0, u1, hi, lo, feats, feats_sem, inner, near, solution, source, late_sem,
):
    load = pltpu.make_async_copy(feats_hbm, feats, feats_sem)
    load.start()
    late = [
        pltpu.make_async_copy(a, b, late_sem.at[n])
        for n, (a, b) in enumerate(
            (
                (inner_hbm, inner), (near_hbm, near), (solution_hbm, solution),
                (source_hbm, source),
            )
        )
    ]
    for one in late:
        one.start()
    split_into(lattice, hi, lo, 0)
    split_into(pair_down, hi, lo, 1)
    split_into(down_child, hi, lo, 3)
    vec = jnp.sum(gathered[...], axis=0)
    vec = dot3(jnp.concatenate([vec] * 4, axis=0), hi[0], lo[0])
    for axis, bits in ((0, 3), (1, 4)):
        place = lax.axis_index(AXES[axis])
        for bit in reversed(range(bits)):
            n = 1 + lax.rem(lax.div(place, 2**bit), 2)
            vec = dot3(vec, hi[n], lo[n])
    child = lambda x, p: dot3(x, hi[3 + p], lo[3 + p])
    great = jnp.concatenate([child(vec, 2 * a + b)[:2] for b in range(2) for a in range(2)], axis=0)
    spread = lambda x: jnp.concatenate([child(x, p) for p in range(4)], axis=0)
    grand = permute(perm4[...], spread(great))
    parent = spread(grand) + far_parent[...]
    parent = permute(perm8[...], parent)
    local[...] = spread(parent) + far_leaf[...]
    equiv_cols = col_feats(pad_points(equiv_pts), 0.0)

    first = lax.broadcasted_iota(jnp.int32, (2, 128), 1) < 64
    is_top = jnp.where(lax.broadcasted_iota(jnp.int32, (8, 128), 0) < 4, 1.0, 0.0)

    def distances(a, m, u):
        rows = feats[pl.ds(pl.multiple_of(a * LANES + 128 * m, 128), 128), :]
        at = 128 * (m % 4)
        u[at : at + 128, :] = dot(rows, equiv_cols)

    def finish(a, m, u):
        at = 128 * (m % 4)
        k_hi, k_lo = two_parts(power(u[at : at + 128, :]))
        row = lax.rem(a, 2) * 256 + m * 16 + lax.div(a, 2) * 2
        weight = jnp.concatenate(
            [local[pl.ds(row + 128 * half + c, 1), :] for half in range(2) for c in range(2)], axis=0
        )
        top = weight.astype(bf16).astype(f32)
        both = jnp.concatenate([top, weight - top], axis=0).astype(bf16)
        sums = dot_t(both, k_hi) + dot_t(jnp.concatenate([top, top], axis=0).astype(bf16), k_lo) * is_top
        sums = sums[:4] + sums[4:]
        total = jnp.where(first, sums[:2], sums[2:])
        for c in range(2):
            pot[c, pl.ds(a * 8 + m, 1), :] = total[c : c + 1]

    load.wait()
    for m in range(4):
        distances(0, m, u0)

    def step(i, carry):
        for a in (2 * i, 2 * i + 1):
            for m in range(4):
                distances(a, m + 4, u1)
                finish(a, m, u0)
            for m in range(4, 8):
                distances(jnp.minimum(a + 1, NX - 1), m - 4, u0)
                finish(a, m, u1)
        return carry

    lax.fori_loop(0, NX // 2, step, 0)
    for one in late:
        one.wait()
    for a in range(NX):
        rows = slice(8 * a, 8 * a + 8)
        close = near if a in (0, NX - 1) else inner
        total = [pot[c, rows, :] + close[c, rows, :] for c in range(2)]
        value = pairs(source, a) - scale_frac * (pairs(solution, a) * total[0] - total[1])
        value = jnp.where(live_pairs(counts, a), value, 0.0)
        out[a, pl.ds(0, NX // 2, stride=2), :] = value[:, :64]
        out[a, pl.ds(1, NX // 2, stride=2), :] = value[:, 64:]


def ring(axis, step):
    count = lax.axis_size(axis)
    return [(i, (i + step) % count) for i in range(count)]


def call(kernel, in_specs, out_shape, scratch, out_specs=None, cost=None):
    return pl.pallas_call(
        kernel,
        out_shape=out_shape,
        in_specs=in_specs,
        out_specs=out_specs or jax.tree.map(lambda _: VMEM, out_shape),
        scratch_shapes=scratch,
        compiler_params=PARAMS,
        cost_estimate=cost,
    )


def shape(*dims, dtype=f32):
    return jax.ShapeDtypeStruct(dims, dtype)


def shards(
    coords, weights, solution, source, counts, check_points, equiv_points, check_solve,
    up_children, far_transfer, down_children, pair_up, lattice_map, pair_down,
):
    perm8, perm4 = box_perm(4), box_perm(2)
    halves = [pltpu.VMEM((7, 256, 256), bf16)] * 2
    feats, pts, boxes, gy_next, gy_prev, gx_edge, up = call(
        upward_kernel,
        [VMEM] * 7 + [pl.BlockSpec(memory_space=pl.ANY)] * 3,
        (
            shape(NX * LANES, FEATS, dtype=bf16),
            shape(NX, 8, LANES),
            shape(4, 12, 16, 256),
            shape(128, 256),
            shape(128, 256),
            shape(2, 168, 256),
            shape(128, 2, 256),
        ),
        [pltpu.VMEM((512, 256), f32)] * 2
        + [pltpu.VMEM((LANES, 256), f32)]
        + [pltpu.VMEM((512, 256), f32)]
        + halves
        + [pltpu.VMEM((NX * LANES, FEATS), bf16), pltpu.SemaphoreType.DMA]
        + [pltpu.VMEM((NX, 8, LANES), f32), pltpu.SemaphoreType.DMA]
        + [pltpu.VMEM((7, 256, 256), f32), pltpu.SemaphoreType.DMA((3,))],
        out_specs=(pl.BlockSpec(memory_space=pl.ANY),) * 2 + (VMEM,) * 5,
    )(
        coords, weights, solution, counts, check_points, jnp.asarray(perm8, bf16),
        jnp.asarray(perm4, bf16), check_solve[None], up_children, pair_up,
    )
    gy_low = lax.ppermute(gy_next, "gy", ring("gy", 1))
    gy_high = lax.ppermute(gy_prev, "gy", ring("gy", -1))
    first, last = call(pack_kernel, [VMEM] * 3, (shape(168, 256), shape(168, 256)), [])(
        gy_low, gy_high, gx_edge
    )
    gx_low = lax.ppermute(last, "gx", ring("gx", 1))
    gx_high = lax.ppermute(first, "gx", ring("gx", -1))
    gathered = lax.all_to_all(up, AXES, 0, 0, tiled=True)
    roles = jnp.asarray(role_tiles(), bf16)
    near_scratch = (
        [pltpu.VMEM((NX + 2, 8, PADDED), f32)] * 2
        + [pltpu.VMEM((NX + 2, FEATS, PADDED), bf16)] * 2
        + [pltpu.VMEM((512, 512), f32)] * 2
        + [pltpu.VMEM((256, 128), f32)] * 2
    )
    gy_low_in, gy_high_in, _ = lax.optimization_barrier((gy_low, gy_high, first))
    inner = call(
        inner_kernel,
        [VMEM] * 4 + [pl.BlockSpec(memory_space=pl.ANY)],
        shape(2, 128, 128),
        [pltpu.VMEM((NX * LANES, FEATS), bf16), pltpu.SemaphoreType.DMA] + near_scratch,
        cost=pl.CostEstimate(flops=4 * 10**10, bytes_accessed=10**7, transcendentals=2 * 10**7),
    )(pts, gy_low_in, gy_high_in, roles, feats)
    near, far_leaf, far_parent = call(
        middle_kernel,
        [VMEM] * 7 + [pl.BlockSpec(memory_space=pl.ANY)] * 2,
        (shape(2, 128, 128), shape(512, 256), shape(128, 256)),
        [pltpu.VMEM((NX * LANES, FEATS), bf16), pltpu.SemaphoreType.DMA((2,))]
        + [pltpu.VMEM((40, 256, 256), bf16), pltpu.SemaphoreType.DMA]
        + near_scratch
        + [pltpu.VMEM((4, 16, 32, 256), f32), pltpu.VMEM((4, 3, 16, 16, 256), bf16)],
    )(
        pts, gy_low, gy_high, gx_low, gx_high, boxes, roles, feats,
        far_transfer,
    )
    return call(
        downward_kernel,
        [VMEM] * 10 + [pl.BlockSpec(memory_space=pl.ANY)] * 5,
        shape(NX, NX, 64),
        [pltpu.VMEM((512, 256), f32), pltpu.VMEM((2, 128, 128), f32)]
        + [pltpu.VMEM((512, 256), f32)] * 2
        + halves
        + [pltpu.VMEM((NX * LANES, FEATS), bf16), pltpu.SemaphoreType.DMA]
        + [pltpu.VMEM((2, 128, 128), f32)] * 2
        + [pltpu.VMEM((NX, NX, 64), f32)] * 2
        + [pltpu.SemaphoreType.DMA((4,))],
    )(
        gathered, lattice_map[None], pair_down, down_children,
        jnp.asarray(perm8.T, bf16), jnp.asarray(perm4.T, bf16), far_leaf, far_parent,
        equiv_points, counts, inner, near, solution, source, feats,
    )


def solution(mesh):
    box = P("gx", "gy", None)
    return jax.shard_map(
        shards,
        mesh=mesh,
        in_specs=(P(None, "gx", "gy", None), box, box, box, P("gx", "gy")) + (P(),) * 9,
        out_specs=box,
        check_vma=False,
    )
```
